256 devices in a mesh: dp: 64 (over x, z, core), mp: 4 (over y).
Axes of the slice: x: 4, y: 4, z: 8, core: 2. Of those that a mesh axis runs over, the one named last changes fastest.
Arguments:
- hidden_in: bfloat16 [32768, 5120], P('dp'), may hold values from -8 to 8
- input_norm_gain: bfloat16 [5120], P('dp'), may hold values from 0.5 to 1.5
- w_query: bfloat16 [5120, 2560], P('dp', 'mp'), may hold values from -1 to 1
- w_keyval: bfloat16 [2, 5120, 512], P(None, 'dp', 'mp'), may hold values from -1 to 1
- b_query: float32 [2560], P('mp'), may hold values from -3 to 3
- b_keyval: float32 [2, 512], P(None, 'mp'), may hold values from -3 to 3
- upstream: bfloat16 [32768, 2560], P('dp', 'mp'), may hold values from -6 to 6
- lengths: int32 [256, 4], P('dp'), may hold values from 0 to 128, as said below
Outputs:
- attended: bfloat16 [32768, 2560], P('dp', 'mp')
- grad_query: float32 [5120, 2560], P('dp', 'mp')
- grad_keyval: float32 [2, 5120, 512], P(None, 'dp', 'mp')
- grad_bias_query: float32 [2560], P('mp')
- grad_bias_keyval: float32 [2, 512], P(None, 'mp')
- gain_gradient: float32 [5120], P('dp')
The draws below stay inside these ranges and needn't reach their ends.
Inputs may be any that keep to these rules, and one draw needn't show every extreme that they name: The lengths of one row sum to at most 128; a zero is an empty slot; some row holds one document of 128 tokens.
All inputs are finite; a program needn't handle non-finite values.
Results may differ from the reference program's by a relative error of at most 0.011.
Values may be sent and summed in bfloat16 or wider, within the bound.
No kernel may reach another device: no remote copies, remote signals or barrier semaphores. Data moves between devices by JAX's collectives and lax.ppermute only.
A program may use at most 128 MiB of HBM per device.

```python
import jax
import jax.numpy as jnp
from jax import lax

MODEL_WIDTH = 5120
HEAD_SIZE = 128
QUERY_HEADS = 20
KEYVALUE_HEADS = 4
ROW_TOKENS = 128
DOCS = 4
ROWS_DEV = 4
QW = 2560
KW = 512
PACKED_ROWS = 256
TOKENS = 32768


def shared_weights(key):
    query_key = jax.random.fold_in(key, 71)
    keyval_key = jax.random.fold_in(key, 72)
    spread = MODEL_WIDTH ** (-0.5)
    w_query = jax.random.truncated_normal(query_key, -6.0, 6.0, (MODEL_WIDTH, QW), jnp.float32) * spread
    w_keyval = jax.random.truncated_normal(keyval_key, -6.0, 6.0, (2, MODEL_WIDTH, KW), jnp.float32) * spread
    return (w_query, w_keyval)


def draw_w_query(key, part):
    return shared_weights(key)[0].astype(jnp.bfloat16)


def draw_w_keyval(key, part):
    return shared_weights(key)[1].astype(jnp.bfloat16)


def draw_hidden_in(key, part):
    w_query, w_keyval = shared_weights(key)
    key = jax.random.fold_in(key, 23)
    noise_key = jax.random.fold_in(key, 0)
    noise_sample = jax.random.truncated_normal(noise_key, -6.0, 6.0, (TOKENS, MODEL_WIDTH), jnp.float32)
    group_factor = QUERY_HEADS // KEYVALUE_HEADS
    head_count = jnp.arange(KEYVALUE_HEADS, dtype=jnp.int32)
    q_cols = head_count * (group_factor * HEAD_SIZE) + HEAD_SIZE - 1
    k_cols = head_count * HEAD_SIZE + HEAD_SIZE - 1
    query_directions = w_query[:, q_cols].T
    key_directions = w_keyval[0][:, k_cols].T
    directions = jnp.stack([key_directions, key_directions, key_directions, query_directions], axis=1).reshape(4 * KEYVALUE_HEADS, MODEL_WIDTH)
    signal_strength = jnp.repeat(1.5 + 0.5 * head_count.astype(jnp.float32), 4)
    first_entry = TOKENS - ROW_TOKENS
    planted_signal = signal_strength[:, None] * MODEL_WIDTH ** 0.5 * directions + noise_sample[first_entry:first_entry + 4 * KEYVALUE_HEADS]
    full_tensor = noise_sample
    full_tensor = full_tensor.at[first_entry:first_entry + 4 * KEYVALUE_HEADS].set(planted_signal)
    return jnp.clip(full_tensor, -8.0, 8.0).astype(jnp.bfloat16)


def draw_lengths(key, part):
    key = jax.random.fold_in(key, 5)
    first_key, second_key = jax.random.split(key)
    ranks = PACKED_ROWS // ROWS_DEV
    rank = jnp.arange(PACKED_ROWS, dtype=jnp.int32) // ROWS_DEV
    low = ROW_TOKENS * 3 // 16 + ROW_TOKENS * 9 // 16 * rank // max(ranks - 1, 1)
    fill = jax.random.randint(first_key, (PACKED_ROWS,), low, low + ROW_TOKENS // 4 + 1)
    fill = jnp.minimum(fill, ROW_TOKENS).astype(jnp.int32)
    cuts = jax.random.randint(second_key, (PACKED_ROWS, DOCS - 1), 0, fill[:, None] + 1)
    cuts = jnp.sort(cuts, axis=1).astype(jnp.int32)
    edges = jnp.concatenate([jnp.zeros((PACKED_ROWS, 1), jnp.int32), cuts, fill[:, None]], axis=1)
    lengths = (edges[:, 1:] - edges[:, :-1]).astype(jnp.int32)
    single = jnp.zeros((DOCS,), jnp.int32).at[0].set(ROW_TOKENS)
    return lengths.at[PACKED_ROWS - 1].set(single)


def block_scale(stream_key, dims, cuts, low, top_value):
    def one(axis_at, parts):
        steps = jax.random.uniform(jax.random.fold_in(jax.random.fold_in(stream_key, 6), axis_at), (parts,), jnp.float32, low / len(cuts), top_value / len(cuts))
        return jnp.repeat(jnp.exp(steps), dims[axis_at] // parts).reshape((-1,) + (1,) * (len(dims) - axis_at - 1))

    loudness = one(*cuts[0])
    for cut in cuts[1:]:
        loudness = loudness * one(*cut)
    return loudness


def bell_draw(stream_key, dims, deviation, limit, shards=(), kind=jnp.bfloat16):
    entries = deviation * jax.random.normal(stream_key, dims, jnp.float32)
    if shards:
        entries = entries * block_scale(stream_key, dims, shards, -0.22, 0.18)
    return jnp.clip(entries, -limit, limit).astype(kind)


def setup_inputs(seed: int = 0) -> dict:
    key_of = jax.random.split(jax.random.key(seed), 9)
    hidden_in = draw_hidden_in(jax.random.fold_in(key_of[8], 71), 0)
    input_norm_gain = jnp.clip(1.0 + 0.1 * jax.random.normal(key_of[1], (MODEL_WIDTH,), jnp.float32), 0.5, 1.5).astype(jnp.bfloat16)
    w_query = draw_w_query(jax.random.fold_in(key_of[8], 71), 0)
    w_keyval = draw_w_keyval(jax.random.fold_in(key_of[8], 71), 0)
    b_query = bell_draw(key_of[4], (QW,), 0.5, 3.0, ((0, 4),), jnp.float32)
    b_keyval = bell_draw(key_of[5], (2, KW), 0.5, 3.0, ((1, 4),), jnp.float32)
    upstream = bell_draw(key_of[6], (TOKENS, QW), 1.0, 6.0, ((0, 64), (1, 4)))
    lengths = draw_lengths(jax.random.fold_in(key_of[8], 71), 0)
    return dict(hidden_in=hidden_in, input_norm_gain=input_norm_gain, w_query=w_query, w_keyval=w_keyval, b_query=b_query, b_keyval=b_keyval, upstream=upstream, lengths=lengths)


def doc_layout(lengths, width):
    ends = jnp.cumsum(lengths, axis=1).astype(jnp.int32)
    place = jnp.arange(width, dtype=jnp.int32)[None, :, None]
    passed = place >= ends[:, None, :]
    segment = lax.optimization_barrier(jnp.sum(passed.astype(jnp.int32), axis=2))
    start = lax.optimization_barrier(jnp.max(jnp.where(passed, ends[:, None, :], 0), axis=2))
    position = (place[:, :, 0] - start).astype(jnp.float32)
    real = (place[:, :, 0] < ends[:, -1:]).astype(jnp.float32)
    return (segment, position, real)

def rotation(position, head_dim):
    half = head_dim // 2
    freq = 1000000.0 ** (-(2.0 * jnp.arange(half, dtype=jnp.float32)) / head_dim)
    angle = position[..., None] * freq
    return (jnp.cos(angle), jnp.sin(angle))

def apply_rotary(values, cosine_table, sine_table, sign):
    half = values.shape[-1] // 2
    first_entry = values[..., :half]
    second = values[..., half:]
    cos_b = cosine_table[:, :, None, :]
    sin_b = sign * sine_table[:, :, None, :]
    return jnp.concatenate([first_entry * cos_b - second * sin_b, second * cos_b + first_entry * sin_b], axis=-1)

def mix(form, left, right):
    return jnp.einsum(form, left.astype(jnp.float32), right.astype(jnp.float32))

def attend(query_rotated, key_rotated, value_rows, segment, attention_gradient):
    width = query_rotated.shape[1]
    scale = 1.0 / query_rotated.shape[-1] ** 0.5
    scores = mix('rqkgd,rskd->rkgqs', query_rotated, key_rotated) * scale
    causal = jnp.arange(width)[:, None] >= jnp.arange(width)[None, :]
    same = segment[:, :, None] == segment[:, None, :]
    allowed = (same & causal[None])[:, None, None, :, :]
    scores = jnp.where(allowed, scores, -1e+30)
    top = lax.optimization_barrier(jnp.max(scores, axis=-1, keepdims=True))
    expo = jnp.exp(scores - top)
    probs = expo / lax.optimization_barrier(jnp.sum(expo, axis=-1, keepdims=True))
    probs_b = probs.astype(jnp.bfloat16)
    output = mix('rkgqs,rskd->rqkgd', probs_b, value_rows).astype(jnp.bfloat16)
    d_probs = mix('rqkgd,rskd->rkgqs', attention_gradient, value_rows)
    d_value = mix('rkgqs,rqkgd->rskd', probs_b, attention_gradient)
    d_scores = probs * (d_probs - lax.optimization_barrier(jnp.sum(probs * d_probs, axis=-1, keepdims=True))) * scale
    d_scores_b = d_scores.astype(jnp.bfloat16)
    d_qrot = mix('rkgqs,rskd->rqkgd', d_scores_b, key_rotated)
    d_krot = mix('rkgqs,rqkgd->rskd', d_scores_b, query_rotated)
    return (output, d_qrot, d_krot, d_value)

def reference(hidden_in, input_norm_gain, w_query, w_keyval, b_query, b_keyval, upstream, lengths):
    group_factor = QUERY_HEADS // KEYVALUE_HEADS
    input_complete = hidden_in.astype(jnp.float32)
    reciprocal_deviation = lax.rsqrt(lax.optimization_barrier(jnp.mean(input_complete * input_complete, axis=1, keepdims=True)) + 1e-06)
    input_centered = input_complete * reciprocal_deviation
    normalized_input = (input_centered * input_norm_gain.astype(jnp.float32)).astype(jnp.bfloat16)
    query = jnp.dot(normalized_input, w_query, preferred_element_type=jnp.float32) + b_query
    key = jnp.dot(normalized_input, w_keyval[0], preferred_element_type=jnp.float32) + b_keyval[0]
    value_rows = jnp.dot(normalized_input, w_keyval[1], preferred_element_type=jnp.float32) + b_keyval[1]
    segment, position, real = doc_layout(lengths, ROW_TOKENS)
    cosine_table, sine_table = rotation(position, HEAD_SIZE)
    query_rotated = apply_rotary(query.reshape(PACKED_ROWS, ROW_TOKENS, QUERY_HEADS, HEAD_SIZE), cosine_table, sine_table, 1.0).astype(jnp.bfloat16)
    query_rotated = query_rotated.reshape(PACKED_ROWS, ROW_TOKENS, KEYVALUE_HEADS, group_factor, HEAD_SIZE)
    key_rotated = apply_rotary(key.reshape(PACKED_ROWS, ROW_TOKENS, KEYVALUE_HEADS, HEAD_SIZE), cosine_table, sine_table, 1.0).astype(jnp.bfloat16)
    value_broadcast = value_rows.astype(jnp.bfloat16).reshape(PACKED_ROWS, ROW_TOKENS, KEYVALUE_HEADS, HEAD_SIZE)
    total = jnp.sum(lengths).astype(jnp.float32)
    weight = real * PACKED_ROWS / total
    attention_gradient = (upstream.astype(jnp.float32).reshape(PACKED_ROWS, ROW_TOKENS, QUERY_HEADS, HEAD_SIZE) * weight[:, :, None, None]).astype(jnp.bfloat16)
    attention_gradient = attention_gradient.reshape(PACKED_ROWS, ROW_TOKENS, KEYVALUE_HEADS, group_factor, HEAD_SIZE)
    output, d_qrot, d_krot, d_value = attend(query_rotated, key_rotated, value_broadcast, segment, attention_gradient)
    attended = output.reshape(TOKENS, QW)
    d_query = apply_rotary(d_qrot.reshape(PACKED_ROWS, ROW_TOKENS, QUERY_HEADS, HEAD_SIZE), cosine_table, sine_table, -1.0).astype(jnp.bfloat16).reshape(TOKENS, QW)
    d_key = apply_rotary(d_krot, cosine_table, sine_table, -1.0).astype(jnp.bfloat16).reshape(TOKENS, KW)
    d_val = d_value.astype(jnp.bfloat16).reshape(TOKENS, KW)
    grad_query = jnp.dot(normalized_input.T, d_query, preferred_element_type=jnp.float32)
    grad_keyval = jnp.stack([jnp.dot(normalized_input.T, d_key, preferred_element_type=jnp.float32), jnp.dot(normalized_input.T, d_val, preferred_element_type=jnp.float32)])
    grad_bias_query = lax.optimization_barrier(jnp.sum(d_query.astype(jnp.float32), axis=0))
    grad_bias_keyval = jnp.stack([lax.optimization_barrier(jnp.sum(d_key.astype(jnp.float32), axis=0)), lax.optimization_barrier(jnp.sum(d_val.astype(jnp.float32), axis=0))])
    normalized_gradient = jnp.dot(d_query, w_query.T, preferred_element_type=jnp.float32)
    normalized_gradient = normalized_gradient + jnp.dot(d_key, w_keyval[0].T, preferred_element_type=jnp.float32)
    normalized_gradient = normalized_gradient + jnp.dot(d_val, w_keyval[1].T, preferred_element_type=jnp.float32)
    gain_gradient = lax.optimization_barrier(jnp.sum(normalized_gradient * input_centered, axis=0))
    return (attended, grad_query, grad_keyval, grad_bias_query, grad_bias_keyval, gain_gradient)
```

```python
import functools

import jax
import jax.numpy as jnp
from jax import lax
from jax.experimental import pallas as pl
from jax.experimental.pallas import tpu as pltpu
from jax.sharding import PartitionSpec as P

D = 128
ROW = 128
XS, ZS, CS = 4, 8, 2
BF = jnp.bfloat16
F4 = jnp.float32
ORDER = [0, 1, 7, 2, 6, 3, 5, 4]
PLACE = [ORDER.index(dz) for dz in range(8)]


def _perm(move):
    pairs = []
    for x in range(XS):
        for z in range(ZS):
            for c in range(CS):
                a, b, e = move(x, z, c)
                pairs.append(((x * ZS + z) * CS + c, ((a % XS) * ZS + b % ZS) * CS + e % CS))
    return pairs


CORE = _perm(lambda x, z, c: (x, z, 1 - c))
XP = _perm(lambda x, z, c: (x + 1, z, c))
XM = _perm(lambda x, z, c: (x - 1, z, c))
ZP = _perm(lambda x, z, c: (x, z + 1, c))
ZM = _perm(lambda x, z, c: (x, z - 1, c))
FLIPS = [
    CORE,
    _perm(lambda x, z, c: (x ^ 1, z, c)),
    _perm(lambda x, z, c: (x ^ 2, z, c)),
    _perm(lambda x, z, c: (x, z ^ 1, c)),
    _perm(lambda x, z, c: (x, z ^ 2, c)),
    _perm(lambda x, z, c: (x, z ^ 4, c)),
]


def send(a, perm):
    return lax.ppermute(a, "dp", perm)


def add(*parts):
    total = parts[0].astype(F4)
    for p in parts[1:]:
        total = total + p.astype(F4)
    return total.astype(BF)


def norm_kernel(pos_ref, h_ref, xt_ref, xr_ref):
    tokens, width = h_ref.shape
    ss = jnp.zeros((tokens, 1), F4)
    for b in range(8):
        h = h_ref[:, b * 640 : (b + 1) * 640].astype(F4)
        ss = ss + jnp.sum(h * h, axis=1, keepdims=True)
    rstd = lax.rsqrt(ss / width + 1e-06)
    x, z, c = pos_ref[0], pos_ref[1], pos_ref[2]
    for b in range(8):
        xh = (h_ref[:, b * 640 : (b + 1) * 640].astype(F4) * rstd).astype(BF)
        xt = xh.T
        for j in range(8):
            dx = lax.rem(b // 2 - x + XS, XS)
            dz = lax.rem((b % 2) * 4 + j // 2 - z + ZS, ZS)
            dc = lax.rem(j % 2 + c, CS)
            place = jnp.where(dz == 0, 0, jnp.where(dz <= 4, 2 * dz - 1, 16 - 2 * dz))
            xt_ref[dc * 32 + dx * 8 + place] = xt[j * 80 : (j + 1) * 80]
    for b in range(8):
        xr_ref[:, b * 640 : (b + 1) * 640] = xt_ref[b * 8 : (b + 1) * 8].reshape(640, tokens).T


def norm(pos, hidden):
    tokens, width = hidden.shape
    return pl.pallas_call(
        norm_kernel,
        out_shape=(
            jax.ShapeDtypeStruct((64, 80, tokens), BF),
            jax.ShapeDtypeStruct((tokens, width), BF),
        ),
        in_specs=[
            pl.BlockSpec(memory_space=pltpu.SMEM),
            pl.BlockSpec(memory_space=pltpu.VMEM),
        ],
        out_specs=(
            pl.BlockSpec(memory_space=pltpu.VMEM),
            pl.BlockSpec(memory_space=pltpu.VMEM),
        ),
        compiler_params=pltpu.CompilerParams(vmem_limit_bytes=40 * 2**20),
        cost_estimate=pl.CostEstimate(
            flops=10 * tokens * width, bytes_accessed=6 * tokens * width, transcendentals=0
        ),
        name="norm_layout",
    )(pos, hidden)


def dot(a, b, dims):
    return lax.dot_general(a, b, ((dims[:1], dims[1:]), ((), ())), preferred_element_type=F4)


def attention_kernel(a_rows, b_slots, *refs):
    na, nb = len(a_rows), len(b_slots)
    a_refs, refs = refs[:na], refs[na:]
    b_refs, refs = refs[:nb], refs[nb:]
    xr, bq, bkv, up, cosf, sinf, mask, real, out_ref, d_ref, sum_ref, wa, wb, qkv, sems = refs
    copies = []
    for i, (r, off) in enumerate(zip(a_refs, a_rows)):
        copies.append(pltpu.make_async_copy(r, wa.at[pl.ds(off, r.shape[0])], sems.at[i]))
    for i, (r, (blk, place)) in enumerate(zip(b_refs, b_slots)):
        copies.append(
            pltpu.make_async_copy(r, wb.at[pl.ds(blk, 4), place], sems.at[na + i])
        )
    for cp in copies:
        cp.start()
    for cp in copies:
        cp.wait()
    qacc = None
    kvacc = None
    for b in range(8):
        xb = xr[:, b * 640 : (b + 1) * 640]
        pa = dot(xb, wa[b * 640 : (b + 1) * 640], (1, 0))
        pb = dot(xb, wb[b].reshape(640, 256), (1, 0))
        qacc = pa if qacc is None else qacc + pa
        kvacc = pb if kvacc is None else kvacc + pb
    qkv[:, :640] = qacc + bq[...]
    qkv[:, 640:] = kvacc + bkv[...]
    scale = 1.0 / D**0.5
    for r in range(4):
        rows = slice(r * ROW, (r + 1) * ROW)
        co, si = cosf[rows], sinf[rows]

        def turn(v, s):
            return v * co + pltpu.roll(v, 64, 1) * s

        k = turn(qkv[rows, 640:768], si).astype(BF)
        v = qkv[rows, 768:896].astype(BF)
        q = jnp.concatenate(
            [turn(qkv[rows, h * D : (h + 1) * D], si).astype(BF) for h in range(5)], axis=0
        )
        ga = jnp.concatenate(
            [(up[rows, h * D : (h + 1) * D].astype(F4) * real[rows]).astype(BF) for h in range(5)],
            axis=0,
        )
        allowed = jnp.concatenate([mask[r]] * 5, axis=0) > 0.0
        scores = jnp.where(allowed, dot(q, k, (1, 1)) * scale, -1e30)
        expo = jnp.exp(scores - jnp.max(scores, axis=1, keepdims=True))
        probs = expo / jnp.sum(expo, axis=1, keepdims=True)
        probs_b = probs.astype(BF)
        att = dot(probs_b, v, (1, 0)).astype(BF)
        dp = dot(ga, v, (1, 1))
        dv = dot(probs_b, ga, (0, 0))
        ds = probs * (dp - jnp.sum(probs * dp, axis=1, keepdims=True)) * scale
        dsb = ds.astype(BF)
        dq = dot(dsb, k, (1, 0))
        dk = dot(dsb, q, (0, 0))
        for h in range(5):
            hs = slice(h * ROW, (h + 1) * ROW)
            out_ref[rows, h * D : (h + 1) * D] = att[hs]
            d_ref[rows, h * D : (h + 1) * D] = turn(dq[hs], -si).astype(BF)
        d_ref[rows, 640:768] = turn(dk, -si).astype(BF)
        d_ref[rows, 768:896] = dv.astype(BF)
    for i in range(7):
        sum_ref[i : i + 1, :] = jnp.sum(
            d_ref[:, i * D : (i + 1) * D].astype(F4), axis=0, keepdims=True
        )
    sum_ref[7:8, :] = jnp.sum(real[...] + jnp.zeros((4 * ROW, D), F4), axis=0, keepdims=True)


def attention(a_pieces, b_pieces, xr, bq, bkv, up, cosf, sinf, mask, real):
    tokens, width = xr.shape
    a_arrays = [a for a, _ in a_pieces]
    b_arrays = [b for b, _ in b_pieces]
    n = len(a_arrays) + len(b_arrays)
    anyspec = pl.BlockSpec(memory_space=pl.ANY)
    vm = pl.BlockSpec(memory_space=pltpu.VMEM)
    return pl.pallas_call(
        functools.partial(
            attention_kernel, [o for _, o in a_pieces], [o for _, o in b_pieces]
        ),
        out_shape=(
            jax.ShapeDtypeStruct((tokens, 640), BF),
            jax.ShapeDtypeStruct((tokens, 896), BF),
            jax.ShapeDtypeStruct((8, 128), F4),
        ),
        in_specs=[anyspec] * n + [vm] * 8,
        out_specs=(vm, vm, vm),
        scratch_shapes=[
            pltpu.VMEM((width, 640), BF),
            pltpu.VMEM((8, 8, 80, 256), BF),
            pltpu.VMEM((tokens, 896), F4),
            pltpu.SemaphoreType.DMA((n,)),
        ],
        compiler_params=pltpu.CompilerParams(vmem_limit_bytes=48 * 2**20),
        cost_estimate=pl.CostEstimate(
            flops=2 * tokens * width * 896, bytes_accessed=16 * 2**20, transcendentals=400000
        ),
        name="project_attend",
    )(*a_arrays, *b_arrays, xr, bq, bkv, up, cosf, sinf, mask, real)


def grad_kernel(xt_ref, d_ref, ga_ref, gb_ref):
    d = d_ref[...]
    for dx in range(XS):
        g = dot(xt_ref[dx * 8 : (dx + 1) * 8].reshape(640, 512), d, (1, 0)).astype(BF)
        ga_ref[dx] = g[:, :640]
        for p in range(8):
            gb_ref[p, dx] = g[p * 80 : (p + 1) * 80, 640:]


def weight_grad(xt, d, core):
    return pl.pallas_call(
        grad_kernel,
        grid=(1,),
        out_shape=(
            jax.ShapeDtypeStruct((4, 640, 640), BF),
            jax.ShapeDtypeStruct((8, 4, 80, 256), BF),
        ),
        in_specs=[
            pl.BlockSpec((32, 80, 512), lambda i: (core, 0, 0)),
            pl.BlockSpec((512, 896), lambda i: (0, 0)),
        ],
        out_specs=(
            pl.BlockSpec((4, 640, 640), lambda i: (0, 0, 0)),
            pl.BlockSpec((8, 4, 80, 256), lambda i: (0, 0, 0, 0)),
        ),
        compiler_params=pltpu.CompilerParams(vmem_limit_bytes=48 * 2**20),
        cost_estimate=pl.CostEstimate(
            flops=2 * 512 * 2560 * 896, bytes_accessed=8 * 2**20, transcendentals=0
        ),
        name="weight_grad",
    )(xt, d)


def gather_q(w):
    up = [w]
    for _ in range(4):
        up.append(send(up[-1], ZM))
    down = [w]
    for _ in range(3):
        down.append(send(down[-1], ZP))
    chunk = dict((dz, up[dz]) for dz in range(5))
    chunk.update((8 - k, down[k]) for k in range(1, 4))
    pieces = []
    for lo, hi, cut in ((0, 3, 160), (3, 8, 160)):
        g = jnp.concatenate([chunk[dz] for dz in ORDER[lo:hi]], axis=0)
        off = lo * 80
        r1 = send(g, XM)
        r3 = send(g, XP)
        pieces += [(g, off), (r1, 640 + off), (r3, 3 * 640 + off)]
        pieces += [
            (send(r1[:cut], XM), 2 * 640 + off),
            (send(r3[cut:], XP), 2 * 640 + off + cut),
        ]
    return pieces + [(send(a, CORE), 2560 + o) for a, o in pieces]


def gather_kv(w):
    r1 = send(w, XM)
    r3 = send(w, XP)
    r2 = jnp.concatenate([send(r1[:40], XM), send(r3[40:], XP)], axis=0)
    own = jnp.stack([w, r1, r2, r3])
    pieces = [(own, (0, 0))]
    u = own
    for k in range(1, 5):
        u = send(u, ZM)
        pieces.append((u, (0, PLACE[k])))
    u = own
    for k in range(1, 4):
        u = send(u, ZP)
        pieces.append((u, (0, PLACE[8 - k])))
    return pieces + [(send(a, CORE), (4, p)) for a, (_, p) in pieces]


def ring_z(chunk):
    u = chunk[4]
    for dz in (3, 2, 1):
        u = add(send(u, ZP), chunk[dz])
    d = chunk[5]
    for dz in (6, 7):
        d = add(send(d, ZM), chunk[dz])
    return send(u, ZP), send(d, ZM)


def ring_x(blocks, cut):
    b0, b1, b2, b3 = blocks
    t1 = send(b2[:cut], XP)
    t3 = send(b2[cut:], XM)
    s1 = jnp.concatenate([add(b1[:cut], t1), b1[cut:]], axis=0)
    s3 = jnp.concatenate([b3[:cut], add(b3[cut:], t3)], axis=0)
    return send(s1, XP), send(s3, XM)


def scatter_q(own, other):
    swapped = {}
    groups = ((240, 640, 160), (0, 240, 160))
    for lo, hi, _ in groups:
        for dx in (2, 1, 3, 0):
            swapped[lo, dx] = send(other[dx, lo:hi], CORE)
    chunk = {}
    for lo, hi, cut in groups:
        blocks = [add(own[dx, lo:hi], swapped[lo, dx]) for dx in range(4)]
        s1, s3 = ring_x(blocks, cut)
        got = add(blocks[0], s1, s3)
        for i, dz in enumerate(ORDER[lo // 80 : hi // 80]):
            chunk[dz] = got[i * 80 : (i + 1) * 80]
    u, d = ring_z(chunk)
    return chunk[0].astype(F4) + u.astype(F4) + d.astype(F4)


def scatter_kv(own, other):
    swapped = send(other, CORE)
    both = add(own, swapped)
    chunk = dict((dz, both[PLACE[dz]]) for dz in range(8))
    u, d = ring_z(chunk)
    got = add(chunk[0], u, d)
    s1, s3 = ring_x([got[i] for i in range(4)], 40)
    return got[0].astype(F4) + s1.astype(F4) + s3.astype(F4)


def doc_layout(lengths):
    ends = jnp.cumsum(lengths, axis=1)
    place = jnp.arange(ROW, dtype=jnp.int32)[None, :, None]
    passed = place >= ends[:, None, :]
    segment = jnp.sum(passed.astype(jnp.int32), axis=2)
    start = jnp.max(jnp.where(passed, ends[:, None, :], 0), axis=2)
    position = (place[:, :, 0] - start).astype(F4)
    real = (place[:, :, 0] < ends[:, -1:]).astype(F4)
    return segment, position, real


def per_device(hidden, gain, w_query, w_keyval, b_query, b_keyval, upstream, lengths):
    tokens = hidden.shape[0]
    i = lax.axis_index("dp")
    pos = jnp.stack([i // 16, (i // 2) % 8, i % 2]).astype(jnp.int32)
    g32 = gain.astype(F4)[:, None]
    w_kv = jnp.concatenate([w_keyval[0], w_keyval[1]], axis=1)
    a_pieces = gather_q((w_query.astype(F4) * g32).astype(BF))
    b_pieces = gather_kv((w_kv.astype(F4) * g32).astype(BF))
    xt, xr = norm(pos, hidden)

    segment, position, real = doc_layout(lengths)
    freq = 1000000.0 ** (-(2.0 * jnp.arange(D // 2, dtype=F4)) / D)
    angle = position.reshape(tokens, 1) * freq
    cos, sin = jnp.cos(angle), jnp.sin(angle)
    cosf = jnp.concatenate([cos, cos], axis=1)
    sinf = jnp.concatenate([-sin, sin], axis=1)
    causal = jnp.arange(ROW)[:, None] >= jnp.arange(ROW)[None, :]
    mask = ((segment[:, :, None] == segment[:, None, :]) & causal[None]).astype(F4)

    attended, d, sums = attention(
        a_pieces,
        b_pieces,
        xr,
        b_query.reshape(1, 640),
        b_keyval.reshape(1, 256),
        upstream,
        cosf,
        sinf,
        mask,
        real.reshape(tokens, 1),
    )
    ga_other, gb_other = weight_grad(xt, d, 1)
    ga_own, gb_own = weight_grad(xt, d, 0)
    g_q = scatter_q(ga_own, ga_other)
    g_kv = scatter_kv(gb_own, gb_other)
    for flip in FLIPS:
        sums = sums + send(sums, flip)

    factor = 4.0 * lax.axis_size("dp") / sums[7, 0]
    scaled = factor * g32
    grad_query = g_q * scaled
    g_kv_scaled = g_kv * scaled
    grad_keyval = jnp.stack([g_kv_scaled[:, :D], g_kv_scaled[:, D:]])
    bias = sums * factor
    grad_bias_query = bias[:5].reshape(640)
    grad_bias_keyval = bias[5:7]
    part = jnp.sum(g_q * w_query.astype(F4), axis=1) + jnp.sum(g_kv * w_kv.astype(F4), axis=1)
    gain_gradient = lax.psum(part * factor, "mp")
    return (attended, grad_query, grad_keyval, grad_bias_query, grad_bias_keyval, gain_gradient)


def solution(mesh):
    return jax.shard_map(
        per_device,
        mesh=mesh,
        in_specs=(
            P("dp", None),
            P("dp"),
            P("dp", "mp"),
            P(None, "dp", "mp"),
            P("mp"),
            P(None, "mp"),
            P("dp", "mp"),
            P("dp", None),
        ),
        out_specs=(
            P("dp", "mp"),
            P("dp", "mp"),
            P(None, "dp", "mp"),
            P("mp"),
            P(None, "mp"),
            P("dp"),
        ),
        check_vma=False,
    )
```

```python
import functools

import jax
import jax.numpy as jnp
from jax import lax
from jax.experimental import pallas as pl
from jax.experimental.pallas import tpu as pltpu
from jax.sharding import PartitionSpec as P

D = 128
ROW = 128
XS, ZS, CS = 4, 8, 2
BF = jnp.bfloat16
F4 = jnp.float32
A_COLS, B_COLS = 512, 384
B_ROWS = 88
PLACE = [0, 1, 3, 5, 7, 6, 4, 2]
ORDER = [0, 1, 7, 2, 6, 3, 5, 4]


def _perm(move):
    pairs = []
    for x in range(XS):
        for z in range(ZS):
            for c in range(CS):
                a, b, e = move(x, z, c)
                pairs.append(((x * ZS + z) * CS + c, ((a % XS) * ZS + b % ZS) * CS + e % CS))
    return pairs


CORE = _perm(lambda x, z, c: (x, z, 1 - c))
X_BY = [_perm(lambda x, z, c, k=k: (x + k, z, c)) for k in range(XS)]
Z_BY = [_perm(lambda x, z, c, k=k: (x, z + k, c)) for k in range(ZS)]
XP, XM, ZP, ZM = X_BY[1], X_BY[3], Z_BY[1], Z_BY[7]
FLIPS = [
    CORE,
    _perm(lambda x, z, c: (x ^ 1, z, c)),
    _perm(lambda x, z, c: (x ^ 2, z, c)),
    _perm(lambda x, z, c: (x, z ^ 1, c)),
    _perm(lambda x, z, c: (x, z ^ 2, c)),
    _perm(lambda x, z, c: (x, z ^ 4, c)),
]


def send(a, perm):
    return lax.ppermute(a, "dp", perm)


def add(*parts):
    total = parts[0].astype(F4)
    for p in parts[1:]:
        total = total + p.astype(F4)
    return total.astype(BF)


def turn_kernel(pos_ref, h_ref, ht_ref, rstd_ref):
    tokens, width = h_ref.shape
    x, z, c = pos_ref[0], pos_ref[1], pos_ref[2]
    ss = jnp.zeros((1, tokens), F4)
    for b in range(8):
        ht = h_ref[:, b * 640 : (b + 1) * 640].T
        hf = ht.astype(F4)
        ss = ss + jnp.sum(hf * hf, axis=0, keepdims=True)
        for j in range(8):
            dx = lax.rem(b // 2 - x + XS, XS)
            dz = lax.rem((b % 2) * 4 + j // 2 - z + ZS, ZS)
            dc = lax.rem(j % 2 + c, CS)
            place = jnp.where(dz == 0, 0, jnp.where(dz <= 4, 2 * dz - 1, 16 - 2 * dz))
            ht_ref[dc * 32 + dx * 8 + place] = ht[j * 80 : (j + 1) * 80]
    rstd_ref[...] = lax.rsqrt(ss / width + 1e-06)


def turn_hidden(pos, hidden):
    tokens, width = hidden.shape
    vm = pl.BlockSpec(memory_space=pltpu.VMEM)
    return pl.pallas_call(
        turn_kernel,
        out_shape=(
            jax.ShapeDtypeStruct((64, 80, tokens), BF),
            jax.ShapeDtypeStruct((1, tokens), F4),
        ),
        in_specs=[pl.BlockSpec(memory_space=pltpu.SMEM), vm],
        out_specs=(vm, vm),
        compiler_params=pltpu.CompilerParams(vmem_limit_bytes=32 * 2**20),
        cost_estimate=pl.CostEstimate(
            flops=4 * tokens * width, bytes_accessed=4 * tokens * width, transcendentals=0
        ),
        name="turn_hidden",
    )(pos, hidden)


def norm_kernel(slots, *refs):
    n = len(slots)
    ht_ref, rstd_ref = refs[n : n + 2]
    nt_ref, nr_ref, total_ref, rows, table, sems = refs[n + 2 :]
    tokens = ht_ref.shape[2]
    copies = [
        pltpu.make_async_copy(r.at[:, :, pl.ds(0, 128)], rows.at[i], sems.at[i])
        for i, r in enumerate(refs[:n])
    ]
    for cp in copies:
        cp.start()
    for cp in copies:
        cp.wait()
    for i, (blk, place) in enumerate(slots):
        for dx in range(4):
            at = (blk + dx) * 8 + place
            table[at : at + 1, :] = rows[i, dx, 80:81, :].astype(F4)
    lane = lax.broadcasted_iota(jnp.int32, (64, 128), 1)
    counts = jnp.where((lane >= 80) & (lane < 84), table[...], 0.0)
    total = jnp.sum(jnp.sum(counts, axis=0, keepdims=True), axis=1, keepdims=True)
    total_ref[...] = total + jnp.zeros((1, 128), F4)
    gains = table[...].T
    rstd = rstd_ref[...]
    for b in range(8):
        for j in range(8):
            i = b * 8 + j
            xhat = ht_ref[i].astype(F4) * rstd
            nt_ref[i] = (xhat * gains[:80, i : i + 1]).astype(BF)
        nr_ref[:, b * 640 : (b + 1) * 640] = nt_ref[b * 8 : (b + 1) * 8].reshape(640, tokens).T


def norm(b_pieces, ht, rstd):
    tokens = ht.shape[2]
    n = len(b_pieces)
    vm = pl.BlockSpec(memory_space=pltpu.VMEM)
    return pl.pallas_call(
        functools.partial(norm_kernel, [slot for _, slot in b_pieces]),
        out_shape=(
            jax.ShapeDtypeStruct(ht.shape, BF),
            jax.ShapeDtypeStruct((tokens, 64 * 80), BF),
            jax.ShapeDtypeStruct((1, 128), F4),
        ),
        in_specs=[pl.BlockSpec(memory_space=pl.ANY)] * n + [vm] * 2,
        out_specs=(vm, vm, vm),
        scratch_shapes=[
            pltpu.VMEM((n, 4, B_ROWS, 128), BF),
            pltpu.VMEM((64, 128), F4),
            pltpu.SemaphoreType.DMA((n,)),
        ],
        compiler_params=pltpu.CompilerParams(vmem_limit_bytes=36 * 2**20),
        cost_estimate=pl.CostEstimate(
            flops=4 * tokens * 5120, bytes_accessed=6 * tokens * 5120, transcendentals=0
        ),
        name="norm_layout",
    )(*[a for a, _ in b_pieces], ht, rstd)


def dot(a, b, dims):
    return lax.dot_general(a, b, ((dims[:1], dims[1:]), ((), ())), preferred_element_type=F4)


def attention_kernel(a_rows, b_slots, *refs):
    na, nb = len(a_rows), len(b_slots)
    a_refs, refs = refs[:na], refs[na:]
    b_refs, refs = refs[:nb], refs[nb:]
    xr, bias, up, cosf, sinf, mask, real, total, out_ref, d_ref, sum_ref, wa, wb, qkv, sems = refs
    a_copies = [[] for _ in range(8)]
    for i, (r, off) in enumerate(zip(a_refs, a_rows)):
        cp = pltpu.make_async_copy(r, wa.at[pl.ds(off, r.shape[0])], sems.at[i])
        a_copies[off // 640].append(cp)
    b_copies = [[], []]
    for i, (r, (blk, place)) in enumerate(zip(b_refs, b_slots)):
        cp = pltpu.make_async_copy(
            r.at[:, pl.ds(0, 80)], wb.at[pl.ds(blk, 4), place], sems.at[na + i]
        )
        b_copies[blk // 4].append(cp)
    for half in range(2):
        for cp in b_copies[half] + [c for blk in a_copies[half * 4 : half * 4 + 4] for c in blk]:
            cp.start()
    acc_a = None
    acc_b = None
    for b in range(8):
        for cp in (b_copies[b // 4] if b % 4 == 0 else []) + a_copies[b]:
            cp.wait()
        xb = xr[:, b * 640 : (b + 1) * 640]
        pa = dot(xb, wa[b * 640 : (b + 1) * 640], (1, 0))
        pb = dot(xb, wb[b].reshape(640, B_COLS), (1, 0))
        acc_a = pa if acc_a is None else acc_a + pa
        acc_b = pb if acc_b is None else acc_b + pb
    qkv[:, :A_COLS] = acc_a + bias[:, :A_COLS]
    qkv[:, A_COLS:] = acc_b + bias[:, A_COLS:]
    scale = 1.0 / D**0.5
    weight = real[...] * 256.0 / total[:, 0:1]
    for r in range(4):
        rows = slice(r * ROW, (r + 1) * ROW)
        co, si = cosf[rows], sinf[rows]

        def turn(v, s):
            return v * co + pltpu.roll(v, 64, 1) * s

        k = turn(qkv[rows, 640:768], si).astype(BF)
        v = qkv[rows, 768:896].astype(BF)
        q = jnp.concatenate(
            [turn(qkv[rows, h * D : (h + 1) * D], si).astype(BF) for h in range(5)], axis=0
        )
        ga = jnp.concatenate(
            [(up[rows, h * D : (h + 1) * D].astype(F4) * weight[rows]).astype(BF) for h in range(5)],
            axis=0,
        )
        allowed = jnp.concatenate([mask[r]] * 5, axis=0) > 0.0
        scores = jnp.where(allowed, dot(q, k, (1, 1)) * scale, -1e30)
        expo = jnp.exp(scores - jnp.max(scores, axis=1, keepdims=True))
        probs = expo / jnp.sum(expo, axis=1, keepdims=True)
        probs_b = probs.astype(BF)
        att = dot(probs_b, v, (1, 0)).astype(BF)
        dp = dot(ga, v, (1, 1))
        dv = dot(probs_b, ga, (0, 0))
        ds = probs * (dp - jnp.sum(probs * dp, axis=1, keepdims=True)) * scale
        dsb = ds.astype(BF)
        dq = dot(dsb, k, (1, 0))
        dk = dot(dsb, q, (0, 0))
        for h in range(5):
            hs = slice(h * ROW, (h + 1) * ROW)
            out_ref[rows, h * D : (h + 1) * D] = att[hs]
            d_ref[rows, h * D : (h + 1) * D] = turn(dq[hs], -si).astype(BF)
        d_ref[rows, 640:768] = turn(dk, -si).astype(BF)
        d_ref[rows, 768:896] = dv.astype(BF)
    for i in range(7):
        sum_ref[i : i + 1, :] = jnp.sum(
            d_ref[:, i * D : (i + 1) * D].astype(F4), axis=0, keepdims=True
        )
    sum_ref[7:8, :] = jnp.zeros((1, D), F4)


def attention(a_pieces, b_pieces, xr, bias, up, cosf, sinf, mask, real, total):
    tokens, width = xr.shape
    a_arrays = [a for a, _ in a_pieces]
    b_arrays = [b for b, _ in b_pieces]
    n = len(a_arrays) + len(b_arrays)
    anyspec = pl.BlockSpec(memory_space=pl.ANY)
    vm = pl.BlockSpec(memory_space=pltpu.VMEM)
    return pl.pallas_call(
        functools.partial(
            attention_kernel, [o for _, o in a_pieces], [o for _, o in b_pieces]
        ),
        out_shape=(
            jax.ShapeDtypeStruct((tokens, 640), BF),
            jax.ShapeDtypeStruct((tokens, 896), BF),
            jax.ShapeDtypeStruct((8, 128), F4),
        ),
        in_specs=[anyspec] * n + [vm] * 8,
        out_specs=(vm, vm, vm),
        scratch_shapes=[
            pltpu.VMEM((width, A_COLS), BF),
            pltpu.VMEM((8, 8, 80, B_COLS), BF),
            pltpu.VMEM((tokens, 896), F4),
            pltpu.SemaphoreType.DMA((n,)),
        ],
        compiler_params=pltpu.CompilerParams(vmem_limit_bytes=48 * 2**20),
        cost_estimate=pl.CostEstimate(
            flops=2 * tokens * width * 896, bytes_accessed=16 * 2**20, transcendentals=400000
        ),
        name="project_attend",
    )(*a_arrays, *b_arrays, xr, bias, up, cosf, sinf, mask, real, total)


def grad_kernel(xt_ref, d_ref, ga_ref, gb_ref):
    d = d_ref[...]
    for dx in range(XS):
        g = dot(xt_ref[dx * 8 : (dx + 1) * 8].reshape(640, 512), d, (1, 0)).astype(BF)
        ga_ref[dx] = g[:, :A_COLS]
        for p in range(8):
            gb_ref[p, dx] = g[p * 80 : (p + 1) * 80, A_COLS:]


def weight_grad(xt, d, core):
    return pl.pallas_call(
        grad_kernel,
        grid=(1,),
        out_shape=(
            jax.ShapeDtypeStruct((4, 640, A_COLS), BF),
            jax.ShapeDtypeStruct((8, 4, 80, B_COLS), BF),
        ),
        in_specs=[
            pl.BlockSpec((32, 80, 512), lambda i: (core, 0, 0)),
            pl.BlockSpec((512, 896), lambda i: (0, 0)),
        ],
        out_specs=(
            pl.BlockSpec((4, 640, A_COLS), lambda i: (0, 0, 0)),
            pl.BlockSpec((8, 4, 80, B_COLS), lambda i: (0, 0, 0, 0)),
        ),
        compiler_params=pltpu.CompilerParams(vmem_limit_bytes=48 * 2**20),
        cost_estimate=pl.CostEstimate(
            flops=2 * 512 * 2560 * 896, bytes_accessed=8 * 2**20, transcendentals=0
        ),
        name="weight_grad",
    )(xt, d)


def tie(*arrays):
    return lax.optimization_barrier(arrays)


def gather(wa, wb, beside):
    chunk = {0: wa}
    own = jnp.stack([wb] + [send(wb, X_BY[4 - dx]) for dx in (1, 2, 3)])
    for k in (4, 3, 5):
        chunk[8 - k] = send(wa, Z_BY[k])
    wa, own = tie(wa, own)
    u, d = send(own, ZM), send(own, ZP)
    b_pieces = [(own, (0, 0)), (u, (0, PLACE[1])), (d, (0, PLACE[7]))]
    for k in (2, 6, 1, 7):
        chunk[8 - k] = send(wa, Z_BY[k])
    g = jnp.concatenate([chunk[dz] for dz in ORDER], axis=0)
    g, u, d = tie(g, u, d)
    r1, r3 = send(g, XM), send(g, XP)
    extra = beside(g)
    u, d = send(u, ZM), send(d, ZP)
    u, d, extra = tie(u, d, extra)
    b_pieces += [(u, (0, PLACE[2])), (d, (0, PLACE[6]))]
    u, d = send(u, ZM), send(d, ZP)
    b_pieces += [(u, (0, PLACE[3])), (d, (0, PLACE[5]))]
    r1, r3, u = tie(r1, r3, u)
    u = send(u, ZM)
    b_pieces.append((u, (0, PLACE[4])))
    a_pieces = [(g, 0), (r1, 640), (r3, 3 * 640)]
    a_pieces += [(send(r1[:320], XM), 2 * 640), (send(r3[320:], XP), 2 * 640 + 320)]
    a_pieces += [(send(a, CORE), 2560 + o) for a, o in a_pieces]
    b_pieces += [(send(a, CORE), (4, p)) for a, (_, p) in b_pieces]
    return a_pieces, b_pieces, extra


def scatter(a_own, a_other, b_own, b_other, sums):
    block = {2: send(a_other[2], CORE)}
    swapped = send(b_other, CORE)
    for dx in (1, 3, 0):
        block[dx] = send(a_other[dx], CORE)
    chunk = dict((dz, add(b_own[PLACE[dz]], swapped[PLACE[dz]])) for dz in range(8))
    u, d = send(chunk[4], ZP), send(chunk[5], ZM)
    b2 = add(a_own[2], block[2])
    t1, t3 = send(b2[:320], XP), send(b2[320:], XM)
    u, d, t1, t3, sums = tie(u, d, t1, t3, sums)
    u, d = send(add(u, chunk[3]), ZP), send(add(d, chunk[6]), ZM)
    s1 = jnp.concatenate(
        [add(a_own[1, :320], block[1][:320], t1), add(a_own[1, 320:], block[1][320:])], axis=0
    )
    s3 = jnp.concatenate(
        [add(a_own[3, :320], block[3][:320]), add(a_own[3, 320:], block[3][320:], t3)], axis=0
    )
    s1, s3 = send(s1, XP), send(s3, XM)
    for flip in FLIPS[:3]:
        sums = sums + send(sums, flip)
    u, d, sums = tie(u, d, sums)
    u, d = send(add(u, chunk[2]), ZP), send(add(d, chunk[7]), ZM)
    for flip in FLIPS[3:]:
        sums = sums + send(sums, flip)
    u, s1, s3, sums = tie(u, s1, s3, sums)
    u = send(add(u, chunk[1]), ZP)
    got = add(a_own[0], block[0], s1, s3).reshape(8, 80, A_COLS)
    total_a = got[0].astype(F4)
    for k in (4, 3, 5, 2, 6, 1, 7):
        total_a = total_a + send(got[PLACE[k]], Z_BY[k]).astype(F4)
    got = add(chunk[0], u, d)
    total_b = got[0].astype(F4)
    for k in (2, 1, 3):
        total_b = total_b + send(got[k], X_BY[k]).astype(F4)
    return total_a, total_b, sums


def doc_layout(lengths):
    ends = jnp.cumsum(lengths, axis=1)
    place = jnp.arange(ROW, dtype=jnp.int32)[None, :, None]
    passed = place >= ends[:, None, :]
    segment = jnp.sum(passed.astype(jnp.int32), axis=2)
    start = jnp.max(jnp.where(passed, ends[:, None, :], 0), axis=2)
    position = (place[:, :, 0] - start).astype(F4)
    real = (place[:, :, 0] < ends[:, -1:]).astype(F4)
    return segment, position, real


def tables(lengths, tokens):
    segment, position, real = doc_layout(lengths)
    freq = 1000000.0 ** (-(2.0 * jnp.arange(D // 2, dtype=F4)) / D)
    angle = position.reshape(tokens, 1) * freq
    cos, sin = jnp.cos(angle), jnp.sin(angle)
    cosf = jnp.concatenate([cos, cos], axis=1)
    sinf = jnp.concatenate([-sin, sin], axis=1)
    causal = jnp.arange(ROW)[:, None] >= jnp.arange(ROW)[None, :]
    mask = ((segment[:, :, None] == segment[:, None, :]) & causal[None]).astype(F4)
    return cosf, sinf, mask, real.reshape(tokens, 1)


def per_device(hidden, gain, w_query, w_keyval, b_query, b_keyval, upstream, lengths):
    tokens = hidden.shape[0]
    i = lax.axis_index("dp")
    pos = jnp.stack([i // 16, (i // 2) % 8, i % 2]).astype(jnp.int32)
    w_all = jnp.concatenate([w_query, w_keyval[0], w_keyval[1]], axis=1)
    extra = jnp.concatenate([gain, jnp.sum(lengths, axis=1).astype(BF)])
    extra = jnp.pad(extra[None, :], ((0, 7), (0, B_COLS - 84)))

    def beside(ready):
        h, l, _ = tie(hidden, lengths, ready)
        return turn_hidden(pos, h) + tables(l, tokens)

    a_pieces, b_pieces, (ht, rstd, cosf, sinf, mask, real) = gather(
        w_query[:, :A_COLS], jnp.concatenate([w_all[:, A_COLS:], extra], axis=0), beside
    )
    xt, xr, total = norm(b_pieces, ht, rstd)
    attended, d, sums = attention(
        a_pieces,
        b_pieces,
        xr,
        jnp.concatenate([b_query, b_keyval[0], b_keyval[1]]).reshape(1, 896),
        upstream,
        cosf,
        sinf,
        mask,
        real,
        total,
    )
    ga_other, gb_other = weight_grad(xt, d, 1)
    ga_own, gb_own = weight_grad(xt, d, 0)
    g_a, g_b, sums = scatter(ga_own, ga_other, gb_own, gb_other, sums)

    grad_query = jnp.concatenate([g_a, g_b[:, : 640 - A_COLS]], axis=1)
    grad_keyval = jnp.stack([g_b[:, 640 - A_COLS : 768 - A_COLS], g_b[:, 768 - A_COLS :]])
    grad_bias_query = sums[:5].reshape(640)
    grad_bias_keyval = sums[5:7]
    w32 = w_all.astype(F4)
    part = jnp.sum(g_a * w32[:, :A_COLS], axis=1) + jnp.sum(g_b * w32[:, A_COLS:], axis=1)
    part = part / gain.astype(F4)
    one, two, three = [
        lax.ppermute(part, "mp", [(y, y ^ k) for y in range(4)]) for k in (1, 2, 3)
    ]
    gain_gradient = (part + one) + (two + three)
    return (attended, grad_query, grad_keyval, grad_bias_query, grad_bias_keyval, gain_gradient)


def solution(mesh):
    return jax.shard_map(
        per_device,
        mesh=mesh,
        in_specs=(
            P("dp", None),
            P("dp"),
            P("dp", "mp"),
            P(None, "dp", "mp"),
            P("mp"),
            P(None, "mp"),
            P("dp", "mp"),
            P("dp", None),
        ),
        out_specs=(
            P("dp", "mp"),
            P("dp", "mp"),
            P(None, "dp", "mp"),
            P("mp"),
            P(None, "mp"),
            P("dp"),
        ),
        check_vma=False,
    )
```

```python
import functools

import jax
import jax.numpy as jnp
from jax import lax
from jax.experimental import pallas as pl
from jax.experimental.pallas import tpu as pltpu
from jax.sharding import PartitionSpec as P

D = 128
ROW = 128
XS, ZS, CS = 4, 8, 2
BF = jnp.bfloat16
F4 = jnp.float32
A_COLS, B_COLS = 512, 384
W_ROWS = 88


def _perm(move):
    pairs = []
    for x in range(XS):
        for z in range(ZS):
            for c in range(CS):
                a, b, e = move(x, z, c)
                pairs.append(((x * ZS + z) * CS + c, ((a % XS) * ZS + b % ZS) * CS + e % CS))
    return pairs


CORE = _perm(lambda x, z, c: (x, z, 1 - c))
X_BY = [_perm(lambda x, z, c, k=k: (x + k, z, c)) for k in range(XS)]
RING = _perm(lambda x, z, c: (x, z + 1 - 2 * c, c))
BACK = _perm(lambda x, z, c: (x, z - 1 + 2 * c, c))
FLIPS = [
    CORE,
    _perm(lambda x, z, c: (x ^ 1, z, c)),
    _perm(lambda x, z, c: (x ^ 2, z, c)),
    _perm(lambda x, z, c: (x, z ^ 1, c)),
    _perm(lambda x, z, c: (x, z ^ 2, c)),
    _perm(lambda x, z, c: (x, z ^ 4, c)),
]


def send(a, perm):
    return lax.ppermute(a, "dp", perm)


def add(*parts):
    total = parts[0].astype(F4)
    for p in parts[1:]:
        total = total + p.astype(F4)
    return total.astype(BF)


def tie(*arrays):
    return lax.optimization_barrier(arrays)


def dot(a, b, dims):
    return lax.dot_general(a, b, ((dims[:1], dims[1:]), ((), ())), preferred_element_type=F4)


VM = pl.BlockSpec(memory_space=pltpu.VMEM)
ANY = pl.BlockSpec(memory_space=pl.ANY)


def params(mib):
    return pltpu.CompilerParams(vmem_limit_bytes=mib * 2**20)


def turn_kernel(pos_ref, h_ref, ht_ref, rstd_ref):
    tokens, width = h_ref.shape
    x, z, c = pos_ref[0], pos_ref[1], pos_ref[2]
    ss = jnp.zeros((1, tokens), F4)
    for b in range(8):
        ht = h_ref[:, b * 640 : (b + 1) * 640].T
        hf = ht.astype(F4)
        ss = ss + jnp.sum(hf * hf, axis=0, keepdims=True)
        for j in range(8):
            dx = lax.rem(b // 2 - x + XS, XS)
            e = lax.rem((1 - 2 * c) * (z - (b % 2) * 4 - j // 2) + ZS, ZS)
            dc = lax.rem(j % 2 + c, CS)
            ht_ref[e * 8 + dc * 4 + dx] = ht[j * 80 : (j + 1) * 80]
    rstd_ref[...] = lax.rsqrt(ss / width + 1e-06)


def turn_hidden(pos, hidden):
    tokens, width = hidden.shape
    return pl.pallas_call(
        turn_kernel,
        out_shape=(
            jax.ShapeDtypeStruct((64, 80, tokens), BF),
            jax.ShapeDtypeStruct((1, tokens), F4),
        ),
        in_specs=[pl.BlockSpec(memory_space=pltpu.SMEM), VM],
        out_specs=(VM, VM),
        compiler_params=params(16),
        cost_estimate=pl.CostEstimate(
            flops=4 * tokens * width, bytes_accessed=4 * tokens * width, transcendentals=0
        ),
        name="turn_hidden",
    )(pos, hidden)


def project_blocks(blocks, maps, wa_refs, wb_refs, ht_ref, rstd_ref, nt_ref, scratch):
    hs, wa, wb, table, sems = scratch
    groups = []
    n = 0
    for i, e in enumerate(blocks):
        group = [pltpu.make_async_copy(ht_ref.at[pl.ds(e * 8, 8)], hs.at[i], sems.at[n])]
        n += 1
        for refs, dst in ((wb_refs, wb), (wa_refs, wa)):
            for src, take, dc in maps[i]:
                src = refs[src] if take is None else refs[src].at[take]
                to = dst.at[i] if dc is None else dst.at[i, dc]
                group.append(pltpu.make_async_copy(src, to, sems.at[n]))
                n += 1
        groups.append(group)
    for cp in [cp for group in groups for cp in group]:
        cp.start()
    rstd = rstd_ref[...]
    acc_a = acc_b = None
    for i in range(len(blocks)):
        for cp in groups[i]:
            cp.wait()
        for j in range(8):
            table[j : j + 1, :] = wb[i, j // 4, j % 4, 80:81, 0:128].astype(F4)
        rows = table[...]
        gains = rows.T
        for j in range(8):
            xhat = hs[i, j].astype(F4) * rstd
            nt_ref[i * 8 + j] = (xhat * gains[:80, j : j + 1]).astype(BF)
        xb = nt_ref[i * 8 : (i + 1) * 8].reshape(640, rstd.shape[1]).T
        pa = dot(xb, wa[i].reshape(640, A_COLS), (1, 0))
        pb = dot(xb, wb[i, :, :, :80].reshape(640, B_COLS), (1, 0))
        lane = lax.broadcasted_iota(jnp.int32, (8, 128), 1)
        real = jnp.sum(jnp.where((lane >= 80) & (lane < 84), rows, 0.0), axis=0, keepdims=True)
        if i == 0:
            acc_a, acc_b, acc_real = pa, pb, real
        else:
            acc_a, acc_b, acc_real = acc_a + pa, acc_b + pb, acc_real + real
    return acc_a, acc_b, acc_real


def project_scratch(n, copies):
    return [
        pltpu.VMEM((n, 8, 80, 512), BF),
        pltpu.VMEM((n, 2, 4, 80, A_COLS), BF),
        pltpu.VMEM((n, 2, 4, W_ROWS, B_COLS), BF),
        pltpu.VMEM((8, 128), F4),
        pltpu.SemaphoreType.DMA((copies,)),
    ]


def project_kernel(blocks, maps, count, first, *refs):
    wa_refs, wb_refs = refs[:count], refs[count : 2 * count]
    refs = refs[2 * count :]
    ht_ref, rstd_ref = refs[:2]
    refs = refs[2:]
    if not first:
        old, old_real = refs[:2]
        refs = refs[2:]
    nt_ref, acc, acc_real = refs[:3]
    pa, pb, real = project_blocks(
        blocks, maps, wa_refs, wb_refs, ht_ref, rstd_ref, nt_ref, refs[3:]
    )
    if not first:
        pa = pa + old[:, :A_COLS]
        pb = pb + old[:, A_COLS:]
        real = real + old_real[...]
    acc[:, :A_COLS] = pa
    acc[:, A_COLS:] = pb
    acc_real[...] = real


def project(blocks, maps, wa, wb, ht, rstd, state):
    tokens = ht.shape[2]
    n = len(blocks)
    first = state is None
    copies = n + 2 * sum(len(m) for m in maps)
    return pl.pallas_call(
        functools.partial(project_kernel, blocks, maps, len(wa), first),
        out_shape=(
            jax.ShapeDtypeStruct((8 * n, 80, tokens), BF),
            jax.ShapeDtypeStruct((tokens, 896), F4),
            jax.ShapeDtypeStruct((1, 128), F4),
        ),
        in_specs=[ANY] * (2 * len(wa) + 1) + [VM] * (1 if first else 3),
        out_specs=(VM, VM, VM),
        scratch_shapes=project_scratch(n, copies),
        compiler_params=params(20),
        cost_estimate=pl.CostEstimate(
            flops=2 * n * tokens * 640 * 896, bytes_accessed=n * 2**21, transcendentals=0
        ),
        name="project",
    )(*wa, *wb, ht, rstd, *(() if first else state))


def attention_kernel(blocks, maps, count, *refs):
    wa_refs, wb_refs = refs[:count], refs[count : 2 * count]
    refs = refs[2 * count :]
    ht_ref, rstd_ref, old, old_real, bias, up, cosf, sinf, mask, real = refs[:10]
    nt_ref, out_ref, d_ref, sum_ref, qkv = refs[10:15]
    pa, pb, new_real = project_blocks(
        blocks, maps, wa_refs, wb_refs, ht_ref, rstd_ref, nt_ref, refs[15:]
    )
    qkv[:, :A_COLS] = old[:, :A_COLS] + pa + bias[:, :A_COLS]
    qkv[:, A_COLS:] = old[:, A_COLS:] + pb + bias[:, A_COLS:]
    total = jnp.sum(old_real[...] + new_real, axis=1, keepdims=True)
    scale = 1.0 / D**0.5
    weight = real[...] * 256.0 / total
    for r in range(4):
        rows = slice(r * ROW, (r + 1) * ROW)
        co, si = cosf[rows], sinf[rows]

        def turn(v, s):
            return v * co + pltpu.roll(v, 64, 1) * s

        k = turn(qkv[rows, 640:768], si).astype(BF)
        v = qkv[rows, 768:896].astype(BF)
        q = jnp.concatenate(
            [turn(qkv[rows, h * D : (h + 1) * D], si).astype(BF) for h in range(5)], axis=0
        )
        ga = jnp.concatenate(
            [(up[rows, h * D : (h + 1) * D].astype(F4) * weight[rows]).astype(BF) for h in range(5)],
            axis=0,
        )
        allowed = jnp.concatenate([mask[r]] * 5, axis=0) > 0.0
        scores = jnp.where(allowed, dot(q, k, (1, 1)) * scale, -1e30)
        expo = jnp.exp(scores - jnp.max(scores, axis=1, keepdims=True))
        probs = expo / jnp.sum(expo, axis=1, keepdims=True)
        probs_b = probs.astype(BF)
        att = dot(probs_b, v, (1, 0)).astype(BF)
        dp = dot(ga, v, (1, 1))
        dv = dot(probs_b, ga, (0, 0))
        ds = probs * (dp - jnp.sum(probs * dp, axis=1, keepdims=True)) * scale
        dsb = ds.astype(BF)
        dq = dot(dsb, k, (1, 0))
        dk = dot(dsb, q, (0, 0))
        for h in range(5):
            hs = slice(h * ROW, (h + 1) * ROW)
            out_ref[rows, h * D : (h + 1) * D] = att[hs]
            d_ref[rows, h * D : (h + 1) * D] = turn(dq[hs], -si).astype(BF)
        d_ref[rows, 640:768] = turn(dk, -si).astype(BF)
        d_ref[rows, 768:896] = dv.astype(BF)
    for i in range(7):
        sum_ref[i : i + 1, :] = jnp.sum(
            d_ref[:, i * D : (i + 1) * D].astype(F4), axis=0, keepdims=True
        )
    sum_ref[7:8, :] = jnp.zeros((1, D), F4)


def attention(blocks, maps, wa, wb, ht, rstd, state, bias, up, tables):
    tokens = ht.shape[2]
    copies = len(blocks) + 2 * sum(len(m) for m in maps)
    return pl.pallas_call(
        functools.partial(attention_kernel, blocks, maps, len(wa)),
        out_shape=(
            jax.ShapeDtypeStruct((8, 80, tokens), BF),
            jax.ShapeDtypeStruct((tokens, 640), BF),
            jax.ShapeDtypeStruct((tokens, 896), BF),
            jax.ShapeDtypeStruct((8, 128), F4),
        ),
        in_specs=[ANY] * (2 * len(wa) + 1) + [VM] * 9,
        out_specs=(VM, VM, VM, VM),
        scratch_shapes=[pltpu.VMEM((tokens, 896), F4)] + project_scratch(1, copies),
        compiler_params=params(24),
        cost_estimate=pl.CostEstimate(
            flops=2 * tokens * 1280 * 896, bytes_accessed=8 * 2**20, transcendentals=400000
        ),
        name="attend",
    )(*wa, *wb, ht, rstd, *state, bias, up, *tables)


def grad_kernel(n, nt_ref, d_ref, *outs):
    d = d_ref[...]
    for i in range(n):
        for dc in range(2):
            at = i * 8 + dc * 4
            g = dot(nt_ref[at : at + 4].reshape(320, 512), d, (1, 0)).astype(BF)
            to = dc if i == 0 else 1 - dc
            for dx in range(4):
                rows = g[dx * 80 : (dx + 1) * 80]
                outs[2 * i][to, dx] = rows[:, :A_COLS]
                outs[2 * i + 1][to, dx] = rows[:, A_COLS:]


def weight_grad(nt, d):
    n = nt.shape[0] // 8
    return pl.pallas_call(
        functools.partial(grad_kernel, n),
        out_shape=[
            jax.ShapeDtypeStruct((2, 4, 80, cols), BF) for _ in range(n) for cols in (A_COLS, B_COLS)
        ],
        in_specs=[VM, VM],
        out_specs=[VM] * (2 * n),
        compiler_params=params(12),
        cost_estimate=pl.CostEstimate(
            flops=2 * n * 512 * 640 * 896, bytes_accessed=n * 2**21, transcendentals=0
        ),
        name="weight_grad",
    )(nt, d)


def gather_project(w, pos, hidden, lengths, tokens):
    xs = [w] + [send(w, X_BY[4 - dx]) for dx in (1, 2, 3)]
    own_a = jnp.stack([a[:80, :A_COLS] for a in xs])
    own_b = jnp.stack([a[:, A_COLS:] for a in xs])
    oth_a, oth_b = send(own_a, CORE), send(own_b, CORE)
    ra, rb = [jnp.stack([own_a, oth_a])], [jnp.stack([own_b, oth_b])]
    pair = [[(0, None, None)], [(1, 0, 1), (1, 1, 0)]]
    single = [[(0, None, 0), (1, None, 1)]]
    ra.append(send(ra[0], RING))
    rb.append(send(rb[0], RING))
    hidden, lengths, _ = tie(hidden, lengths, ra[0])
    ht, rstd = turn_hidden(pos, hidden)
    tabs = tables(lengths, tokens)
    nts = []
    state = None
    for k in (1, 2, 3):
        if k == 1:
            ra[1], ht, rstd, *tabs = tie(ra[1], ht, rstd, *tabs)
        else:
            ra[k], *state = tie(ra[k], *state)
        last = (lambda r: r[0]) if k == 3 else (lambda r: r)
        ra.append(send(last(ra[k]), RING))
        swap_a = send(ra[k], CORE)
        rb.append(send(last(rb[k]), RING))
        swap_b = send(rb[k], CORE)
        if k == 1:
            nt, *state = project([0], single, (own_a, oth_a), (own_b, oth_b), ht, rstd, None)
            nts.append(nt)
        nt, *state = project(
            [k, 8 - k], pair, (ra[k], swap_a), (rb[k], swap_b), ht, rstd, state
        )
        nts.append(nt)
    wa = (ra[4], send(ra[4], CORE))
    wb = (rb[4], send(rb[4], CORE))
    return ([4], single, wa, wb, ht, rstd, state), tabs, nts


def scatter(nts, d, sums):
    near, far = {}, {}
    near[4] = weight_grad(nts[4], d)
    for k in (3, 2, 1):
        g = weight_grad(nts[k], d)
        near[k], far[k] = g[:2], g[2:]
    near[0] = weight_grad(nts[0], d)
    t = [None, None]
    for p in range(2):
        got = send(near[4][p][1], CORE)
        t[p] = send(add(near[4][p][0], got), BACK)
    for k in (3, 2, 1):
        if k == 3:
            t[0], sums = tie(t[0], sums)
            for flip in FLIPS[:3]:
                sums = sums + send(sums, flip)
        for p in range(2):
            got = send(far[k][p], CORE)
            if k == 3:
                s = jnp.stack([add(near[k][p][0], got[0], t[p]), add(near[k][p][1], got[1])])
            else:
                s = add(near[k][p], got, t[p])
            t[p] = send(s, BACK)
    t[1], sums = tie(t[1], sums)
    for flip in FLIPS[3:]:
        sums = sums + send(sums, flip)
    parts = []
    for p in range(2):
        got = send(add(near[0][p][1], t[p][1]), CORE)
        parts.append(add(near[0][p][0], t[p][0], got))
    y = [jnp.concatenate([parts[0][k], parts[1][k]], axis=1) for k in range(4)]
    total = y[0].astype(F4)
    for k in (2, 1, 3):
        total = total + send(y[k], X_BY[k]).astype(F4)
    return total, sums


def doc_layout(lengths):
    ends = jnp.cumsum(lengths, axis=1)
    place = jnp.arange(ROW, dtype=jnp.int32)[None, :, None]
    passed = place >= ends[:, None, :]
    segment = jnp.sum(passed.astype(jnp.int32), axis=2)
    start = jnp.max(jnp.where(passed, ends[:, None, :], 0), axis=2)
    position = (place[:, :, 0] - start).astype(F4)
    real = (place[:, :, 0] < ends[:, -1:]).astype(F4)
    return segment, position, real


def tables(lengths, tokens):
    segment, position, real = doc_layout(lengths)
    freq = 1000000.0 ** (-(2.0 * jnp.arange(D // 2, dtype=F4)) / D)
    angle = position.reshape(tokens, 1) * freq
    cos, sin = jnp.cos(angle), jnp.sin(angle)
    cosf = jnp.concatenate([cos, cos], axis=1)
    sinf = jnp.concatenate([-sin, sin], axis=1)
    causal = jnp.arange(ROW)[:, None] >= jnp.arange(ROW)[None, :]
    mask = ((segment[:, :, None] == segment[:, None, :]) & causal[None]).astype(F4)
    return cosf, sinf, mask, real.reshape(tokens, 1)


def per_device(hidden, gain, w_query, w_keyval, b_query, b_keyval, upstream, lengths):
    tokens = hidden.shape[0]
    i = lax.axis_index("dp")
    pos = jnp.stack([i // 16, (i // 2) % 8, i % 2]).astype(jnp.int32)
    w_all = jnp.concatenate([w_query, w_keyval[0], w_keyval[1]], axis=1)
    extra = jnp.concatenate([gain, jnp.sum(lengths, axis=1).astype(BF)])
    extra = jnp.pad(extra[None, :], ((0, 7), (A_COLS, B_COLS - 84)))
    last, tabs, nts = gather_project(
        jnp.concatenate([w_all, extra], axis=0), pos, hidden, lengths, tokens
    )
    bias = jnp.concatenate([b_query, b_keyval[0], b_keyval[1]]).reshape(1, 896)
    nt, attended, d, sums = attention(*last, bias, upstream, tabs)
    g, sums = scatter(nts + [nt], d, sums)
    grad_query = g[:, :640]
    grad_keyval = jnp.stack([g[:, 640:768], g[:, 768:]])
    grad_bias_query = sums[:5].reshape(640)
    grad_bias_keyval = sums[5:7]
    part = jnp.sum(g * w_all.astype(F4), axis=1) / gain.astype(F4)
    one, two, three = [
        lax.ppermute(part, "mp", [(y, y ^ k) for y in range(4)]) for k in (1, 2, 3)
    ]
    gain_gradient = (part + one) + (two + three)
    return (attended, grad_query, grad_keyval, grad_bias_query, grad_bias_keyval, gain_gradient)


def solution(mesh):
    return jax.shard_map(
        per_device,
        mesh=mesh,
        in_specs=(
            P("dp", None),
            P("dp"),
            P("dp", "mp"),
            P(None, "dp", "mp"),
            P("mp"),
            P(None, "mp"),
            P("dp", "mp"),
            P("dp", None),
        ),
        out_specs=(
            P("dp", "mp"),
            P("dp", "mp"),
            P(None, "dp", "mp"),
            P("mp"),
            P(None, "mp"),
            P("dp"),
        ),
        check_vma=False,
    )
```

```python
import functools

import jax
import jax.numpy as jnp
from jax import lax
from jax.experimental import pallas as pl
from jax.experimental.pallas import tpu as pltpu
from jax.sharding import PartitionSpec as P

D = 128
ROW = 128
XS, ZS, CS = 4, 8, 2
BF = jnp.bfloat16
F4 = jnp.float32
A_COLS, B_COLS = 512, 384
W_ROWS = 88


def _perm(move):
    pairs = []
    for x in range(XS):
        for z in range(ZS):
            for c in range(CS):
                a, b, e = move(x, z, c)
                pairs.append(((x * ZS + z) * CS + c, ((a % XS) * ZS + b % ZS) * CS + e % CS))
    return pairs


CORE = _perm(lambda x, z, c: (x, z, 1 - c))
X_BY = [_perm(lambda x, z, c, k=k: (x + k, z, c)) for k in range(XS)]
RING = _perm(lambda x, z, c: (x, z + 1 - 2 * c, c))
BACK = _perm(lambda x, z, c: (x, z - 1 + 2 * c, c))
FLIPS = [
    CORE,
    _perm(lambda x, z, c: (x ^ 1, z, c)),
    _perm(lambda x, z, c: (x ^ 2, z, c)),
    _perm(lambda x, z, c: (x, z ^ 1, c)),
    _perm(lambda x, z, c: (x, z ^ 2, c)),
    _perm(lambda x, z, c: (x, z ^ 4, c)),
]


def send(a, perm):
    return lax.ppermute(a, "dp", perm)


def add(*parts):
    total = parts[0].astype(F4)
    for p in parts[1:]:
        total = total + p.astype(F4)
    return total.astype(BF)


def tie(*arrays):
    return lax.optimization_barrier(arrays)


def dot(a, b, dims):
    return lax.dot_general(a, b, ((dims[:1], dims[1:]), ((), ())), preferred_element_type=F4)


VM = pl.BlockSpec(memory_space=pltpu.VMEM)
HBM = pl.BlockSpec(memory_space=pltpu.HBM)


def params(mib):
    return pltpu.CompilerParams(vmem_limit_bytes=mib * 2**20)


def turn_kernel(pos_ref, h_ref, out_ref, rstd_ref, ht_ref, sem):
    tokens, width = h_ref.shape
    x, z, c = pos_ref[0], pos_ref[1], pos_ref[2]
    ss = jnp.zeros((1, tokens), F4)
    for b in range(8):
        ht = h_ref[:, b * 640 : (b + 1) * 640].T
        hf = ht.astype(F4)
        ss = ss + jnp.sum(hf * hf, axis=0, keepdims=True)
        for j in range(8):
            dx = lax.rem(b // 2 - x + XS, XS)
            e = lax.rem((1 - 2 * c) * (z - (b % 2) * 4 - j // 2) + ZS, ZS)
            dc = lax.rem(j % 2 + c, CS)
            ht_ref[e * 8 + dc * 4 + dx] = ht[j * 80 : (j + 1) * 80]
    rstd_ref[...] = lax.rsqrt(ss / width + 1e-06)
    copy = pltpu.make_async_copy(ht_ref, out_ref, sem)
    copy.start()
    copy.wait()


def turn_hidden(pos, hidden):
    tokens, width = hidden.shape
    return pl.pallas_call(
        turn_kernel,
        out_shape=(
            jax.ShapeDtypeStruct((64, 80, tokens), BF),
            jax.ShapeDtypeStruct((1, tokens), F4),
        ),
        in_specs=[pl.BlockSpec(memory_space=pltpu.SMEM), VM],
        out_specs=(HBM, VM),
        scratch_shapes=[pltpu.VMEM((64, 80, tokens), BF), pltpu.SemaphoreType.DMA],
        compiler_params=params(20),
        cost_estimate=pl.CostEstimate(
            flops=4 * tokens * width, bytes_accessed=4 * tokens * width, transcendentals=0
        ),
        name="turn_hidden",
    )(pos, hidden)


def project_blocks(blocks, maps, wa_refs, wb_refs, ht_ref, rstd_ref, nt_ref, scratch):
    hs, wa, wb, table, sems, nt, nt_sem = scratch
    groups = []
    n = 0
    for i, e in enumerate(blocks):
        group = [pltpu.make_async_copy(ht_ref.at[pl.ds(e * 8, 8)], hs.at[i], sems.at[n])]
        n += 1
        for refs, dst in ((wb_refs, wb), (wa_refs, wa)):
            for src, take, dc in maps[i]:
                src = refs[src] if take is None else refs[src].at[take]
                to = dst.at[i] if dc is None else dst.at[i, dc]
                group.append(pltpu.make_async_copy(src, to, sems.at[n]))
                n += 1
        groups.append(group)
    for cp in [cp for group in groups for cp in group]:
        cp.start()
    rstd = rstd_ref[...]
    acc_a = acc_b = None
    outs = []
    for i in range(len(blocks)):
        for cp in groups[i]:
            cp.wait()
        for j in range(8):
            table[j : j + 1, :] = wb[i, j // 4, j % 4, 80:81, 0:128].astype(F4)
        rows = table[...]
        gains = rows.T
        for j in range(8):
            xhat = hs[i, j].astype(F4) * rstd
            nt[i * 8 + j] = (xhat * gains[:80, j : j + 1]).astype(BF)
        part = pl.ds(i * 8, 8)
        out = pltpu.make_async_copy(nt.at[part], nt_ref.at[part], nt_sem.at[i])
        out.start()
        outs.append(out)
        xb = nt[i * 8 : (i + 1) * 8].reshape(640, rstd.shape[1]).T
        pa = dot(xb, wa[i].reshape(640, A_COLS), (1, 0))
        pb = dot(xb, wb[i, :, :, :80].reshape(640, B_COLS), (1, 0))
        lane = lax.broadcasted_iota(jnp.int32, (8, 128), 1)
        real = jnp.sum(jnp.where((lane >= 80) & (lane < 84), rows, 0.0), axis=0, keepdims=True)
        if i == 0:
            acc_a, acc_b, acc_real = pa, pb, real
        else:
            acc_a, acc_b, acc_real = acc_a + pa, acc_b + pb, acc_real + real
    for out in outs:
        out.wait()
    return acc_a, acc_b, acc_real


def project_scratch(n, copies):
    return [
        pltpu.VMEM((n, 8, 80, 512), BF),
        pltpu.VMEM((n, 2, 4, 80, A_COLS), BF),
        pltpu.VMEM((n, 2, 4, W_ROWS, B_COLS), BF),
        pltpu.VMEM((8, 128), F4),
        pltpu.SemaphoreType.DMA((copies,)),
        pltpu.VMEM((8 * n, 80, 512), BF),
        pltpu.SemaphoreType.DMA((n,)),
    ]


def project_kernel(blocks, maps, count, first, *refs):
    wa_refs, wb_refs = refs[:count], refs[count : 2 * count]
    refs = refs[2 * count :]
    ht_ref, rstd_ref = refs[:2]
    refs = refs[2:]
    if not first:
        old, old_real = refs[:2]
        refs = refs[2:]
    nt_ref, acc, acc_real = refs[:3]
    pa, pb, real = project_blocks(
        blocks, maps, wa_refs, wb_refs, ht_ref, rstd_ref, nt_ref, refs[3:]
    )
    if not first:
        pa = pa + old[:, :A_COLS]
        pb = pb + old[:, A_COLS:]
        real = real + old_real[...]
    acc[:, :A_COLS] = pa
    acc[:, A_COLS:] = pb
    acc_real[...] = real


def project(blocks, maps, wa, wb, ht, rstd, state):
    tokens = ht.shape[2]
    n = len(blocks)
    first = state is None
    copies = n + 2 * sum(len(m) for m in maps)
    return pl.pallas_call(
        functools.partial(project_kernel, blocks, maps, len(wa), first),
        out_shape=(
            jax.ShapeDtypeStruct((8 * n, 80, tokens), BF),
            jax.ShapeDtypeStruct((tokens, 896), F4),
            jax.ShapeDtypeStruct((1, 128), F4),
        ),
        in_specs=[HBM] * (2 * len(wa) + 1) + [VM] * (1 if first else 3),
        out_specs=(HBM, VM, VM),
        scratch_shapes=project_scratch(n, copies),
        compiler_params=params(20),
        cost_estimate=pl.CostEstimate(
            flops=2 * n * tokens * 640 * 896, bytes_accessed=n * 2**21, transcendentals=0
        ),
        name="project",
    )(*wa, *wb, ht, rstd, *(() if first else state))


def attention_kernel(blocks, maps, count, *refs):
    wa_refs, wb_refs = refs[:count], refs[count : 2 * count]
    refs = refs[2 * count :]
    ht_ref, rstd_ref, old, old_real, bias, up, cosf, sinf, mask, real = refs[:10]
    nt_ref, out_ref, d_ref, sum_ref, qkv = refs[10:15]
    pa, pb, new_real = project_blocks(
        blocks, maps, wa_refs, wb_refs, ht_ref, rstd_ref, nt_ref, refs[15:]
    )
    qkv[:, :A_COLS] = old[:, :A_COLS] + pa + bias[:, :A_COLS]
    qkv[:, A_COLS:] = old[:, A_COLS:] + pb + bias[:, A_COLS:]
    total = jnp.sum(old_real[...] + new_real, axis=1, keepdims=True)
    scale = 1.0 / D**0.5
    weight = real[...] * 256.0 / total
    for r in range(4):
        rows = slice(r * ROW, (r + 1) * ROW)
        co, si = cosf[rows], sinf[rows]

        def turn(v, s):
            return v * co + pltpu.roll(v, 64, 1) * s

        k = turn(qkv[rows, 640:768], si).astype(BF)
        v = qkv[rows, 768:896].astype(BF)
        q = jnp.concatenate(
            [turn(qkv[rows, h * D : (h + 1) * D], si).astype(BF) for h in range(5)], axis=0
        )
        ga = jnp.concatenate(
            [(up[rows, h * D : (h + 1) * D].astype(F4) * weight[rows]).astype(BF) for h in range(5)],
            axis=0,
        )
        allowed = jnp.concatenate([mask[r]] * 5, axis=0) > 0.0
        scores = jnp.where(allowed, dot(q, k, (1, 1)) * scale, -1e30)
        expo = jnp.exp(scores - jnp.max(scores, axis=1, keepdims=True))
        probs = expo / jnp.sum(expo, axis=1, keepdims=True)
        probs_b = probs.astype(BF)
        att = dot(probs_b, v, (1, 0)).astype(BF)
        dp = dot(ga, v, (1, 1))
        dv = dot(probs_b, ga, (0, 0))
        ds = probs * (dp - jnp.sum(probs * dp, axis=1, keepdims=True)) * scale
        dsb = ds.astype(BF)
        dq = dot(dsb, k, (1, 0))
        dk = dot(dsb, q, (0, 0))
        for h in range(5):
            hs = slice(h * ROW, (h + 1) * ROW)
            out_ref[rows, h * D : (h + 1) * D] = att[hs]
            d_ref[rows, h * D : (h + 1) * D] = turn(dq[hs], -si).astype(BF)
        d_ref[rows, 640:768] = turn(dk, -si).astype(BF)
        d_ref[rows, 768:896] = dv.astype(BF)
    for i in range(7):
        sum_ref[i : i + 1, :] = jnp.sum(
            d_ref[:, i * D : (i + 1) * D].astype(F4), axis=0, keepdims=True
        )
    sum_ref[7:8, :] = jnp.zeros((1, D), F4)


def attention(blocks, maps, wa, wb, ht, rstd, state, bias, up, tables):
    tokens = ht.shape[2]
    copies = len(blocks) + 2 * sum(len(m) for m in maps)
    return pl.pallas_call(
        functools.partial(attention_kernel, blocks, maps, len(wa)),
        out_shape=(
            jax.ShapeDtypeStruct((8, 80, tokens), BF),
            jax.ShapeDtypeStruct((tokens, 640), BF),
            jax.ShapeDtypeStruct((tokens, 896), BF),
            jax.ShapeDtypeStruct((8, D), F4),
        ),
        in_specs=[HBM] * (2 * len(wa) + 1) + [VM] * 9,
        out_specs=(HBM, VM, VM, VM),
        scratch_shapes=[pltpu.VMEM((tokens, 896), F4)] + project_scratch(1, copies),
        compiler_params=params(24),
        cost_estimate=pl.CostEstimate(
            flops=2 * tokens * 1280 * 896, bytes_accessed=8 * 2**20, transcendentals=400000
        ),
        name="attend",
    )(*wa, *wb, ht, rstd, *state, bias, up, *tables)


def grad_kernel(n, nt_ref, d_ref, *refs):
    outs, (nt, sems) = refs[: 2 * n], refs[2 * n :]
    copies = []
    for i in range(n):
        part = pl.ds(i * 8, 8)
        copies.append(pltpu.make_async_copy(nt_ref.at[part], nt.at[part], sems.at[i]))
    for cp in copies:
        cp.start()
    d = d_ref[...]
    for i in range(n):
        copies[i].wait()
        for dc in range(2):
            at = i * 8 + dc * 4
            g = dot(nt[at : at + 4].reshape(320, 512), d, (1, 0)).astype(BF)
            to = dc if i == 0 else 1 - dc
            for dx in range(4):
                rows = g[dx * 80 : (dx + 1) * 80]
                outs[2 * i][to, dx] = rows[:, :A_COLS]
                outs[2 * i + 1][to, dx] = rows[:, A_COLS:]


def weight_grad(nt, d):
    n = nt.shape[0] // 8
    shapes = [(2, 4, 80, A_COLS), (2, 4, 80, B_COLS)] * n
    return pl.pallas_call(
        functools.partial(grad_kernel, n),
        out_shape=[jax.ShapeDtypeStruct(shape, BF) for shape in shapes],
        in_specs=[HBM, VM],
        out_specs=[VM] * (2 * n),
        scratch_shapes=[pltpu.VMEM(nt.shape, BF), pltpu.SemaphoreType.DMA((n,))],
        compiler_params=params(12),
        cost_estimate=pl.CostEstimate(
            flops=2 * n * 512 * 640 * 896, bytes_accessed=n * 2**21, transcendentals=0
        ),
        name="weight_grad",
    )(nt, d)


def gather_project(w, pos, hidden, lengths, bias, tokens):
    xs = [w] + [send(w, X_BY[4 - dx]) for dx in (1, 2, 3)]
    own_a = jnp.stack([a[:80, :A_COLS] for a in xs])
    own_b = jnp.stack([a[:, A_COLS:] for a in xs])
    oth_a, oth_b = send(own_a, CORE), send(own_b, CORE)
    ra, rb = [jnp.stack([own_a, oth_a])], [jnp.stack([own_b, oth_b])]
    pair = [[(0, None, None)], [(1, 0, 1), (1, 1, 0)]]
    single = [[(0, None, 0), (1, None, 1)]]
    ra.append(send(ra[0], RING))
    rb.append(send(rb[0], RING))
    hidden, lengths, bias, _ = tie(hidden, lengths, bias, ra[0])
    ht, rstd = turn_hidden(pos, hidden)
    tabs = (bias,) + tables(lengths, tokens)
    nts = []
    state = None
    for k in (1, 2, 3):
        if k == 1:
            ra[1], ht, rstd, *tabs = tie(ra[1], ht, rstd, *tabs)
        else:
            ra[k], *state = tie(ra[k], *state)
        last = (lambda r: r[0]) if k == 3 else (lambda r: r)
        ra.append(send(last(ra[k]), RING))
        swap_a = send(ra[k], CORE)
        rb.append(send(last(rb[k]), RING))
        swap_b = send(rb[k], CORE)
        if k == 1:
            nt, *state = project([0], single, (own_a, oth_a), (own_b, oth_b), ht, rstd, None)
            nts.append(nt)
        nt, *state = project(
            [k, 8 - k], pair, (ra[k], swap_a), (rb[k], swap_b), ht, rstd, state
        )
        nts.append(nt)
    ra[4], rb[4], *state = tie(ra[4], rb[4], *state)
    wa = (ra[4], send(ra[4], CORE))
    wb = (rb[4], send(rb[4], CORE))
    return ([4], single, wa, wb, ht, rstd, state), tabs, nts


def scatter(nts, d, sums):
    near, far = {}, {}
    near[4] = weight_grad(nts[4], d)
    room = [(1, 2), (2, 3), (3, 4), (4, 6), (6, 8), (8, 0)]
    pending = None
    slot = 0

    def exchange(arrived):
        nonlocal sums, pending, slot
        slot += 1
        if pending is not None and room[pending[0]][1] == slot:
            arrived, got = tie(arrived, pending[1])
            sums = sums + got
            pending = None
        for i, (start, _) in enumerate(room):
            if start == slot:
                arrived, sums = tie(arrived, sums)
                pending = (i, send(sums, FLIPS[i]))
        return arrived

    t = [None, None]
    for p in range(2):
        got = send(near[4][p][1], CORE)
        s = add(near[4][p][0], got)
        if p == 1:
            s, d = tie(s, d)
        t[p] = send(s, BACK)
    for k in (3, 2, 1):
        g = weight_grad(nts[k], d)
        near[k], far[k] = g[:2], g[2:]
        for p in range(2):
            got = send(far[k][p], CORE)
            back = exchange(t[p])
            if k == 3:
                s = jnp.stack([add(near[k][p][0], got[0], back), add(near[k][p][1], got[1])])
            else:
                s = add(near[k][p], got, back)
            if p == 0:
                s, d = tie(s, d)
            t[p] = send(s, BACK)
    near[0] = weight_grad(nts[0], d)
    parts = []
    for p in range(2):
        back = exchange(t[p])
        got = send(add(near[0][p][1], back[1]), CORE)
        parts.append(add(near[0][p][0], back[0], got))
    y = [jnp.concatenate([parts[0][k], parts[1][k]], axis=1) for k in range(4)]
    total = y[0].astype(F4)
    for k in (2, 1, 3):
        total = total + send(y[k], X_BY[k]).astype(F4)
    return total, sums + pending[1]


def doc_layout(lengths):
    ends = jnp.cumsum(lengths, axis=1)
    place = jnp.arange(ROW, dtype=jnp.int32)[None, :, None]
    passed = place >= ends[:, None, :]
    segment = jnp.sum(passed.astype(jnp.int32), axis=2)
    start = jnp.max(jnp.where(passed, ends[:, None, :], 0), axis=2)
    position = (place[:, :, 0] - start).astype(F4)
    real = (place[:, :, 0] < ends[:, -1:]).astype(F4)
    return segment, position, real


def tables(lengths, tokens):
    segment, position, real = doc_layout(lengths)
    freq = 1000000.0 ** (-(2.0 * jnp.arange(D // 2, dtype=F4)) / D)
    angle = position.reshape(tokens, 1) * freq
    cos, sin = jnp.cos(angle), jnp.sin(angle)
    cosf = jnp.concatenate([cos, cos], axis=1)
    sinf = jnp.concatenate([-sin, sin], axis=1)
    causal = jnp.arange(ROW)[:, None] >= jnp.arange(ROW)[None, :]
    mask = ((segment[:, :, None] == segment[:, None, :]) & causal[None]).astype(F4)
    return cosf, sinf, mask, jnp.broadcast_to(real.reshape(tokens, 1), (tokens, D))


def per_device(hidden, gain, w_query, w_keyval, b_query, b_keyval, upstream, lengths):
    tokens = hidden.shape[0]
    i = lax.axis_index("dp")
    pos = jnp.stack([i // 16, (i // 2) % 8, i % 2]).astype(jnp.int32)
    w_all = jnp.concatenate([w_query, w_keyval[0], w_keyval[1]], axis=1)
    extra = jnp.concatenate([gain, jnp.sum(lengths, axis=1).astype(BF)])
    extra = jnp.pad(extra[None, :], ((0, 7), (A_COLS, B_COLS - 84)))
    bias = jnp.concatenate([b_query, b_keyval[0], b_keyval[1]]).reshape(1, 896)
    last, (bias, *tabs), nts = gather_project(
        jnp.concatenate([w_all, extra], axis=0), pos, hidden, lengths, bias, tokens
    )
    nt, attended, d, sums = attention(*last, bias, upstream, tabs)
    g, sums = scatter(nts + [nt], d, sums)
    grad_query = g[:, :640]
    grad_keyval = jnp.stack([g[:, 640:768], g[:, 768:]])
    grad_bias_query = sums[:5].reshape(640)
    grad_bias_keyval = sums[5:7]
    part = jnp.sum(g * w_all.astype(F4), axis=1) / gain.astype(F4)
    one, two, three = [
        lax.ppermute(part, "mp", [(y, y ^ k) for y in range(4)]) for k in (1, 2, 3)
    ]
    gain_gradient = (part + one) + (two + three)
    return (attended, grad_query, grad_keyval, grad_bias_query, grad_bias_keyval, gain_gradient)


def solution(mesh):
    return jax.shard_map(
        per_device,
        mesh=mesh,
        in_specs=(
            P("dp", None),
            P("dp"),
            P("dp", "mp"),
            P(None, "dp", "mp"),
            P("mp"),
            P(None, "mp"),
            P("dp", "mp"),
            P("dp", None),
        ),
        out_specs=(
            P("dp", "mp"),
            P("dp", "mp"),
            P(None, "dp", "mp"),
            P("mp"),
            P(None, "mp"),
            P("dp"),
        ),
        check_vma=False,
    )
```

```python
import functools

import jax
import jax.numpy as jnp
from jax import lax
from jax.experimental import pallas as pl
from jax.experimental.pallas import tpu as pltpu
from jax.sharding import PartitionSpec as P

D = 128
ROW = 128
XS, ZS, CS = 4, 8, 2
BF = jnp.bfloat16
F4 = jnp.float32
A_COLS, B_COLS = 512, 384
W_ROWS = 88


def _perm(move):
    pairs = []
    for x in range(XS):
        for z in range(ZS):
            for c in range(CS):
                a, b, e = move(x, z, c)
                pairs.append(((x * ZS + z) * CS + c, ((a % XS) * ZS + b % ZS) * CS + e % CS))
    return pairs


CORE = _perm(lambda x, z, c: (x, z, 1 - c))
IN_X = [_perm(lambda x, z, c, k=k: (x + k * (1 - 2 * c), z, c)) for k in range(XS)]
IN_Z = [_perm(lambda x, z, c, k=k: (x, z + k * (1 - 2 * c), c)) for k in range(ZS)]
OUT_X = [_perm(lambda x, z, c, k=k: (x - k * (1 - 2 * c), z, c)) for k in range(XS)]
OUT_Z = [_perm(lambda x, z, c, k=k: (x, z - k * (1 - 2 * c), c)) for k in range(ZS)]
FLIPS = [
    CORE,
    _perm(lambda x, z, c: (x ^ 1, z, c)),
    _perm(lambda x, z, c: (x ^ 2, z, c)),
    _perm(lambda x, z, c: (x, z ^ 1, c)),
    _perm(lambda x, z, c: (x, z ^ 2, c)),
    _perm(lambda x, z, c: (x, z ^ 4, c)),
]


def send(a, perm):
    return lax.ppermute(a, "dp", perm)


def add(*parts):
    total = parts[0].astype(F4)
    for p in parts[1:]:
        total = total + p.astype(F4)
    return total.astype(BF)


def tie(*arrays):
    return lax.optimization_barrier(arrays)


def dot(a, b, dims):
    return lax.dot_general(a, b, ((dims[:1], dims[1:]), ((), ())), preferred_element_type=F4)


VM = pl.BlockSpec(memory_space=pltpu.VMEM)
HBM = pl.BlockSpec(memory_space=pltpu.HBM)


def params(mib):
    return pltpu.CompilerParams(vmem_limit_bytes=mib * 2**20)


def cost(flops, size):
    return pl.CostEstimate(flops=flops, bytes_accessed=size, transcendentals=0)


def join_kernel(n, *refs):
    sems = refs[n + 1]
    copies = [pltpu.make_async_copy(refs[i], refs[n].at[i], sems.at[i]) for i in range(n)]
    for cp in copies:
        cp.start()
    for cp in copies:
        cp.wait()


def join(parts):
    n = len(parts)
    shape = (n,) + parts[0].shape
    return pl.pallas_call(
        functools.partial(join_kernel, n),
        out_shape=jax.ShapeDtypeStruct(shape, BF),
        in_specs=[HBM] * n,
        out_specs=HBM,
        scratch_shapes=[pltpu.SemaphoreType.DMA((n,))],
        cost_estimate=cost(0, 2 * n * parts[0].size * 2),
        name="join",
    )(*parts)


def turn_kernel(pos_ref, h_ref, out_ref, rstd_ref, ht_ref, sem):
    tokens, width = h_ref.shape
    x, z, c = pos_ref[0], pos_ref[1], pos_ref[2]
    ss = jnp.zeros((1, tokens), F4)
    for b in range(8):
        ht = h_ref[:, b * 640 : (b + 1) * 640].T
        hf = ht.astype(F4)
        ss = ss + jnp.sum(hf * hf, axis=0, keepdims=True)
        for j in range(8):
            up = 2 * (j % 2) - 1
            f = lax.rem(up * (b // 2 - x) + XS, XS)
            e = lax.rem(up * ((b % 2) * 4 + j // 2 - z) + ZS, ZS)
            dc = lax.rem(j % 2 + c, CS)
            ht_ref[e, dc, f] = ht[j * 80 : (j + 1) * 80]
    rstd_ref[...] = lax.rsqrt(ss / width + 1e-06)
    copy = pltpu.make_async_copy(ht_ref, out_ref, sem)
    copy.start()
    copy.wait()


def turn_hidden(pos, hidden):
    tokens, width = hidden.shape
    shape = (ZS, CS, XS, 80, tokens)
    return pl.pallas_call(
        turn_kernel,
        out_shape=(jax.ShapeDtypeStruct(shape, BF), jax.ShapeDtypeStruct((1, tokens), F4)),
        in_specs=[pl.BlockSpec(memory_space=pltpu.SMEM), VM],
        out_specs=(HBM, VM),
        scratch_shapes=[pltpu.VMEM(shape, BF), pltpu.SemaphoreType.DMA],
        compiler_params=params(20),
        cost_estimate=cost(4 * tokens * width, 4 * tokens * width),
        name="turn_hidden",
    )(pos, hidden)


def project_blocks(blocks, maps, wb_refs, ht_ref, rstd_ref, nt_ref, nr_ref, scratch):
    hs, wb, table, sems, nt, nr, out_sems = scratch
    groups = []
    n = 0
    for i, e in enumerate(blocks):
        group = [pltpu.make_async_copy(ht_ref.at[e], hs.at[i], sems.at[n])]
        n += 1
        for src, dc in maps[i]:
            group.append(pltpu.make_async_copy(wb_refs[src], wb.at[i, dc], sems.at[n]))
            n += 1
        groups.append(group)
    for cp in [cp for group in groups for cp in group]:
        cp.start()
    rstd = rstd_ref[...]
    tokens = rstd.shape[1]
    outs = []
    for i, e in enumerate(blocks):
        for cp in groups[i]:
            cp.wait()
        for j in range(8):
            table[j : j + 1, :] = wb[i, j // 4, j % 4, 80:81, 0:128].astype(F4)
        rows = table[...]
        gains = rows.T
        for j in range(8):
            xhat = hs[i, j // 4, j % 4].astype(F4) * rstd
            nt[i, j // 4, j % 4] = (xhat * gains[:80, j : j + 1]).astype(BF)
        outs.append(pltpu.make_async_copy(nt.at[i], nt_ref.at[e], out_sems.at[2 * i]))
        outs[-1].start()
        nr[i] = nt[i].reshape(640, tokens).T
        if nr_ref is not None:
            outs.append(pltpu.make_async_copy(nr.at[i], nr_ref.at[e], out_sems.at[2 * i + 1]))
            outs[-1].start()
        part = dot(nr[i], wb[i, :, :, :80].reshape(640, B_COLS), (1, 0))
        lane = lax.broadcasted_iota(jnp.int32, (8, 128), 1)
        count = jnp.sum(jnp.where((lane >= 80) & (lane < 84), rows, 0.0), axis=0, keepdims=True)
        acc, real = (part, count) if i == 0 else (acc + part, real + count)
    for out in outs:
        out.wait()
    return acc, real


def project_scratch(n, copies, tokens):
    return [
        pltpu.VMEM((n, CS, XS, 80, tokens), BF),
        pltpu.VMEM((n, CS, XS, W_ROWS, B_COLS), BF),
        pltpu.VMEM((8, 128), F4),
        pltpu.SemaphoreType.DMA((copies,)),
        pltpu.VMEM((n, CS, XS, 80, tokens), BF),
        pltpu.VMEM((n, tokens, 640), BF),
        pltpu.SemaphoreType.DMA((2 * n,)),
    ]


def project_kernel(blocks, maps, count, first, *refs):
    wb_refs, (ht_ref, rstd_ref), refs = refs[:count], refs[count : count + 2], refs[count + 2 :]
    if not first:
        (_, _, old, old_real), refs = refs[:4], refs[4:]
    nt_ref, nr_ref, acc_ref, real_ref = refs[:4]
    acc, real = project_blocks(
        blocks, maps, wb_refs, ht_ref, rstd_ref, nt_ref, nr_ref, refs[4:]
    )
    if not first:
        acc = acc + old[...]
        real = real + old_real[...]
    acc_ref[...] = acc
    real_ref[...] = real


def project(blocks, maps, wb, ht, rstd, state):
    tokens = ht.shape[4]
    n = len(blocks)
    count = len(wb)
    copies = n + sum(len(m) for m in maps)
    state = () if state is None else state
    return pl.pallas_call(
        functools.partial(project_kernel, blocks, maps, count, not state),
        out_shape=(
            jax.ShapeDtypeStruct(ht.shape, BF),
            jax.ShapeDtypeStruct((ZS, tokens, 640), BF),
            jax.ShapeDtypeStruct((tokens, B_COLS), F4),
            jax.ShapeDtypeStruct((1, 128), F4),
        ),
        in_specs=[HBM] * (count + 1) + [VM] + ([HBM, HBM, VM, VM] if state else []),
        out_specs=(HBM, HBM, VM, VM),
        scratch_shapes=project_scratch(n, copies, tokens),
        input_output_aliases={count + 2: 0, count + 3: 1} if state else {},
        compiler_params=params(20),
        cost_estimate=cost(2 * n * tokens * 640 * B_COLS, n * 2**21),
        name="project",
    )(*wb, ht, rstd, *state)


def attention_kernel(blocks, maps, count, wa_slots, *refs):
    wb_refs, refs = refs[:count], refs[count:]
    wa_refs, refs = refs[: len(wa_slots)], refs[len(wa_slots) :]
    ht_ref, rstd_ref, _, nr_in, old, old_real, bias, up, cosf, sinf, mask, real = refs[:12]
    nt_ref, out_ref, d_ref, sum_ref = refs[12:16]
    qkv, wa, nr_all, sems = refs[16:20]
    early = []
    for i, (r, (dc, f)) in enumerate(zip(wa_refs, wa_slots)):
        early.append(pltpu.make_async_copy(r, wa.at[:, dc, f], sems.at[i]))
    others = [e for e in range(ZS) if e not in blocks]
    for i, e in enumerate(others):
        early.append(
            pltpu.make_async_copy(nr_in.at[e], nr_all.at[i], sems.at[len(wa_slots) + i])
        )
    for cp in early:
        cp.start()
    acc_b, new_real = project_blocks(
        blocks, maps, wb_refs, ht_ref, rstd_ref, nt_ref, None, refs[20:]
    )
    last = refs[25]
    for cp in early:
        cp.wait()
    acc_a = dot(last[0], wa[blocks[0]].reshape(640, A_COLS), (1, 0))
    for i, e in enumerate(others):
        acc_a = acc_a + dot(nr_all[i], wa[e].reshape(640, A_COLS), (1, 0))
    qkv[:, :A_COLS] = acc_a + bias[:, :A_COLS]
    qkv[:, A_COLS:] = old[...] + acc_b + bias[:, A_COLS:]
    total = jnp.sum(old_real[...] + new_real, axis=1, keepdims=True)
    scale = 1.0 / D**0.5
    weight = real[...] * 256.0 / total
    for r in range(4):
        rows = slice(r * ROW, (r + 1) * ROW)
        co, si = cosf[rows], sinf[rows]

        def turn(v, s):
            return v * co + pltpu.roll(v, 64, 1) * s

        k = turn(qkv[rows, 640:768], si).astype(BF)
        v = qkv[rows, 768:896].astype(BF)
        q = jnp.concatenate(
            [turn(qkv[rows, h * D : (h + 1) * D], si).astype(BF) for h in range(5)], axis=0
        )
        ga = jnp.concatenate(
            [(up[rows, h * D : (h + 1) * D].astype(F4) * weight[rows]).astype(BF) for h in range(5)],
            axis=0,
        )
        allowed = jnp.concatenate([mask[r]] * 5, axis=0) > 0.0
        scores = jnp.where(allowed, dot(q, k, (1, 1)) * scale, -1e30)
        expo = jnp.exp(scores - jnp.max(scores, axis=1, keepdims=True))
        probs = expo / jnp.sum(expo, axis=1, keepdims=True)
        probs_b = probs.astype(BF)
        att = dot(probs_b, v, (1, 0)).astype(BF)
        dp = dot(ga, v, (1, 1))
        dv = dot(probs_b, ga, (0, 0))
        ds = probs * (dp - jnp.sum(probs * dp, axis=1, keepdims=True)) * scale
        dsb = ds.astype(BF)
        dq = dot(dsb, k, (1, 0))
        dk = dot(dsb, q, (0, 0))
        for h in range(5):
            hs = slice(h * ROW, (h + 1) * ROW)
            out_ref[rows, h * D : (h + 1) * D] = att[hs]
            d_ref[rows, h * D : (h + 1) * D] = turn(dq[hs], -si).astype(BF)
        d_ref[rows, 640:768] = turn(dk, -si).astype(BF)
        d_ref[rows, 768:896] = dv.astype(BF)
    for i in range(7):
        sum_ref[i : i + 1, :] = jnp.sum(
            d_ref[:, i * D : (i + 1) * D].astype(F4), axis=0, keepdims=True
        )
    sum_ref[7:8, :] = jnp.zeros((1, D), F4)


def attention(blocks, maps, wb, wa, wa_slots, ht, rstd, state, bias, up, tables):
    tokens = ht.shape[4]
    copies = len(blocks) + sum(len(m) for m in maps)
    count = len(wb) + len(wa)
    return pl.pallas_call(
        functools.partial(attention_kernel, blocks, maps, len(wb), wa_slots),
        out_shape=(
            jax.ShapeDtypeStruct(ht.shape, BF),
            jax.ShapeDtypeStruct((tokens, 640), BF),
            jax.ShapeDtypeStruct((tokens, 896), BF),
            jax.ShapeDtypeStruct((8, D), F4),
        ),
        in_specs=[HBM] * (count + 1) + [VM, HBM, HBM] + [VM] * 8,
        out_specs=(HBM, VM, VM, VM),
        scratch_shapes=[
            pltpu.VMEM((tokens, 896), F4),
            pltpu.VMEM((ZS, CS, XS, 80, A_COLS), BF),
            pltpu.VMEM((ZS - 1, tokens, 640), BF),
            pltpu.SemaphoreType.DMA((len(wa) + ZS - 1,)),
        ]
        + project_scratch(1, copies, tokens),
        input_output_aliases={count + 2: 0},
        compiler_params=params(36),
        cost_estimate=cost(2 * tokens * 5120 * A_COLS, 16 * 2**20),
        name="attend",
    )(*wb, *wa, ht, rstd, *state, bias, up, *tables)


def grad_kernel(jobs, count, nt_ref, d_ref, *refs):
    outs, (nt, sems) = refs[:count], refs[count:]
    copies = []
    for i, (out, slot, part, e, dc, f) in enumerate(jobs):
        if part == 0:
            cp = pltpu.make_async_copy(nt_ref.at[:, dc, f], nt.at[i], sems.at[i])
        else:
            cp = pltpu.make_async_copy(nt_ref.at[e, dc], nt.at[i, pl.ds(0, XS)], sems.at[i])
        cp.start()
        copies.append(cp)
    for i, (out, slot, part, *_) in enumerate(jobs):
        copies[i].wait()
        if part == 0:
            g = dot(nt[i].reshape(640, 512), d_ref[:, :A_COLS], (1, 0))
            outs[out][slot] = g.astype(BF).reshape(ZS, 80, A_COLS)
        else:
            g = dot(nt[i, :XS].reshape(320, 512), d_ref[:, A_COLS:], (1, 0))
            outs[out][slot] = g.astype(BF).reshape(XS, 80, B_COLS)


def weight_grad(groups, nt, d):
    jobs = [(i, j) + job for i, group in enumerate(groups) for j, job in enumerate(group)]
    n = len(jobs)
    shapes = [
        (len(g),) + ((ZS, 80, A_COLS) if g[0][0] == 0 else (XS, 80, B_COLS)) for g in groups
    ]
    return pl.pallas_call(
        functools.partial(grad_kernel, jobs, len(groups)),
        out_shape=[jax.ShapeDtypeStruct(shape, BF) for shape in shapes],
        in_specs=[HBM, VM],
        out_specs=[VM] * len(groups),
        scratch_shapes=[pltpu.VMEM((n, ZS, 80, 512), BF), pltpu.SemaphoreType.DMA((n,))],
        compiler_params=params(16),
        cost_estimate=cost(n * 2 * 512 * 640 * 512, n * 2**20),
        name="weight_grad",
    )(nt, d)


def gather_project(wa, wb, pos, hidden, lengths, bias, tokens):
    near = {0: wa}
    own_b = jnp.stack([wb] + [send(wb, IN_X[k]) for k in (1, 2, 3)])
    for k in (4, 3, 5):
        near[k] = send(wa, IN_Z[k])
    wa, own_b = tie(wa, own_b)
    for k in (2, 6, 1, 7):
        near[k] = send(wa, IN_Z[k])
    oth_b = send(own_b, CORE)
    b0, b1 = send(own_b, IN_Z[1]), send(oth_b, IN_Z[1])
    own_a = join([near[k] for k in range(ZS)])
    oth_a = send(own_a, CORE)
    a0, a1 = send(own_a, IN_X[1]), send(oth_a, IN_X[1])
    hidden, lengths, bias, _ = tie(hidden, lengths, bias, own_a)
    ht, rstd = turn_hidden(pos, hidden)
    tabs = (bias,) + tables(lengths, tokens)
    b0, ht, rstd, *tabs = tie(b0, ht, rstd, *tabs)
    state = None
    for k in (1, 2, 3):
        if k == 2:
            b0, a0, *state = tie(b0, a0, *state)
        if k == 3:
            b0, a1, *state = tie(b0, a1, *state)
        n0 = send(b0, IN_Z[1])
        q0, q1 = send(b0, CORE), send(b1, CORE)
        n1 = send(b1, IN_Z[1]) if k < 3 else None
        if k == 1:
            state = project([0], [[(0, 0), (1, 1)]], (own_b, oth_b), ht, rstd, None)
        state = project(
            [k, 8 - k], [[(0, 0), (2, 1)], [(1, 1), (3, 0)]], (b0, b1, q0, q1), ht, rstd, state
        )
        b0, b1 = n0, n1
        if k == 2:
            a2 = send(a0, IN_X[1])
    a_pieces = [(own_a, (0, 0)), (oth_a, (1, 0)), (a0, (0, 1)), (a1, (1, 3))]
    a_pieces += [(send(a0, CORE), (1, 1)), (send(a1, CORE), (0, 3))]
    b0, a2, *state = tie(b0, a2, *state)
    a_pieces += [(a2, (0, 2)), (send(a2, CORE), (1, 2))]
    wb = (b0, send(b0, CORE))
    wa, slots = [p[0] for p in a_pieces], [p[1] for p in a_pieces]
    return ([4], [[(0, 0), (1, 1)]], wb, wa, slots, ht, rstd, state), tabs


def scatter(nt, d, sums):
    flips = iter([FLIPS[3], FLIPS[4], FLIPS[5], FLIPS[0], FLIPS[1], FLIPS[2]])
    a_near, a_far, b_near, b_far = weight_grad(
        [[(0, None, 0, 2)], [(0, None, 1, 2)], [(1, 4, 0, None)], [(1, 4, 1, None)]], nt, d
    )
    flip = send(sums, next(flips))
    s_a = add(a_near[0], send(a_far[0], CORE))
    s_b = add(b_near[0], send(b_far[0], CORE))
    s_a, s_b, d = tie(s_a, s_b, d)
    a0, b0, b1 = send(s_a, OUT_X[1]), send(s_b, OUT_Z[1]), None
    for k in (3, 2, 1):
        groups = [[(1, k, 0, None), (1, 8 - k, 1, None)], [(1, k, 1, None), (1, 8 - k, 0, None)]]
        if k == 3:
            groups += [
                [(0, None, 0, 1), (0, None, 1, 3)],
                [(0, None, 1, 1), (0, None, 0, 3)],
            ]
        near, far, *a = weight_grad(groups, nt, d)
        if k == 3:
            b0, d = tie(b0, d)
            a0, d = tie(a0, d)
            a_got = send(a[1], CORE)
            got = send(far, CORE)
            s_a, s_b = add(a[0][1], a_got[1]), add(near[1], got[1])
            s_a, s_b, flip, sums = tie(s_a, s_b, flip, sums)
            a1, b1 = send(s_a, OUT_X[1]), send(s_b, OUT_Z[1])
            b0 = send(add(near[0], got[0], b0), OUT_Z[1])
            a0 = send(add(a[0][0], a_got[0], a0), OUT_X[1])
        else:
            got = send(far, CORE)
            b0 = send(add(near[0], got[0], b0), OUT_Z[1])
            s_b = add(near[1], got[1], b1)
            s_b, flip, sums = tie(s_b, flip, sums)
            b1 = send(s_b, OUT_Z[1])
            if k == 2:
                a1, d = tie(a1, d)
            else:
                a0, d = tie(a0, d)
        sums = sums + flip
        flip = send(sums, next(flips))
    a_own, a_oth, b_own, b_oth = weight_grad(
        [[(0, None, 0, 0)], [(0, None, 1, 0)], [(1, 0, 0, None)], [(1, 0, 1, None)]], nt, d
    )
    a0, flip, sums = tie(a0, flip, sums)
    sums = sums + flip
    flip = send(sums, next(flips))
    a_y = add(a_own[0], a0, send(add(a_oth[0], a1), CORE))
    total_a = a_y[0].astype(F4)
    for k in (4, 3, 5, 2, 6, 1, 7):
        total_a = total_a + send(a_y[k], OUT_Z[k]).astype(F4)
    b0, a_y, flip, sums = tie(b0, a_y, flip, sums)
    sums = sums + flip
    flip = send(sums, next(flips))
    b_y = add(b_own[0], b0, send(add(b_oth[0], b1), CORE))
    total_b = b_y[0].astype(F4)
    for k in (2, 1, 3):
        total_b = total_b + send(b_y[k], OUT_X[k]).astype(F4)
    return total_a, total_b, sums + flip


def doc_layout(lengths):
    ends = jnp.cumsum(lengths, axis=1)
    place = jnp.arange(ROW, dtype=jnp.int32)[None, :, None]
    passed = place >= ends[:, None, :]
    segment = jnp.sum(passed.astype(jnp.int32), axis=2)
    start = jnp.max(jnp.where(passed, ends[:, None, :], 0), axis=2)
    position = (place[:, :, 0] - start).astype(F4)
    real = (place[:, :, 0] < ends[:, -1:]).astype(F4)
    return segment, position, real


def tables(lengths, tokens):
    segment, position, real = doc_layout(lengths)
    freq = 1000000.0 ** (-(2.0 * jnp.arange(D // 2, dtype=F4)) / D)
    angle = position.reshape(tokens, 1) * freq
    cos, sin = jnp.cos(angle), jnp.sin(angle)
    cosf = jnp.concatenate([cos, cos], axis=1)
    sinf = jnp.concatenate([-sin, sin], axis=1)
    causal = jnp.arange(ROW)[:, None] >= jnp.arange(ROW)[None, :]
    mask = ((segment[:, :, None] == segment[:, None, :]) & causal[None]).astype(F4)
    return cosf, sinf, mask, jnp.broadcast_to(real.reshape(tokens, 1), (tokens, D))


def per_device(hidden, gain, w_query, w_keyval, b_query, b_keyval, upstream, lengths):
    tokens = hidden.shape[0]
    i = lax.axis_index("dp")
    pos = jnp.stack([i // 16, (i // 2) % 8, i % 2]).astype(jnp.int32)
    extra = jnp.concatenate([gain, jnp.sum(lengths, axis=1).astype(BF)])
    extra = jnp.pad(extra[None, :], ((0, 7), (0, B_COLS - 84)))
    w_a = w_query[:, :A_COLS]
    w_b = jnp.concatenate([w_query[:, A_COLS:], w_keyval[0], w_keyval[1]], axis=1)
    bias = jnp.concatenate([b_query, b_keyval[0], b_keyval[1]]).reshape(1, 896)
    last, (bias, *tabs) = gather_project(
        w_a, jnp.concatenate([w_b, extra], axis=0), pos, hidden, lengths, bias, tokens
    )
    nt, attended, d, sums = attention(*last, bias, upstream, tabs)
    g_a, g_b, sums = scatter(nt, d, sums)
    grad_query = jnp.concatenate([g_a, g_b[:, : 640 - A_COLS]], axis=1)
    grad_keyval = jnp.stack([g_b[:, 640 - A_COLS : 768 - A_COLS], g_b[:, 768 - A_COLS :]])
    grad_bias_query = sums[:5].reshape(640)
    grad_bias_keyval = sums[5:7]
    part = jnp.sum(g_a * w_a.astype(F4), axis=1) + jnp.sum(g_b * w_b.astype(F4), axis=1)
    part = part / gain.astype(F4)
    one, two, three = [
        lax.ppermute(part, "mp", [(y, y ^ k) for y in range(4)]) for k in (1, 2, 3)
    ]
    gain_gradient = (part + one) + (two + three)
    return (attended, grad_query, grad_keyval, grad_bias_query, grad_bias_keyval, gain_gradient)


def solution(mesh):
    return jax.shard_map(
        per_device,
        mesh=mesh,
        in_specs=(
            P("dp", None),
            P("dp"),
            P("dp", "mp"),
            P(None, "dp", "mp"),
            P("mp"),
            P(None, "mp"),
            P("dp", "mp"),
            P("dp", None),
        ),
        out_specs=(
            P("dp", "mp"),
            P("dp", "mp"),
            P(None, "dp", "mp"),
            P("mp"),
            P(None, "mp"),
            P("dp"),
        ),
        check_vma=False,
    )
```

```python
import functools

import jax
import jax.numpy as jnp
from jax import lax
from jax.experimental import pallas as pl
from jax.experimental.pallas import tpu as pltpu
from jax.sharding import PartitionSpec as P

D = 128
ROW = 128
XS, ZS, CS = 4, 8, 2
BF = jnp.bfloat16
F4 = jnp.float32
A_COLS, B_COLS = 512, 384
W_ROWS = 88


def _perm(move):
    pairs = []
    for x in range(XS):
        for z in range(ZS):
            for c in range(CS):
                a, b, e = move(x, z, c)
                pairs.append(((x * ZS + z) * CS + c, ((a % XS) * ZS + b % ZS) * CS + e % CS))
    return pairs


CORE = _perm(lambda x, z, c: (x, z, 1 - c))
X_BY = [_perm(lambda x, z, c, k=k: (x + k, z, c)) for k in range(XS)]
RING = _perm(lambda x, z, c: (x, z + 1 - 2 * c, c))
BACK = _perm(lambda x, z, c: (x, z - 1 + 2 * c, c))
FLIPS = [
    CORE,
    _perm(lambda x, z, c: (x ^ 1, z, c)),
    _perm(lambda x, z, c: (x ^ 2, z, c)),
    _perm(lambda x, z, c: (x, z ^ 1, c)),
    _perm(lambda x, z, c: (x, z ^ 2, c)),
    _perm(lambda x, z, c: (x, z ^ 4, c)),
]


def send(a, perm):
    return lax.ppermute(a, "dp", perm)


def add(*parts):
    total = parts[0].astype(F4)
    for p in parts[1:]:
        total = total + p.astype(F4)
    return total.astype(BF)


def tie(*arrays):
    return lax.optimization_barrier(arrays)


def dot(a, b, dims):
    return lax.dot_general(a, b, ((dims[:1], dims[1:]), ((), ())), preferred_element_type=F4)


VM = pl.BlockSpec(memory_space=pltpu.VMEM)
HBM = pl.BlockSpec(memory_space=pltpu.HBM)


def params(mib):
    return pltpu.CompilerParams(vmem_limit_bytes=mib * 2**20)


def turn_kernel(pos_ref, h_ref, out_ref, rstd_ref, ht_ref, sem):
    tokens, width = h_ref.shape
    x, z, c = pos_ref[0], pos_ref[1], pos_ref[2]
    ss = jnp.zeros((1, tokens), F4)
    for b in range(8):
        ht = h_ref[:, b * 640 : (b + 1) * 640].T
        hf = ht.astype(F4)
        ss = ss + jnp.sum(hf * hf, axis=0, keepdims=True)
        for j in range(8):
            dx = lax.rem(b // 2 - x + XS, XS)
            e = lax.rem((1 - 2 * c) * (z - (b % 2) * 4 - j // 2) + ZS, ZS)
            dc = lax.rem(j % 2 + c, CS)
            ht_ref[e * 8 + dc * 4 + dx] = ht[j * 80 : (j + 1) * 80]
    rstd_ref[...] = lax.rsqrt(ss / width + 1e-06)
    copy = pltpu.make_async_copy(ht_ref, out_ref, sem)
    copy.start()
    copy.wait()


def turn_hidden(pos, hidden):
    tokens, width = hidden.shape
    return pl.pallas_call(
        turn_kernel,
        out_shape=(
            jax.ShapeDtypeStruct((64, 80, tokens), BF),
            jax.ShapeDtypeStruct((1, tokens), F4),
        ),
        in_specs=[pl.BlockSpec(memory_space=pltpu.SMEM), VM],
        out_specs=(HBM, VM),
        scratch_shapes=[pltpu.VMEM((64, 80, tokens), BF), pltpu.SemaphoreType.DMA],
        compiler_params=params(20),
        cost_estimate=pl.CostEstimate(
            flops=4 * tokens * width, bytes_accessed=4 * tokens * width, transcendentals=0
        ),
        name="turn_hidden",
    )(pos, hidden)


def project_blocks(blocks, maps, wa_refs, wb_refs, ht_ref, rstd_ref, nt_ref, scratch):
    hs, wa, wb, table, sems, nt, nt_sem = scratch
    groups = []
    n = 0
    for i, e in enumerate(blocks):
        group = [pltpu.make_async_copy(ht_ref.at[pl.ds(e * 8, 8)], hs.at[i], sems.at[n])]
        n += 1
        for refs, dst, part in ((wb_refs, wb, 1), (wa_refs, wa, 0)):
            for src, take, dc in maps[part][i]:
                src = refs[src] if take is None else refs[src].at[take]
                to = dst.at[i] if dc is None else dst.at[i, dc]
                group.append(pltpu.make_async_copy(src, to, sems.at[n]))
                n += 1
        groups.append(group)
    for cp in [cp for group in groups for cp in group]:
        cp.start()
    rstd = rstd_ref[...]
    acc_a = acc_b = None
    outs = []
    for i in range(len(blocks)):
        for cp in groups[i]:
            cp.wait()
        for j in range(8):
            table[j : j + 1, :] = wb[i, j // 4, j % 4, 80:81, 0:128].astype(F4)
        rows = table[...]
        gains = rows.T
        for j in range(8):
            xhat = hs[i, j].astype(F4) * rstd
            nt[i * 8 + j] = (xhat * gains[:80, j : j + 1]).astype(BF)
        part = pl.ds(i * 8, 8)
        out = pltpu.make_async_copy(nt.at[part], nt_ref.at[part], nt_sem.at[i])
        out.start()
        outs.append(out)
        xb = nt[i * 8 : (i + 1) * 8].reshape(640, rstd.shape[1]).T
        pa = dot(xb, wa[i].reshape(640, A_COLS), (1, 0))
        pb = dot(xb, wb[i, :, :, :80].reshape(640, B_COLS), (1, 0))
        lane = lax.broadcasted_iota(jnp.int32, (8, 128), 1)
        real = jnp.sum(jnp.where((lane >= 80) & (lane < 84), rows, 0.0), axis=0, keepdims=True)
        if i == 0:
            acc_a, acc_b, acc_real = pa, pb, real
        else:
            acc_a, acc_b, acc_real = acc_a + pa, acc_b + pb, acc_real + real
    for out in outs:
        out.wait()
    return acc_a, acc_b, acc_real


def project_scratch(n, copies):
    return [
        pltpu.VMEM((n, 8, 80, 512), BF),
        pltpu.VMEM((n, 2, 4, 80, A_COLS), BF),
        pltpu.VMEM((n, 2, 4, W_ROWS, B_COLS), BF),
        pltpu.VMEM((8, 128), F4),
        pltpu.SemaphoreType.DMA((copies,)),
        pltpu.VMEM((8 * n, 80, 512), BF),
        pltpu.SemaphoreType.DMA((n,)),
    ]


def project_kernel(blocks, maps, count, first, *refs):
    wa_refs, wb_refs = refs[:count], refs[count : 2 * count]
    refs = refs[2 * count :]
    ht_ref, rstd_ref = refs[:2]
    refs = refs[2:]
    if not first:
        old, old_real = refs[:2]
        refs = refs[2:]
    nt_ref, acc, acc_real = refs[:3]
    pa, pb, real = project_blocks(
        blocks, maps, wa_refs, wb_refs, ht_ref, rstd_ref, nt_ref, refs[3:]
    )
    if not first:
        pa = pa + old[:, :A_COLS]
        pb = pb + old[:, A_COLS:]
        real = real + old_real[...]
    acc[:, :A_COLS] = pa
    acc[:, A_COLS:] = pb
    acc_real[...] = real


def project(blocks, maps, wa, wb, ht, rstd, state):
    tokens = ht.shape[2]
    n = len(blocks)
    first = state is None
    copies = n + sum(len(m) for part in maps for m in part)
    return pl.pallas_call(
        functools.partial(project_kernel, blocks, maps, len(wa), first),
        out_shape=(
            jax.ShapeDtypeStruct((8 * n, 80, tokens), BF),
            jax.ShapeDtypeStruct((tokens, 896), F4),
            jax.ShapeDtypeStruct((1, 128), F4),
        ),
        in_specs=[HBM] * (2 * len(wa) + 1) + [VM] * (1 if first else 3),
        out_specs=(HBM, VM, VM),
        scratch_shapes=project_scratch(n, copies),
        compiler_params=params(20),
        cost_estimate=pl.CostEstimate(
            flops=2 * n * tokens * 640 * 896, bytes_accessed=n * 2**21, transcendentals=0
        ),
        name="project",
    )(*wa, *wb, ht, rstd, *(() if first else state))


def attention_kernel(blocks, maps, count, *refs):
    wa_refs, wb_refs = refs[:count], refs[count : 2 * count]
    refs = refs[2 * count :]
    ht_ref, rstd_ref, old, old_real, bias, up, cosf, sinf, mask, real = refs[:10]
    nt_ref, out_ref, d_ref, sum_ref, qkv = refs[10:15]
    pa, pb, new_real = project_blocks(
        blocks, maps, wa_refs, wb_refs, ht_ref, rstd_ref, nt_ref, refs[15:]
    )
    qkv[:, :A_COLS] = old[:, :A_COLS] + pa + bias[:, :A_COLS]
    qkv[:, A_COLS:] = old[:, A_COLS:] + pb + bias[:, A_COLS:]
    total = jnp.sum(old_real[...] + new_real, axis=1, keepdims=True)
    scale = 1.0 / D**0.5
    weight = real[...] * 256.0 / total
    for r in range(4):
        rows = slice(r * ROW, (r + 1) * ROW)
        co, si = cosf[rows], sinf[rows]

        def turn(v, s):
            return v * co + pltpu.roll(v, 64, 1) * s

        k = turn(qkv[rows, 640:768], si).astype(BF)
        v = qkv[rows, 768:896].astype(BF)
        q = jnp.concatenate(
            [turn(qkv[rows, h * D : (h + 1) * D], si).astype(BF) for h in range(5)], axis=0
        )
        ga = jnp.concatenate(
            [(up[rows, h * D : (h + 1) * D].astype(F4) * weight[rows]).astype(BF) for h in range(5)],
            axis=0,
        )
        allowed = jnp.concatenate([mask[r]] * 5, axis=0) > 0.0
        scores = jnp.where(allowed, dot(q, k, (1, 1)) * scale, -1e30)
        expo = jnp.exp(scores - jnp.max(scores, axis=1, keepdims=True))
        probs = expo / jnp.sum(expo, axis=1, keepdims=True)
        probs_b = probs.astype(BF)
        att = dot(probs_b, v, (1, 0)).astype(BF)
        dp = dot(ga, v, (1, 1))
        dv = dot(probs_b, ga, (0, 0))
        ds = probs * (dp - jnp.sum(probs * dp, axis=1, keepdims=True)) * scale
        dsb = ds.astype(BF)
        dq = dot(dsb, k, (1, 0))
        dk = dot(dsb, q, (0, 0))
        for h in range(5):
            hs = slice(h * ROW, (h + 1) * ROW)
            out_ref[rows, h * D : (h + 1) * D] = att[hs]
            d_ref[rows, h * D : (h + 1) * D] = turn(dq[hs], -si).astype(BF)
        d_ref[rows, 640:768] = turn(dk, -si).astype(BF)
        d_ref[rows, 768:896] = dv.astype(BF)
    for i in range(7):
        sum_ref[i : i + 1, :] = jnp.sum(
            d_ref[:, i * D : (i + 1) * D].astype(F4), axis=0, keepdims=True
        )
    sum_ref[7:8, :] = jnp.zeros((1, D), F4)


def attention(blocks, maps, wa, wb, ht, rstd, state, bias, up, tables):
    tokens = ht.shape[2]
    copies = len(blocks) + sum(len(m) for part in maps for m in part)
    return pl.pallas_call(
        functools.partial(attention_kernel, blocks, maps, len(wa)),
        out_shape=(
            jax.ShapeDtypeStruct((8, 80, tokens), BF),
            jax.ShapeDtypeStruct((tokens, 640), BF),
            jax.ShapeDtypeStruct((tokens, 896), BF),
            jax.ShapeDtypeStruct((8, D), F4),
        ),
        in_specs=[HBM] * (2 * len(wa) + 1) + [VM] * 9,
        out_specs=(HBM, VM, VM, VM),
        scratch_shapes=[pltpu.VMEM((tokens, 896), F4)] + project_scratch(1, copies),
        compiler_params=params(24),
        cost_estimate=pl.CostEstimate(
            flops=2 * tokens * 1280 * 896, bytes_accessed=8 * 2**20, transcendentals=400000
        ),
        name="attend",
    )(*wa, *wb, ht, rstd, *state, bias, up, *tables)


def grad_kernel(n, nt_ref, d_ref, *refs):
    outs, (nt, sems) = refs[: 2 * n], refs[2 * n :]
    copies = []
    for i in range(n):
        part = pl.ds(i * 8, 8)
        copies.append(pltpu.make_async_copy(nt_ref.at[part], nt.at[part], sems.at[i]))
    for cp in copies:
        cp.start()
    d = d_ref[...]
    for i in range(n):
        copies[i].wait()
        for dc in range(2):
            at = i * 8 + dc * 4
            g = dot(nt[at : at + 4].reshape(320, 512), d, (1, 0)).astype(BF)
            out_a = outs[2 * i]
            out_b = outs[2 * (n - 1 - i) + 1]
            to_a = dc if i == 0 else 1 - dc
            to_b = dc if i == n - 1 else 1 - dc
            for dx in range(4):
                rows = g[dx * 80 : (dx + 1) * 80]
                out_a[to_a, dx] = rows[:, :A_COLS]
                out_b[to_b, dx] = rows[:, A_COLS:]


def weight_grad(nt, d):
    n = nt.shape[0] // 8
    shapes = [(2, 4, 80, A_COLS), (2, 4, 80, B_COLS)] * n
    return pl.pallas_call(
        functools.partial(grad_kernel, n),
        out_shape=[jax.ShapeDtypeStruct(shape, BF) for shape in shapes],
        in_specs=[HBM, VM],
        out_specs=[VM] * (2 * n),
        scratch_shapes=[pltpu.VMEM(nt.shape, BF), pltpu.SemaphoreType.DMA((n,))],
        compiler_params=params(12),
        cost_estimate=pl.CostEstimate(
            flops=2 * n * 512 * 640 * 896, bytes_accessed=n * 2**21, transcendentals=0
        ),
        name="weight_grad",
    )(nt, d)


def gather_project(w, pos, hidden, lengths, bias, tokens):
    xs = [w] + [send(w, X_BY[4 - dx]) for dx in (1, 2, 3)]
    own_a = jnp.stack([a[:80, :A_COLS] for a in xs])
    own_b = jnp.stack([a[:, A_COLS:] for a in xs])
    oth_a, oth_b = send(own_a, CORE), send(own_b, CORE)
    ra, rb = [jnp.stack([own_a, oth_a])], [jnp.stack([own_b, oth_b])]
    ring, swapped = [(0, None, None)], [(1, 0, 1), (1, 1, 0)]
    pair = ([ring, swapped], [swapped, ring])
    single = ([[(0, None, 0), (1, None, 1)]],) * 2
    ra.append(send(ra[0], RING))
    rb.append(send(rb[0], BACK))
    hidden, lengths, bias, _ = tie(hidden, lengths, bias, ra[0])
    ht, rstd = turn_hidden(pos, hidden)
    tabs = (bias,) + tables(lengths, tokens)
    nts = []
    state = None
    for k in (1, 2, 3):
        if k == 1:
            ra[1], ht, rstd, *tabs = tie(ra[1], ht, rstd, *tabs)
        else:
            ra[k], *state = tie(ra[k], *state)
        last = (lambda r: r[0]) if k == 3 else (lambda r: r)
        ra.append(send(last(ra[k]), RING))
        swap_a = send(ra[k], CORE)
        rb.append(send(last(rb[k]), BACK))
        swap_b = send(rb[k], CORE)
        if k == 1:
            nt, *state = project([0], single, (own_a, oth_a), (own_b, oth_b), ht, rstd, None)
            nts.append(nt)
        nt, *state = project(
            [k, 8 - k], pair, (ra[k], swap_a), (rb[k], swap_b), ht, rstd, state
        )
        nts.append(nt)
    ra[4], rb[4], *state = tie(ra[4], rb[4], *state)
    wa = (ra[4], send(ra[4], CORE))
    wb = (rb[4], send(rb[4], CORE))
    return ([4], single, wa, wb, ht, rstd, state), tabs, nts


def scatter(nts, d, sums):
    ways = (BACK, RING)
    flips = [FLIPS[3], FLIPS[4], FLIPS[5], FLIPS[0], FLIPS[1], FLIPS[2]]
    room = [(0, 0), (0, 1), (1, 3), (3, 4), (4, 5), (5, 7)]
    pending = (0, send(sums, flips[0]))
    slot = 0

    def exchange(arrived):
        nonlocal sums, pending, slot
        if pending is not None and room[pending[0]][1] == slot:
            arrived, got = tie(arrived, pending[1])
            sums = sums + got
            i = pending[0] + 1
            pending = None
            if i < 6 and room[i][0] == slot:
                pending = (i, send(sums, flips[i]))
        slot += 1
        return arrived

    near4 = weight_grad(nts[4], d)
    t = [None, None]
    for p in range(2):
        s = add(near4[p][0], send(near4[p][1], CORE))
        if p == 1:
            s = exchange(s)
        t[p] = send(s, ways[p])
    for k in (3, 2, 1):
        g = weight_grad(nts[k], d)
        near, far = g[:2], g[2:]
        for p in range(2):
            got = send(far[p], CORE)
            back = exchange(t[p])
            if k == 3:
                s = jnp.stack([add(near[p][0], got[0], back), add(near[p][1], got[1])])
            else:
                s = add(near[p], got, back)
            t[p] = send(s, ways[p])
    near0 = weight_grad(nts[0], d)
    parts = []
    for p in range(2):
        back = exchange(t[p])
        got = send(add(near0[p][1], back[1]), CORE)
        parts.append(add(near0[p][0], back[0], got))
    y = [jnp.concatenate([parts[0][k], parts[1][k]], axis=1) for k in range(4)]
    total = y[0].astype(F4)
    for k in (2, 1, 3):
        total = total + send(y[k], X_BY[k]).astype(F4)
    return total, sums


def doc_layout(lengths):
    ends = jnp.cumsum(lengths, axis=1)
    place = jnp.arange(ROW, dtype=jnp.int32)[None, :, None]
    passed = place >= ends[:, None, :]
    segment = jnp.sum(passed.astype(jnp.int32), axis=2)
    start = jnp.max(jnp.where(passed, ends[:, None, :], 0), axis=2)
    position = (place[:, :, 0] - start).astype(F4)
    real = (place[:, :, 0] < ends[:, -1:]).astype(F4)
    return segment, position, real


def tables(lengths, tokens):
    segment, position, real = doc_layout(lengths)
    freq = 1000000.0 ** (-(2.0 * jnp.arange(D // 2, dtype=F4)) / D)
    angle = position.reshape(tokens, 1) * freq
    cos, sin = jnp.cos(angle), jnp.sin(angle)
    cosf = jnp.concatenate([cos, cos], axis=1)
    sinf = jnp.concatenate([-sin, sin], axis=1)
    causal = jnp.arange(ROW)[:, None] >= jnp.arange(ROW)[None, :]
    mask = ((segment[:, :, None] == segment[:, None, :]) & causal[None]).astype(F4)
    return cosf, sinf, mask, jnp.broadcast_to(real.reshape(tokens, 1), (tokens, D))


def per_device(hidden, gain, w_query, w_keyval, b_query, b_keyval, upstream, lengths):
    tokens = hidden.shape[0]
    i = lax.axis_index("dp")
    pos = jnp.stack([i // 16, (i // 2) % 8, i % 2]).astype(jnp.int32)
    w_all = jnp.concatenate([w_query, w_keyval[0], w_keyval[1]], axis=1)
    extra = jnp.concatenate([gain, jnp.sum(lengths, axis=1).astype(BF)])
    extra = jnp.pad(extra[None, :], ((0, 7), (A_COLS, B_COLS - 84)))
    bias = jnp.concatenate([b_query, b_keyval[0], b_keyval[1]]).reshape(1, 896)
    last, (bias, *tabs), nts = gather_project(
        jnp.concatenate([w_all, extra], axis=0), pos, hidden, lengths, bias, tokens
    )
    nt, attended, d, sums = attention(*last, bias, upstream, tabs)
    g, sums = scatter(nts + [nt], d, sums)
    grad_query = g[:, :640]
    grad_keyval = jnp.stack([g[:, 640:768], g[:, 768:]])
    grad_bias_query = sums[:5].reshape(640)
    grad_bias_keyval = sums[5:7]
    part = jnp.sum(g * w_all.astype(F4), axis=1) / gain.astype(F4)
    one, two, three = [
        lax.ppermute(part, "mp", [(y, y ^ k) for y in range(4)]) for k in (1, 2, 3)
    ]
    gain_gradient = (part + one) + (two + three)
    return (attended, grad_query, grad_keyval, grad_bias_query, grad_bias_keyval, gain_gradient)


def solution(mesh):
    return jax.shard_map(
        per_device,
        mesh=mesh,
        in_specs=(
            P("dp", None),
            P("dp"),
            P("dp", "mp"),
            P(None, "dp", "mp"),
            P("mp"),
            P(None, "mp"),
            P("dp", "mp"),
            P("dp", None),
        ),
        out_specs=(
            P("dp", "mp"),
            P("dp", "mp"),
            P(None, "dp", "mp"),
            P("mp"),
            P(None, "mp"),
            P("dp"),
        ),
        check_vma=False,
    )
```

```python
import functools

import jax
import jax.numpy as jnp
from jax import lax
from jax.experimental import pallas as pl
from jax.experimental.pallas import tpu as pltpu
from jax.sharding import PartitionSpec as P

D = 128
ROW = 128
XS, ZS, CS = 4, 8, 2
BF = jnp.bfloat16
F4 = jnp.float32
A_COLS, B_COLS = 512, 384
W_ROWS = 88


def _perm(move):
    pairs = []
    for x in range(XS):
        for z in range(ZS):
            for c in range(CS):
                a, b, e = move(x, z, c)
                pairs.append(((x * ZS + z) * CS + c, ((a % XS) * ZS + b % ZS) * CS + e % CS))
    return pairs


CORE = _perm(lambda x, z, c: (x, z, 1 - c))
X_BY = [_perm(lambda x, z, c, k=k: (x + k, z, c)) for k in range(XS)]
RING = _perm(lambda x, z, c: (x, z + 1 - 2 * c, c))
BACK = _perm(lambda x, z, c: (x, z - 1 + 2 * c, c))
FLIPS = [
    CORE,
    _perm(lambda x, z, c: (x ^ 1, z, c)),
    _perm(lambda x, z, c: (x ^ 2, z, c)),
    _perm(lambda x, z, c: (x, z ^ 1, c)),
    _perm(lambda x, z, c: (x, z ^ 2, c)),
    _perm(lambda x, z, c: (x, z ^ 4, c)),
]


def send(a, perm):
    return lax.ppermute(a, "dp", perm)


def add(*parts):
    total = parts[0].astype(F4)
    for p in parts[1:]:
        total = total + p.astype(F4)
    return total.astype(BF)


def tie(*arrays):
    return lax.optimization_barrier(arrays)


def dot(a, b, dims):
    return lax.dot_general(a, b, ((dims[:1], dims[1:]), ((), ())), preferred_element_type=F4)


VM = pl.BlockSpec(memory_space=pltpu.VMEM)
HBM = pl.BlockSpec(memory_space=pltpu.HBM)


def params(mib):
    return pltpu.CompilerParams(vmem_limit_bytes=mib * 2**20)


def turn_kernel(pos_ref, h_ref, out_ref, rstd_ref, ht_ref, sem):
    tokens, width = h_ref.shape
    x, z, c = pos_ref[0], pos_ref[1], pos_ref[2]
    ss = jnp.zeros((1, tokens), F4)
    for b in range(8):
        ht = h_ref[:, b * 640 : (b + 1) * 640].T
        hf = ht.astype(F4)
        ss = ss + jnp.sum(hf * hf, axis=0, keepdims=True)
        for j in range(8):
            dx = lax.rem(b // 2 - x + XS, XS)
            e = lax.rem((1 - 2 * c) * (z - (b % 2) * 4 - j // 2) + ZS, ZS)
            dc = lax.rem(j % 2 + c, CS)
            ht_ref[e * 8 + dc * 4 + dx] = ht[j * 80 : (j + 1) * 80]
    rstd_ref[...] = lax.rsqrt(ss / width + 1e-06)
    copy = pltpu.make_async_copy(ht_ref, out_ref, sem)
    copy.start()
    copy.wait()


def turn_hidden(pos, hidden):
    tokens, width = hidden.shape
    return pl.pallas_call(
        turn_kernel,
        out_shape=(
            jax.ShapeDtypeStruct((64, 80, tokens), BF),
            jax.ShapeDtypeStruct((1, tokens), F4),
        ),
        in_specs=[pl.BlockSpec(memory_space=pltpu.SMEM), VM],
        out_specs=(HBM, VM),
        scratch_shapes=[pltpu.VMEM((64, 80, tokens), BF), pltpu.SemaphoreType.DMA],
        compiler_params=params(20),
        cost_estimate=pl.CostEstimate(
            flops=4 * tokens * width, bytes_accessed=4 * tokens * width, transcendentals=0
        ),
        name="turn_hidden",
    )(pos, hidden)


def project_blocks(blocks, maps, wa_refs, wb_refs, ht_ref, rstd_ref, nt_ref, scratch):
    hs, wa, wb, table, sems, nt, nt_sem = scratch
    groups = []
    n = 0
    for i, e in enumerate(blocks):
        group = [pltpu.make_async_copy(ht_ref.at[pl.ds(e * 8, 8)], hs.at[i], sems.at[n])]
        n += 1
        for refs, dst, part in ((wb_refs, wb, 1), (wa_refs, wa, 0)):
            for src, take, dc in maps[part][i]:
                src = refs[src] if take is None else refs[src].at[take]
                to = dst.at[i] if dc is None else dst.at[i, dc]
                group.append(pltpu.make_async_copy(src, to, sems.at[n]))
                n += 1
        groups.append(group)
    for cp in [cp for group in groups for cp in group]:
        cp.start()
    rstd = rstd_ref[...]
    acc_a = acc_b = None
    outs = []
    for i in range(len(blocks)):
        for cp in groups[i]:
            cp.wait()
        for j in range(8):
            table[j : j + 1, :] = wb[i, j // 4, j % 4, 80:81, 0:128].astype(F4)
        rows = table[...]
        gains = rows.T
        for j in range(8):
            xhat = hs[i, j].astype(F4) * rstd
            nt[i * 8 + j] = (xhat * gains[:80, j : j + 1]).astype(BF)
        part = pl.ds(i * 8, 8)
        out = pltpu.make_async_copy(nt.at[part], nt_ref.at[part], nt_sem.at[i])
        out.start()
        outs.append(out)
        xb = nt[i * 8 : (i + 1) * 8].reshape(640, rstd.shape[1]).T
        pa = dot(xb, wa[i].reshape(640, A_COLS), (1, 0))
        pb = dot(xb, wb[i, :, :, :80].reshape(640, B_COLS), (1, 0))
        lane = lax.broadcasted_iota(jnp.int32, (8, 128), 1)
        real = jnp.sum(jnp.where((lane >= 80) & (lane < 84), rows, 0.0), axis=0, keepdims=True)
        if i == 0:
            acc_a, acc_b, acc_real = pa, pb, real
        else:
            acc_a, acc_b, acc_real = acc_a + pa, acc_b + pb, acc_real + real
    for out in outs:
        out.wait()
    return acc_a, acc_b, acc_real


def project_scratch(n, copies):
    return [
        pltpu.VMEM((n, 8, 80, 512), BF),
        pltpu.VMEM((n, 2, 4, 80, A_COLS), BF),
        pltpu.VMEM((n, 2, 4, W_ROWS, B_COLS), BF),
        pltpu.VMEM((8, 128), F4),
        pltpu.SemaphoreType.DMA((copies,)),
        pltpu.VMEM((8 * n, 80, 512), BF),
        pltpu.SemaphoreType.DMA((n,)),
    ]


def project_kernel(blocks, maps, count, first, *refs):
    wa_refs, wb_refs = refs[:count], refs[count : 2 * count]
    refs = refs[2 * count :]
    ht_ref, rstd_ref = refs[:2]
    refs = refs[2:]
    if not first:
        old, old_real = refs[:2]
        refs = refs[2:]
    nt_ref, acc, acc_real = refs[:3]
    pa, pb, real = project_blocks(
        blocks, maps, wa_refs, wb_refs, ht_ref, rstd_ref, nt_ref, refs[3:]
    )
    if not first:
        pa = pa + old[:, :A_COLS]
        pb = pb + old[:, A_COLS:]
        real = real + old_real[...]
    acc[:, :A_COLS] = pa
    acc[:, A_COLS:] = pb
    acc_real[...] = real


def project(blocks, maps, wa, wb, ht, rstd, state):
    tokens = ht.shape[2]
    n = len(blocks)
    first = state is None
    copies = n + sum(len(m) for part in maps for m in part)
    return pl.pallas_call(
        functools.partial(project_kernel, blocks, maps, len(wa), first),
        out_shape=(
            jax.ShapeDtypeStruct((8 * n, 80, tokens), BF),
            jax.ShapeDtypeStruct((tokens, 896), F4),
            jax.ShapeDtypeStruct((1, 128), F4),
        ),
        in_specs=[HBM] * (2 * len(wa) + 1) + [VM] * (1 if first else 3),
        out_specs=(HBM, VM, VM),
        scratch_shapes=project_scratch(n, copies),
        compiler_params=params(20),
        cost_estimate=pl.CostEstimate(
            flops=2 * n * tokens * 640 * 896, bytes_accessed=n * 2**21, transcendentals=0
        ),
        name="project",
    )(*wa, *wb, ht, rstd, *(() if first else state))


def attention_kernel(blocks, maps, count, *refs):
    wa_refs, wb_refs = refs[:count], refs[count : 2 * count]
    refs = refs[2 * count :]
    ht_ref, rstd_ref, old, old_real, bias, up, cosf, sinf, mask, real = refs[:10]
    nt_ref, out_ref, d_ref, sum_ref, qkv = refs[10:15]
    pa, pb, new_real = project_blocks(
        blocks, maps, wa_refs, wb_refs, ht_ref, rstd_ref, nt_ref, refs[15:]
    )
    qkv[:, :A_COLS] = old[:, :A_COLS] + pa + bias[:, :A_COLS]
    qkv[:, A_COLS:] = old[:, A_COLS:] + pb + bias[:, A_COLS:]
    total = jnp.sum(old_real[...] + new_real, axis=1, keepdims=True)
    scale = 1.0 / D**0.5
    weight = real[...] * 256.0 / total
    for r in range(4):
        rows = slice(r * ROW, (r + 1) * ROW)
        co, si = cosf[rows], sinf[rows]

        def turn(v, s):
            return v * co + pltpu.roll(v, 64, 1) * s

        k = turn(qkv[rows, 640:768], si).astype(BF)
        v = qkv[rows, 768:896].astype(BF)
        q = jnp.concatenate(
            [turn(qkv[rows, h * D : (h + 1) * D], si).astype(BF) for h in range(5)], axis=0
        )
        ga = jnp.concatenate(
            [(up[rows, h * D : (h + 1) * D].astype(F4) * weight[rows]).astype(BF) for h in range(5)],
            axis=0,
        )
        allowed = jnp.concatenate([mask[r]] * 5, axis=0) > 0.0
        scores = jnp.where(allowed, dot(q, k, (1, 1)) * scale, -1e30)
        expo = jnp.exp(scores - jnp.max(scores, axis=1, keepdims=True))
        probs = expo / jnp.sum(expo, axis=1, keepdims=True)
        probs_b = probs.astype(BF)
        att = dot(probs_b, v, (1, 0)).astype(BF)
        dp = dot(ga, v, (1, 1))
        dv = dot(probs_b, ga, (0, 0))
        ds = probs * (dp - jnp.sum(probs * dp, axis=1, keepdims=True)) * scale
        dsb = ds.astype(BF)
        dq = dot(dsb, k, (1, 0))
        dk = dot(dsb, q, (0, 0))
        for h in range(5):
            hs = slice(h * ROW, (h + 1) * ROW)
            out_ref[rows, h * D : (h + 1) * D] = att[hs]
            d_ref[rows, h * D : (h + 1) * D] = turn(dq[hs], -si).astype(BF)
        d_ref[rows, 640:768] = turn(dk, -si).astype(BF)
        d_ref[rows, 768:896] = dv.astype(BF)
    for i in range(7):
        sum_ref[i : i + 1, :] = jnp.sum(
            d_ref[:, i * D : (i + 1) * D].astype(F4), axis=0, keepdims=True
        )
    sum_ref[7:8, :] = jnp.zeros((1, D), F4)


def attention(blocks, maps, wa, wb, ht, rstd, state, bias, up, tables):
    tokens = ht.shape[2]
    copies = len(blocks) + sum(len(m) for part in maps for m in part)
    return pl.pallas_call(
        functools.partial(attention_kernel, blocks, maps, len(wa)),
        out_shape=(
            jax.ShapeDtypeStruct((8, 80, tokens), BF),
            jax.ShapeDtypeStruct((tokens, 640), BF),
            jax.ShapeDtypeStruct((tokens, 896), BF),
            jax.ShapeDtypeStruct((8, D), F4),
        ),
        in_specs=[HBM] * (2 * len(wa) + 1) + [VM] * 9,
        out_specs=(HBM, VM, VM, VM),
        scratch_shapes=[pltpu.VMEM((tokens, 896), F4)] + project_scratch(1, copies),
        compiler_params=params(24),
        cost_estimate=pl.CostEstimate(
            flops=2 * tokens * 1280 * 896, bytes_accessed=8 * 2**20, transcendentals=400000
        ),
        name="attend",
    )(*wa, *wb, ht, rstd, *state, bias, up, *tables)


def grad_kernel(n, nt_ref, d_ref, *refs):
    outs, (nt, sems) = refs[: 2 * n], refs[2 * n :]
    copies = []
    for i in range(n):
        part = pl.ds(i * 8, 8)
        copies.append(pltpu.make_async_copy(nt_ref.at[part], nt.at[part], sems.at[i]))
    for cp in copies:
        cp.start()
    d = d_ref[...]
    for i in range(n):
        copies[i].wait()
        for dc in range(2):
            at = i * 8 + dc * 4
            g = dot(nt[at : at + 4].reshape(320, 512), d, (1, 0)).astype(BF)
            out_a = outs[2 * i]
            out_b = outs[2 * i + 1]
            to = dc if i == 0 else 1 - dc
            for dx in range(4):
                rows = g[dx * 80 : (dx + 1) * 80]
                out_a[to, dx] = rows[:, :A_COLS]
                out_b[to, dx] = rows[:, A_COLS:]


def weight_grad(nt, d):
    n = nt.shape[0] // 8
    shapes = [(2, 4, 80, A_COLS), (2, 4, 80, B_COLS)] * n
    return pl.pallas_call(
        functools.partial(grad_kernel, n),
        out_shape=[jax.ShapeDtypeStruct(shape, BF) for shape in shapes],
        in_specs=[HBM, VM],
        out_specs=[VM] * (2 * n),
        scratch_shapes=[pltpu.VMEM(nt.shape, BF), pltpu.SemaphoreType.DMA((n,))],
        compiler_params=params(12),
        cost_estimate=pl.CostEstimate(
            flops=2 * n * 512 * 640 * 896, bytes_accessed=n * 2**21, transcendentals=0
        ),
        name="weight_grad",
    )(nt, d)


def gather_project(w, pos, hidden, lengths, bias, tokens):
    xs = [w] + [send(w, X_BY[4 - dx]) for dx in (1, 2, 3)]
    own_a = jnp.stack([a[:80, :A_COLS] for a in xs])
    own_b = jnp.stack([a[:, A_COLS:] for a in xs])
    oth_a, oth_b = send(own_a, CORE), send(own_b, CORE)
    ra, rb = [jnp.stack([own_a, oth_a])], [jnp.stack([own_b, oth_b])]
    ring, swapped = [(0, None, None)], [(1, 0, 1), (1, 1, 0)]
    pair = ([ring, swapped],) * 2
    single = ([[(0, None, 0), (1, None, 1)]],) * 2
    ra.append(send(ra[0], RING))
    rb.append(send(rb[0], RING))
    hidden, lengths, bias, _ = tie(hidden, lengths, bias, ra[0])
    ht, rstd = turn_hidden(pos, hidden)
    tabs = (bias,) + tables(lengths, tokens)
    nts = []
    state = None
    for k in (1, 2, 3):
        if k == 1:
            ra[1], ht, rstd, *tabs = tie(ra[1], ht, rstd, *tabs)
        else:
            ra[k], *state = tie(ra[k], *state)
        last = (lambda r: r[0]) if k == 3 else (lambda r: r)
        ra.append(send(last(ra[k]), RING))
        swap_a = send(ra[k], CORE)
        rb.append(send(last(rb[k]), RING))
        if k == 3:
            ra[4], rb[3] = tie(ra[4], rb[3])
        swap_b = send(rb[k], CORE)
        if k == 1:
            nt, *state = project([0], single, (own_a, oth_a), (own_b, oth_b), ht, rstd, None)
            nts.append(nt)
        nt, *state = project(
            [k, 8 - k], pair, (ra[k], swap_a), (rb[k], swap_b), ht, rstd, state
        )
        nts.append(nt)
    wa = (ra[4], send(ra[4], CORE))
    rb[4], *state = tie(rb[4], *state)
    wb = (rb[4], send(rb[4], CORE))
    return ([4], single, wa, wb, ht, rstd, state), tabs, nts


def scatter(nts, d, sums):
    flips = iter([FLIPS[3], FLIPS[4], FLIPS[5], FLIPS[0], FLIPS[1], FLIPS[2]])
    flip = send(sums, next(flips))

    def exchange(arrived):
        nonlocal sums, flip
        arrived, got, sums = tie(arrived, flip, sums)
        sums = sums + got
        flip = send(sums, next(flips))
        return arrived

    near4 = weight_grad(nts[4], d)
    t = [None, None]
    for p in (1, 0):
        s = add(near4[p][0], send(near4[p][1], CORE))
        if p == 0:
            s = exchange(s)
        t[p] = send(s, BACK)
    for k in (3, 2, 1):
        g = weight_grad(nts[k], d)
        near, far = g[:2], g[2:]
        for p in (1, 0):
            got = send(far[p], CORE)
            back = t[p]
            if p == 0:
                back = exchange(back)
            if k == 3:
                s = jnp.stack([add(near[p][0], got[0], back), add(near[p][1], got[1])])
            else:
                s = add(near[p], got, back)
            t[p] = send(s, BACK)
    near0 = weight_grad(nts[0], d)
    parts = []
    for p in (1, 0):
        back = t[p] if p == 1 else exchange(t[p])
        got = send(add(near0[p][1], back[1]), CORE)
        parts.insert(0, add(near0[p][0], back[0], got))
    y = [jnp.concatenate([parts[0][k], parts[1][k]], axis=1) for k in range(4)]
    total = y[0].astype(F4)
    for k in (2, 1, 3):
        total = total + send(y[k], X_BY[k]).astype(F4)
    return total, sums + flip


def doc_layout(lengths):
    ends = jnp.cumsum(lengths, axis=1)
    place = jnp.arange(ROW, dtype=jnp.int32)[None, :, None]
    passed = place >= ends[:, None, :]
    segment = jnp.sum(passed.astype(jnp.int32), axis=2)
    start = jnp.max(jnp.where(passed, ends[:, None, :], 0), axis=2)
    position = (place[:, :, 0] - start).astype(F4)
    real = (place[:, :, 0] < ends[:, -1:]).astype(F4)
    return segment, position, real


def tables(lengths, tokens):
    segment, position, real = doc_layout(lengths)
    freq = 1000000.0 ** (-(2.0 * jnp.arange(D // 2, dtype=F4)) / D)
    angle = position.reshape(tokens, 1) * freq
    cos, sin = jnp.cos(angle), jnp.sin(angle)
    cosf = jnp.concatenate([cos, cos], axis=1)
    sinf = jnp.concatenate([-sin, sin], axis=1)
    causal = jnp.arange(ROW)[:, None] >= jnp.arange(ROW)[None, :]
    mask = ((segment[:, :, None] == segment[:, None, :]) & causal[None]).astype(F4)
    return cosf, sinf, mask, jnp.broadcast_to(real.reshape(tokens, 1), (tokens, D))


def per_device(hidden, gain, w_query, w_keyval, b_query, b_keyval, upstream, lengths):
    tokens = hidden.shape[0]
    i = lax.axis_index("dp")
    pos = jnp.stack([i // 16, (i // 2) % 8, i % 2]).astype(jnp.int32)
    w_all = jnp.concatenate([w_query, w_keyval[0], w_keyval[1]], axis=1)
    extra = jnp.concatenate([gain, jnp.sum(lengths, axis=1).astype(BF)])
    extra = jnp.pad(extra[None, :], ((0, 7), (A_COLS, B_COLS - 84)))
    bias = jnp.concatenate([b_query, b_keyval[0], b_keyval[1]]).reshape(1, 896)
    last, (bias, *tabs), nts = gather_project(
        jnp.concatenate([w_all, extra], axis=0), pos, hidden, lengths, bias, tokens
    )
    nt, attended, d, sums = attention(*last, bias, upstream, tabs)
    g, sums = scatter(nts + [nt], d, sums)
    grad_query = g[:, :640]
    grad_keyval = jnp.stack([g[:, 640:768], g[:, 768:]])
    grad_bias_query = sums[:5].reshape(640)
    grad_bias_keyval = sums[5:7]
    part = jnp.sum(g * w_all.astype(F4), axis=1) / gain.astype(F4)
    one, two, three = [
        lax.ppermute(part, "mp", [(y, y ^ k) for y in range(4)]) for k in (1, 2, 3)
    ]
    gain_gradient = (part + one) + (two + three)
    return (attended, grad_query, grad_keyval, grad_bias_query, grad_bias_keyval, gain_gradient)


def solution(mesh):
    return jax.shard_map(
        per_device,
        mesh=mesh,
        in_specs=(
            P("dp", None),
            P("dp"),
            P("dp", "mp"),
            P(None, "dp", "mp"),
            P("mp"),
            P(None, "mp"),
            P("dp", "mp"),
            P("dp", None),
        ),
        out_specs=(
            P("dp", "mp"),
            P("dp", "mp"),
            P(None, "dp", "mp"),
            P("mp"),
            P(None, "mp"),
            P("dp"),
        ),
        check_vma=False,
    )
```

```python
import functools

import jax
import jax.numpy as jnp
from jax import lax
from jax.experimental import pallas as pl
from jax.experimental.pallas import tpu as pltpu
from jax.sharding import PartitionSpec as P

D = 128
ROW = 128
XS, ZS, CS = 4, 8, 2
BF = jnp.bfloat16
F4 = jnp.float32
A_COLS, B_COLS = 512, 384
W_ROWS = 88


def _perm(move):
    pairs = []
    for x in range(XS):
        for z in range(ZS):
            for c in range(CS):
                a, b, e = move(x, z, c)
                pairs.append(((x * ZS + z) * CS + c, ((a % XS) * ZS + b % ZS) * CS + e % CS))
    return pairs


CORE = _perm(lambda x, z, c: (x, z, 1 - c))
X_BY = [_perm(lambda x, z, c, k=k: (x + k, z, c)) for k in range(XS)]
RING = _perm(lambda x, z, c: (x, z + 1 - 2 * c, c))
BACK = _perm(lambda x, z, c: (x, z - 1 + 2 * c, c))
FLIPS = [
    CORE,
    _perm(lambda x, z, c: (x ^ 1, z, c)),
    _perm(lambda x, z, c: (x ^ 2, z, c)),
    _perm(lambda x, z, c: (x, z ^ 1, c)),
    _perm(lambda x, z, c: (x, z ^ 2, c)),
    _perm(lambda x, z, c: (x, z ^ 4, c)),
]


def send(a, perm):
    return lax.ppermute(a, "dp", perm)


def add(*parts):
    total = parts[0].astype(F4)
    for p in parts[1:]:
        total = total + p.astype(F4)
    return total.astype(BF)


def tie(*arrays):
    return lax.optimization_barrier(arrays)


def dot(a, b, dims):
    return lax.dot_general(a, b, ((dims[:1], dims[1:]), ((), ())), preferred_element_type=F4)


VM = pl.BlockSpec(memory_space=pltpu.VMEM)
HBM = pl.BlockSpec(memory_space=pltpu.HBM)


def params(mib):
    return pltpu.CompilerParams(vmem_limit_bytes=mib * 2**20)


def turn_kernel(pos_ref, h_ref, out_ref, rstd_ref, ht_ref, sem):
    tokens, width = h_ref.shape
    x, z, c = pos_ref[0], pos_ref[1], pos_ref[2]
    ss = jnp.zeros((1, tokens), F4)
    for b in range(8):
        ht = h_ref[:, b * 640 : (b + 1) * 640].T
        hf = ht.astype(F4)
        ss = ss + jnp.sum(hf * hf, axis=0, keepdims=True)
        for j in range(8):
            dx = lax.rem(b // 2 - x + XS, XS)
            e = lax.rem((1 - 2 * c) * (z - (b % 2) * 4 - j // 2) + ZS, ZS)
            dc = lax.rem(j % 2 + c, CS)
            ht_ref[e * 8 + dc * 4 + dx] = ht[j * 80 : (j + 1) * 80]
    rstd_ref[...] = lax.rsqrt(ss / width + 1e-06)
    copy = pltpu.make_async_copy(ht_ref, out_ref, sem)
    copy.start()
    copy.wait()


def turn_hidden(pos, hidden):
    tokens, width = hidden.shape
    return pl.pallas_call(
        turn_kernel,
        out_shape=(
            jax.ShapeDtypeStruct((64, 80, tokens), BF),
            jax.ShapeDtypeStruct((1, tokens), F4),
        ),
        in_specs=[pl.BlockSpec(memory_space=pltpu.SMEM), VM],
        out_specs=(HBM, VM),
        scratch_shapes=[pltpu.VMEM((64, 80, tokens), BF), pltpu.SemaphoreType.DMA],
        compiler_params=params(20),
        cost_estimate=pl.CostEstimate(
            flops=4 * tokens * width, bytes_accessed=4 * tokens * width, transcendentals=0
        ),
        name="turn_hidden",
    )(pos, hidden)


def project_blocks(blocks, maps, wa_refs, wb_refs, ht_ref, rstd_ref, nt_ref, scratch):
    hs, wa, wb, table, sems, nt, nt_sem = scratch
    groups = []
    n = 0
    for i, e in enumerate(blocks):
        group = [pltpu.make_async_copy(ht_ref.at[pl.ds(e * 8, 8)], hs.at[i], sems.at[n])]
        n += 1
        for refs, dst, part in ((wb_refs, wb, 1), (wa_refs, wa, 0)):
            for src, take, dc in maps[part][i]:
                src = refs[src] if take is None else refs[src].at[take]
                to = dst.at[i] if dc is None else dst.at[i, dc]
                group.append(pltpu.make_async_copy(src, to, sems.at[n]))
                n += 1
        groups.append(group)
    for cp in [cp for group in groups for cp in group]:
        cp.start()
    rstd = rstd_ref[...]
    acc_a = acc_b = None
    outs = []
    for i in range(len(blocks)):
        for cp in groups[i]:
            cp.wait()
        for j in range(8):
            table[j : j + 1, :] = wb[i, j // 4, j % 4, 80:81, 0:128].astype(F4)
        rows = table[...]
        gains = rows.T
        for j in range(8):
            xhat = hs[i, j].astype(F4) * rstd
            nt[i * 8 + j] = (xhat * gains[:80, j : j + 1]).astype(BF)
        part = pl.ds(i * 8, 8)
        out = pltpu.make_async_copy(nt.at[part], nt_ref.at[part], nt_sem.at[i])
        out.start()
        outs.append(out)
        xb = nt[i * 8 : (i + 1) * 8].reshape(640, rstd.shape[1]).T
        pa = dot(xb, wa[i].reshape(640, A_COLS), (1, 0))
        pb = dot(xb, wb[i, :, :, :80].reshape(640, B_COLS), (1, 0))
        lane = lax.broadcasted_iota(jnp.int32, (8, 128), 1)
        real = jnp.sum(jnp.where((lane >= 80) & (lane < 84), rows, 0.0), axis=0, keepdims=True)
        if i == 0:
            acc_a, acc_b, acc_real = pa, pb, real
        else:
            acc_a, acc_b, acc_real = acc_a + pa, acc_b + pb, acc_real + real
    for out in outs:
        out.wait()
    return acc_a, acc_b, acc_real


def project_scratch(n, copies):
    return [
        pltpu.VMEM((n, 8, 80, 512), BF),
        pltpu.VMEM((n, 2, 4, 80, A_COLS), BF),
        pltpu.VMEM((n, 2, 4, W_ROWS, B_COLS), BF),
        pltpu.VMEM((8, 128), F4),
        pltpu.SemaphoreType.DMA((copies,)),
        pltpu.VMEM((8 * n, 80, 512), BF),
        pltpu.SemaphoreType.DMA((n,)),
    ]


def project_kernel(blocks, maps, count, first, *refs):
    wa_refs, wb_refs = refs[:count], refs[count : 2 * count]
    refs = refs[2 * count :]
    ht_ref, rstd_ref = refs[:2]
    refs = refs[2:]
    if not first:
        old, old_real = refs[:2]
        refs = refs[2:]
    nt_ref, acc, acc_real = refs[:3]
    pa, pb, real = project_blocks(
        blocks, maps, wa_refs, wb_refs, ht_ref, rstd_ref, nt_ref, refs[3:]
    )
    if not first:
        pa = pa + old[:, :A_COLS]
        pb = pb + old[:, A_COLS:]
        real = real + old_real[...]
    acc[:, :A_COLS] = pa
    acc[:, A_COLS:] = pb
    acc_real[...] = real


def project(blocks, maps, wa, wb, ht, rstd, state):
    tokens = ht.shape[2]
    n = len(blocks)
    first = state is None
    copies = n + sum(len(m) for part in maps for m in part)
    return pl.pallas_call(
        functools.partial(project_kernel, blocks, maps, len(wa), first),
        out_shape=(
            jax.ShapeDtypeStruct((8 * n, 80, tokens), BF),
            jax.ShapeDtypeStruct((tokens, 896), F4),
            jax.ShapeDtypeStruct((1, 128), F4),
        ),
        in_specs=[HBM] * (2 * len(wa) + 1) + [VM] * (1 if first else 3),
        out_specs=(HBM, VM, VM),
        scratch_shapes=project_scratch(n, copies),
        compiler_params=params(20),
        cost_estimate=pl.CostEstimate(
            flops=2 * n * tokens * 640 * 896, bytes_accessed=n * 2**21, transcendentals=0
        ),
        name="project",
    )(*wa, *wb, ht, rstd, *(() if first else state))


def attention_kernel(blocks, maps, count, *refs):
    wa_refs, wb_refs = refs[:count], refs[count : 2 * count]
    refs = refs[2 * count :]
    ht_ref, rstd_ref, old, old_real, bias, up, cosf, sinf, mask, real = refs[:10]
    nt_ref, out_ref, d_ref, sum_ref, qkv = refs[10:15]
    pa, pb, new_real = project_blocks(
        blocks, maps, wa_refs, wb_refs, ht_ref, rstd_ref, nt_ref, refs[15:]
    )
    qkv[:, :A_COLS] = old[:, :A_COLS] + pa + bias[:, :A_COLS]
    qkv[:, A_COLS:] = old[:, A_COLS:] + pb + bias[:, A_COLS:]
    total = jnp.sum(old_real[...] + new_real, axis=1, keepdims=True)
    scale = 1.0 / D**0.5
    weight = real[...] * 256.0 / total
    for r in range(4):
        rows = slice(r * ROW, (r + 1) * ROW)
        co, si = cosf[rows], sinf[rows]

        def turn(v, s):
            return v * co + pltpu.roll(v, 64, 1) * s

        k = turn(qkv[rows, 640:768], si).astype(BF)
        v = qkv[rows, 768:896].astype(BF)
        q = jnp.concatenate(
            [turn(qkv[rows, h * D : (h + 1) * D], si).astype(BF) for h in range(5)], axis=0
        )
        ga = jnp.concatenate(
            [(up[rows, h * D : (h + 1) * D].astype(F4) * weight[rows]).astype(BF) for h in range(5)],
            axis=0,
        )
        allowed = jnp.concatenate([mask[r]] * 5, axis=0) > 0.0
        scores = jnp.where(allowed, dot(q, k, (1, 1)) * scale, -1e30)
        expo = jnp.exp(scores - jnp.max(scores, axis=1, keepdims=True))
        probs = expo / jnp.sum(expo, axis=1, keepdims=True)
        probs_b = probs.astype(BF)
        att = dot(probs_b, v, (1, 0)).astype(BF)
        dp = dot(ga, v, (1, 1))
        dv = dot(probs_b, ga, (0, 0))
        ds = probs * (dp - jnp.sum(probs * dp, axis=1, keepdims=True)) * scale
        dsb = ds.astype(BF)
        dq = dot(dsb, k, (1, 0))
        dk = dot(dsb, q, (0, 0))
        for h in range(5):
            hs = slice(h * ROW, (h + 1) * ROW)
            out_ref[rows, h * D : (h + 1) * D] = att[hs]
            d_ref[rows, h * D : (h + 1) * D] = turn(dq[hs], -si).astype(BF)
        d_ref[rows, 640:768] = turn(dk, -si).astype(BF)
        d_ref[rows, 768:896] = dv.astype(BF)
    for i in range(7):
        sum_ref[i : i + 1, :] = jnp.sum(
            d_ref[:, i * D : (i + 1) * D].astype(F4), axis=0, keepdims=True
        )
    sum_ref[7:8, :] = jnp.zeros((1, D), F4)


def attention(blocks, maps, wa, wb, ht, rstd, state, bias, up, tables):
    tokens = ht.shape[2]
    copies = len(blocks) + sum(len(m) for part in maps for m in part)
    return pl.pallas_call(
        functools.partial(attention_kernel, blocks, maps, len(wa)),
        out_shape=(
            jax.ShapeDtypeStruct((8, 80, tokens), BF),
            jax.ShapeDtypeStruct((tokens, 640), BF),
            jax.ShapeDtypeStruct((tokens, 896), BF),
            jax.ShapeDtypeStruct((8, D), F4),
        ),
        in_specs=[HBM] * (2 * len(wa) + 1) + [VM] * 9,
        out_specs=(HBM, VM, VM, VM),
        scratch_shapes=[pltpu.VMEM((tokens, 896), F4)] + project_scratch(1, copies),
        compiler_params=params(24),
        cost_estimate=pl.CostEstimate(
            flops=2 * tokens * 1280 * 896, bytes_accessed=8 * 2**20, transcendentals=400000
        ),
        name="attend",
    )(*wa, *wb, ht, rstd, *state, bias, up, *tables)


def grad_kernel(n, nt_ref, d_ref, *refs):
    outs, (nt, sems) = refs[: 2 * n], refs[2 * n :]
    copies = []
    for i in range(n):
        part = pl.ds(i * 8, 8)
        copies.append(pltpu.make_async_copy(nt_ref.at[part], nt.at[part], sems.at[i]))
    for cp in copies:
        cp.start()
    d = d_ref[...]
    for i in range(n):
        copies[i].wait()
        for dc in range(2):
            at = i * 8 + dc * 4
            g = dot(nt[at : at + 4].reshape(320, 512), d, (1, 0)).astype(BF)
            out_a = outs[2 * i]
            out_b = outs[2 * i + 1]
            to = dc if i == 0 else 1 - dc
            for dx in range(4):
                rows = g[dx * 80 : (dx + 1) * 80]
                out_a[to, dx] = rows[:, :A_COLS]
                out_b[to, dx] = rows[:, A_COLS:]


def weight_grad(nt, d):
    n = nt.shape[0] // 8
    shapes = [(2, 4, 80, A_COLS), (2, 4, 80, B_COLS)] * n
    return pl.pallas_call(
        functools.partial(grad_kernel, n),
        out_shape=[jax.ShapeDtypeStruct(shape, BF) for shape in shapes],
        in_specs=[HBM, VM],
        out_specs=[VM] * (2 * n),
        scratch_shapes=[pltpu.VMEM(nt.shape, BF), pltpu.SemaphoreType.DMA((n,))],
        compiler_params=params(12),
        cost_estimate=pl.CostEstimate(
            flops=2 * n * 512 * 640 * 896, bytes_accessed=n * 2**21, transcendentals=0
        ),
        name="weight_grad",
    )(nt, d)


def gather_project(w, pos, hidden, lengths, bias, tokens):
    xs = [w] + [send(w, X_BY[4 - dx]) for dx in (1, 2, 3)]
    own_a = jnp.stack([a[:80, :A_COLS] for a in xs])
    own_b = jnp.stack([a[:, A_COLS:] for a in xs])
    oth_a, oth_b = send(own_a, CORE), send(own_b, CORE)
    ra, rb = [jnp.stack([own_a, oth_a])], [jnp.stack([own_b, oth_b])]
    ring, swapped = [(0, None, None)], [(1, 0, 1), (1, 1, 0)]
    pair = ([ring, swapped],) * 2
    single = ([[(0, None, 0), (1, None, 1)]],) * 2
    ra.append(send(ra[0], RING))
    rb.append(send(rb[0], RING))
    hidden, lengths, bias, _ = tie(hidden, lengths, bias, ra[0])
    ht, rstd = turn_hidden(pos, hidden)
    tabs = (bias,) + tables(lengths, tokens)
    nts = []
    state = None
    for k in (1, 2, 3):
        if k == 1:
            ra[1], ht, rstd, *tabs = tie(ra[1], ht, rstd, *tabs)
        else:
            ra[k], *state = tie(ra[k], *state)
        last = (lambda r: r[0]) if k == 3 else (lambda r: r)
        ra.append(send(last(ra[k]), RING))
        swap_a = send(ra[k], CORE)
        rb.append(send(last(rb[k]), RING))
        if k == 3:
            ra[4], rb[3] = tie(ra[4], rb[3])
        swap_b = send(rb[k], CORE)
        if k == 1:
            nt, *state = project([0], single, (own_a, oth_a), (own_b, oth_b), ht, rstd, None)
            nts.append(nt)
        nt, *state = project(
            [k, 8 - k], pair, (ra[k], swap_a), (rb[k], swap_b), ht, rstd, state
        )
        nts.append(nt)
    wa = (ra[4], send(ra[4], CORE))
    rb[4], *state = tie(rb[4], *state)
    wb = (rb[4], send(rb[4], CORE))
    return ([4], single, wa, wb, ht, rstd, state), tabs, nts


def scatter(nts, d, sums):
    flips = iter([FLIPS[3], FLIPS[4], FLIPS[5], FLIPS[0], FLIPS[1], FLIPS[2], None])
    flip = send(sums, next(flips))

    def exchange(arrived):
        nonlocal sums, flip
        arrived, got, sums = tie(arrived, flip, sums)
        sums = sums + got
        perm = next(flips)
        flip = None if perm is None else send(sums, perm)
        return arrived

    near4 = weight_grad(nts[4], d)
    early = weight_grad(nts[3], d)
    t = [None, None]
    for p in (1, 0):
        s = add(near4[p][0], send(near4[p][1], CORE))
        if p == 0:
            s, d = tie(exchange(s), d)
        t[p] = send(s, BACK)
    slots = {(3, 0), (2, 0), (1, 1), (1, 0), (0, 1)}
    for k in (3, 2, 1):
        g = early if k == 3 else weight_grad(nts[k], d)
        near, far = g[:2], g[2:]
        for p in (1, 0):
            got = send(far[p], CORE)
            back = exchange(t[p]) if (k, p) in slots else t[p]
            if k == 3:
                s = jnp.stack([add(near[p][0], got[0], back), add(near[p][1], got[1])])
            else:
                s = add(near[p], got, back)
            t[p] = send(s, BACK)
    near0 = weight_grad(nts[0], d)
    parts = []
    for p in (1, 0):
        back = exchange(t[p]) if (0, p) in slots else t[p]
        got = send(add(near0[p][1], back[1]), CORE)
        parts.insert(0, add(near0[p][0], back[0], got))
    y = [jnp.concatenate([parts[0][k], parts[1][k]], axis=1) for k in range(4)]
    total = y[0].astype(F4)
    for k in (2, 1, 3):
        total = total + send(y[k], X_BY[k]).astype(F4)
    return total, sums


def doc_layout(lengths):
    ends = jnp.cumsum(lengths, axis=1)
    place = jnp.arange(ROW, dtype=jnp.int32)[None, :, None]
    passed = place >= ends[:, None, :]
    segment = jnp.sum(passed.astype(jnp.int32), axis=2)
    start = jnp.max(jnp.where(passed, ends[:, None, :], 0), axis=2)
    position = (place[:, :, 0] - start).astype(F4)
    real = (place[:, :, 0] < ends[:, -1:]).astype(F4)
    return segment, position, real


def tables(lengths, tokens):
    segment, position, real = doc_layout(lengths)
    freq = 1000000.0 ** (-(2.0 * jnp.arange(D // 2, dtype=F4)) / D)
    angle = position.reshape(tokens, 1) * freq
    cos, sin = jnp.cos(angle), jnp.sin(angle)
    cosf = jnp.concatenate([cos, cos], axis=1)
    sinf = jnp.concatenate([-sin, sin], axis=1)
    causal = jnp.arange(ROW)[:, None] >= jnp.arange(ROW)[None, :]
    mask = ((segment[:, :, None] == segment[:, None, :]) & causal[None]).astype(F4)
    return cosf, sinf, mask, jnp.broadcast_to(real.reshape(tokens, 1), (tokens, D))


def per_device(hidden, gain, w_query, w_keyval, b_query, b_keyval, upstream, lengths):
    tokens = hidden.shape[0]
    i = lax.axis_index("dp")
    pos = jnp.stack([i // 16, (i // 2) % 8, i % 2]).astype(jnp.int32)
    w_all = jnp.concatenate([w_query, w_keyval[0], w_keyval[1]], axis=1)
    extra = jnp.concatenate([gain, jnp.sum(lengths, axis=1).astype(BF)])
    extra = jnp.pad(extra[None, :], ((0, 7), (A_COLS, B_COLS - 84)))
    bias = jnp.concatenate([b_query, b_keyval[0], b_keyval[1]]).reshape(1, 896)
    last, (bias, *tabs), nts = gather_project(
        jnp.concatenate([w_all, extra], axis=0), pos, hidden, lengths, bias, tokens
    )
    nt, attended, d, sums = attention(*last, bias, upstream, tabs)
    g, sums = scatter(nts + [nt], d, sums)
    grad_query = g[:, :640]
    grad_keyval = jnp.stack([g[:, 640:768], g[:, 768:]])
    grad_bias_query = sums[:5].reshape(640)
    grad_bias_keyval = sums[5:7]
    part = jnp.sum(g * w_all.astype(F4), axis=1) / gain.astype(F4)
    one, two, three = [
        lax.ppermute(part, "mp", [(y, y ^ k) for y in range(4)]) for k in (1, 2, 3)
    ]
    gain_gradient = (part + one) + (two + three)
    return (attended, grad_query, grad_keyval, grad_bias_query, grad_bias_keyval, gain_gradient)


def solution(mesh):
    return jax.shard_map(
        per_device,
        mesh=mesh,
        in_specs=(
            P("dp", None),
            P("dp"),
            P("dp", "mp"),
            P(None, "dp", "mp"),
            P("mp"),
            P(None, "mp"),
            P("dp", "mp"),
            P("dp", None),
        ),
        out_specs=(
            P("dp", "mp"),
            P("dp", "mp"),
            P(None, "dp", "mp"),
            P("mp"),
            P(None, "mp"),
            P("dp"),
        ),
        check_vma=False,
    )
```

```python
import functools

import jax
import jax.numpy as jnp
from jax import lax
from jax.experimental import pallas as pl
from jax.experimental.pallas import tpu as pltpu
from jax.sharding import PartitionSpec as P

D = 128
ROW = 128
XS, ZS, CS = 4, 8, 2
BF = jnp.bfloat16
F4 = jnp.float32
A_COLS, B_COLS = 512, 384
W_ROWS = 88


def _perm(move):
    pairs = []
    for x in range(XS):
        for z in range(ZS):
            for c in range(CS):
                a, b, e = move(x, z, c)
                pairs.append(((x * ZS + z) * CS + c, ((a % XS) * ZS + b % ZS) * CS + e % CS))
    return pairs


CORE = _perm(lambda x, z, c: (x, z, 1 - c))
X_BY = [_perm(lambda x, z, c, k=k: (x + k, z, c)) for k in range(XS)]
RING = _perm(lambda x, z, c: (x, z + 1 - 2 * c, c))
BACK = _perm(lambda x, z, c: (x, z - 1 + 2 * c, c))
FLIPS = [
    CORE,
    _perm(lambda x, z, c: (x ^ 1, z, c)),
    _perm(lambda x, z, c: (x ^ 2, z, c)),
    _perm(lambda x, z, c: (x, z ^ 1, c)),
    _perm(lambda x, z, c: (x, z ^ 2, c)),
    _perm(lambda x, z, c: (x, z ^ 4, c)),
]


def send(a, perm):
    return lax.ppermute(a, "dp", perm)


def add(*parts):
    total = parts[0].astype(F4)
    for p in parts[1:]:
        total = total + p.astype(F4)
    return total.astype(BF)


def tie(*arrays):
    return lax.optimization_barrier(arrays)


def dot(a, b, dims):
    return lax.dot_general(a, b, ((dims[:1], dims[1:]), ((), ())), preferred_element_type=F4)


VM = pl.BlockSpec(memory_space=pltpu.VMEM)
HBM = pl.BlockSpec(memory_space=pltpu.HBM)


def params(mib):
    return pltpu.CompilerParams(vmem_limit_bytes=mib * 2**20)


def turn_kernel(pos_ref, h_ref, out_ref, rstd_ref, ht_ref, sem):
    tokens, width = h_ref.shape
    x, z, c = pos_ref[0], pos_ref[1], pos_ref[2]
    ss = jnp.zeros((1, tokens), F4)
    for b in range(8):
        ht = h_ref[:, b * 640 : (b + 1) * 640].T
        hf = ht.astype(F4)
        ss = ss + jnp.sum(hf * hf, axis=0, keepdims=True)
        for j in range(8):
            dx = lax.rem(b // 2 - x + XS, XS)
            e = lax.rem((1 - 2 * c) * (z - (b % 2) * 4 - j // 2) + ZS, ZS)
            dc = lax.rem(j % 2 + c, CS)
            ht_ref[e * 8 + dc * 4 + dx] = ht[j * 80 : (j + 1) * 80]
    rstd_ref[...] = lax.rsqrt(ss / width + 1e-06)
    copy = pltpu.make_async_copy(ht_ref, out_ref, sem)
    copy.start()
    copy.wait()


def turn_hidden(pos, hidden):
    tokens, width = hidden.shape
    return pl.pallas_call(
        turn_kernel,
        out_shape=(
            jax.ShapeDtypeStruct((64, 80, tokens), BF),
            jax.ShapeDtypeStruct((1, tokens), F4),
        ),
        in_specs=[pl.BlockSpec(memory_space=pltpu.SMEM), VM],
        out_specs=(HBM, VM),
        scratch_shapes=[pltpu.VMEM((64, 80, tokens), BF), pltpu.SemaphoreType.DMA],
        compiler_params=params(20),
        cost_estimate=pl.CostEstimate(
            flops=4 * tokens * width, bytes_accessed=4 * tokens * width, transcendentals=0
        ),
        name="turn_hidden",
    )(pos, hidden)


def project_blocks(blocks, maps, wa_refs, wb_refs, ht_ref, rstd_ref, nt_ref, scratch):
    hs, wa, wb, table, sems, nt, nt_sem = scratch
    groups = []
    n = 0
    for i, e in enumerate(blocks):
        group = [pltpu.make_async_copy(ht_ref.at[pl.ds(e * 8, 8)], hs.at[i], sems.at[n])]
        n += 1
        for refs, dst, part in ((wb_refs, wb, 1), (wa_refs, wa, 0)):
            for src, take, dc in maps[part][i]:
                src = refs[src] if take is None else refs[src].at[take]
                to = dst.at[i] if dc is None else dst.at[i, dc]
                group.append(pltpu.make_async_copy(src, to, sems.at[n]))
                n += 1
        groups.append(group)
    for cp in [cp for group in groups for cp in group]:
        cp.start()
    rstd = rstd_ref[...]
    acc_a = acc_b = None
    outs = []
    for i in range(len(blocks)):
        for cp in groups[i]:
            cp.wait()
        for j in range(8):
            table[j : j + 1, :] = wb[i, j // 4, j % 4, 80:81, 0:128].astype(F4)
        rows = table[...]
        gains = rows.T
        for j in range(8):
            xhat = hs[i, j].astype(F4) * rstd
            nt[i * 8 + j] = (xhat * gains[:80, j : j + 1]).astype(BF)
        part = pl.ds(i * 8, 8)
        out = pltpu.make_async_copy(nt.at[part], nt_ref.at[part], nt_sem.at[i])
        out.start()
        outs.append(out)
        xb = nt[i * 8 : (i + 1) * 8].reshape(640, rstd.shape[1]).T
        pa = dot(xb, wa[i].reshape(640, A_COLS), (1, 0))
        pb = dot(xb, wb[i, :, :, :80].reshape(640, B_COLS), (1, 0))
        lane = lax.broadcasted_iota(jnp.int32, (8, 128), 1)
        real = jnp.sum(jnp.where((lane >= 80) & (lane < 84), rows, 0.0), axis=0, keepdims=True)
        if i == 0:
            acc_a, acc_b, acc_real = pa, pb, real
        else:
            acc_a, acc_b, acc_real = acc_a + pa, acc_b + pb, acc_real + real
    for out in outs:
        out.wait()
    return acc_a, acc_b, acc_real


def project_scratch(n, copies):
    return [
        pltpu.VMEM((n, 8, 80, 512), BF),
        pltpu.VMEM((n, 2, 4, 80, A_COLS), BF),
        pltpu.VMEM((n, 2, 4, W_ROWS, B_COLS), BF),
        pltpu.VMEM((8, 128), F4),
        pltpu.SemaphoreType.DMA((copies,)),
        pltpu.VMEM((8 * n, 80, 512), BF),
        pltpu.SemaphoreType.DMA((n,)),
    ]


def project_kernel(blocks, maps, count, first, *refs):
    wa_refs, wb_refs = refs[:count], refs[count : 2 * count]
    refs = refs[2 * count :]
    ht_ref, rstd_ref = refs[:2]
    refs = refs[2:]
    if not first:
        old, old_real = refs[:2]
        refs = refs[2:]
    nt_ref, acc, acc_real = refs[:3]
    pa, pb, real = project_blocks(
        blocks, maps, wa_refs, wb_refs, ht_ref, rstd_ref, nt_ref, refs[3:]
    )
    if not first:
        pa = pa + old[:, :A_COLS]
        pb = pb + old[:, A_COLS:]
        real = real + old_real[...]
    acc[:, :A_COLS] = pa
    acc[:, A_COLS:] = pb
    acc_real[...] = real


def project(blocks, maps, wa, wb, ht, rstd, state):
    tokens = ht.shape[2]
    n = len(blocks)
    first = state is None
    copies = n + sum(len(m) for part in maps for m in part)
    return pl.pallas_call(
        functools.partial(project_kernel, blocks, maps, len(wa), first),
        out_shape=(
            jax.ShapeDtypeStruct((8 * n, 80, tokens), BF),
            jax.ShapeDtypeStruct((tokens, 896), F4),
            jax.ShapeDtypeStruct((1, 128), F4),
        ),
        in_specs=[HBM] * (2 * len(wa) + 1) + [VM] * (1 if first else 3),
        out_specs=(HBM, VM, VM),
        scratch_shapes=project_scratch(n, copies),
        compiler_params=params(20),
        cost_estimate=pl.CostEstimate(
            flops=2 * n * tokens * 640 * 896, bytes_accessed=n * 2**21, transcendentals=0
        ),
        name="project",
    )(*wa, *wb, ht, rstd, *(() if first else state))


def attention_kernel(blocks, maps, count, *refs):
    wa_refs, wb_refs = refs[:count], refs[count : 2 * count]
    refs = refs[2 * count :]
    ht_ref, rstd_ref, old, old_real, bias, up, cosf, sinf, mask, real = refs[:10]
    nt_ref, out_ref, d_ref, sum_ref, qkv = refs[10:15]
    pa, pb, new_real = project_blocks(
        blocks, maps, wa_refs, wb_refs, ht_ref, rstd_ref, nt_ref, refs[15:]
    )
    qkv[:, :A_COLS] = old[:, :A_COLS] + pa + bias[:, :A_COLS]
    qkv[:, A_COLS:] = old[:, A_COLS:] + pb + bias[:, A_COLS:]
    total = jnp.sum(old_real[...] + new_real, axis=1, keepdims=True)
    scale = 1.0 / D**0.5
    weight = real[...] * 256.0 / total
    for r in range(4):
        rows = slice(r * ROW, (r + 1) * ROW)
        co, si = cosf[rows], sinf[rows]

        def turn(v, s):
            return v * co + pltpu.roll(v, 64, 1) * s

        k = turn(qkv[rows, 640:768], si).astype(BF)
        v = qkv[rows, 768:896].astype(BF)
        q = jnp.concatenate(
            [turn(qkv[rows, h * D : (h + 1) * D], si).astype(BF) for h in range(5)], axis=0
        )
        ga = jnp.concatenate(
            [(up[rows, h * D : (h + 1) * D].astype(F4) * weight[rows]).astype(BF) for h in range(5)],
            axis=0,
        )
        allowed = jnp.concatenate([mask[r]] * 5, axis=0) > 0.0
        scores = jnp.where(allowed, dot(q, k, (1, 1)) * scale, -1e30)
        expo = jnp.exp(scores - jnp.max(scores, axis=1, keepdims=True))
        probs = expo / jnp.sum(expo, axis=1, keepdims=True)
        probs_b = probs.astype(BF)
        att = dot(probs_b, v, (1, 0)).astype(BF)
        dp = dot(ga, v, (1, 1))
        dv = dot(probs_b, ga, (0, 0))
        ds = probs * (dp - jnp.sum(probs * dp, axis=1, keepdims=True)) * scale
        dsb = ds.astype(BF)
        dq = dot(dsb, k, (1, 0))
        dk = dot(dsb, q, (0, 0))
        for h in range(5):
            hs = slice(h * ROW, (h + 1) * ROW)
            out_ref[rows, h * D : (h + 1) * D] = att[hs]
            d_ref[rows, h * D : (h + 1) * D] = turn(dq[hs], -si).astype(BF)
        d_ref[rows, 640:768] = turn(dk, -si).astype(BF)
        d_ref[rows, 768:896] = dv.astype(BF)
    for i in range(7):
        sum_ref[i : i + 1, :] = jnp.sum(
            d_ref[:, i * D : (i + 1) * D].astype(F4), axis=0, keepdims=True
        )
    sum_ref[7:8, :] = jnp.zeros((1, D), F4)


def attention(blocks, maps, wa, wb, ht, rstd, state, bias, up, tables):
    tokens = ht.shape[2]
    copies = len(blocks) + sum(len(m) for part in maps for m in part)
    return pl.pallas_call(
        functools.partial(attention_kernel, blocks, maps, len(wa)),
        out_shape=(
            jax.ShapeDtypeStruct((8, 80, tokens), BF),
            jax.ShapeDtypeStruct((tokens, 640), BF),
            jax.ShapeDtypeStruct((tokens, 896), BF),
            jax.ShapeDtypeStruct((8, D), F4),
        ),
        in_specs=[HBM] * (2 * len(wa) + 1) + [VM] * 9,
        out_specs=(HBM, VM, VM, VM),
        scratch_shapes=[pltpu.VMEM((tokens, 896), F4)] + project_scratch(1, copies),
        compiler_params=params(24),
        cost_estimate=pl.CostEstimate(
            flops=2 * tokens * 1280 * 896, bytes_accessed=8 * 2**20, transcendentals=400000
        ),
        name="attend",
    )(*wa, *wb, ht, rstd, *state, bias, up, *tables)


def grad_kernel(n, nt_ref, d_ref, *refs):
    outs, (nt, sems) = refs[: 2 * n], refs[2 * n :]
    copies = []
    for i in range(n):
        part = pl.ds(i * 8, 8)
        copies.append(pltpu.make_async_copy(nt_ref.at[part], nt.at[part], sems.at[i]))
    for cp in copies:
        cp.start()
    d = d_ref[...]
    for i in range(n):
        copies[i].wait()
        for dc in range(2):
            at = i * 8 + dc * 4
            g = dot(nt[at : at + 4].reshape(320, 512), d, (1, 0)).astype(BF)
            out_a = outs[2 * i]
            out_b = outs[2 * i + 1]
            to = dc if i == 0 else 1 - dc
            for dx in range(4):
                rows = g[dx * 80 : (dx + 1) * 80]
                out_a[to, dx] = rows[:, :A_COLS]
                out_b[to, dx] = rows[:, A_COLS:]


def weight_grad(nt, d):
    n = nt.shape[0] // 8
    shapes = [(2, 4, 80, A_COLS), (2, 4, 80, B_COLS)] * n
    return pl.pallas_call(
        functools.partial(grad_kernel, n),
        out_shape=[jax.ShapeDtypeStruct(shape, BF) for shape in shapes],
        in_specs=[HBM, VM],
        out_specs=[VM] * (2 * n),
        scratch_shapes=[pltpu.VMEM(nt.shape, BF), pltpu.SemaphoreType.DMA((n,))],
        compiler_params=params(12),
        cost_estimate=pl.CostEstimate(
            flops=2 * n * 512 * 640 * 896, bytes_accessed=n * 2**21, transcendentals=0
        ),
        name="weight_grad",
    )(nt, d)


def gather_project(w, pos, hidden, lengths, bias, tokens):
    xs = [w] + [send(w, X_BY[4 - dx]) for dx in (1, 2, 3)]
    own_a = jnp.stack([a[:80, :A_COLS] for a in xs])
    own_b = jnp.stack([a[:, A_COLS:] for a in xs])
    oth_a = send(own_a, CORE)
    ra = [jnp.stack([own_a, oth_a])]
    own_b, ra[0] = tie(own_b, ra[0])
    oth_b = send(own_b, CORE)
    rb = [jnp.stack([own_b, oth_b])]
    ring, swapped = [(0, None, None)], [(1, 0, 1), (1, 1, 0)]
    pair = ([ring, swapped],) * 2
    single = ([[(0, None, 0), (1, None, 1)]],) * 2
    ra.append(send(ra[0], RING))
    rb.append(send(rb[0], RING))
    hidden, lengths, bias, _ = tie(hidden, lengths, bias, ra[0])
    ht, rstd = turn_hidden(pos, hidden)
    tabs = (bias,) + tables(lengths, tokens)
    nts = []
    state = None
    for k in (1, 2, 3):
        if k == 1:
            ra[1], ht, rstd, *tabs = tie(ra[1], ht, rstd, *tabs)
        else:
            ra[k], *state = tie(ra[k], *state)
        last = (lambda r: r[0]) if k == 3 else (lambda r: r)
        ra.append(send(last(ra[k]), RING))
        swap_a = send(ra[k], CORE)
        rb.append(send(last(rb[k]), RING))
        if k == 3:
            ra[4], rb[3] = tie(ra[4], rb[3])
        swap_b = send(rb[k], CORE)
        if k == 1:
            nt, *state = project([0], single, (own_a, oth_a), (own_b, oth_b), ht, rstd, None)
            nts.append(nt)
        nt, *state = project(
            [k, 8 - k], pair, (ra[k], swap_a), (rb[k], swap_b), ht, rstd, state
        )
        nts.append(nt)
    wa = (ra[4], send(ra[4], CORE))
    rb[4], *state = tie(rb[4], *state)
    wb = (rb[4], send(rb[4], CORE))
    return ([4], single, wa, wb, ht, rstd, state), tabs, nts


def scatter(nts, d, sums):
    flips = iter([FLIPS[3], FLIPS[4], FLIPS[5], FLIPS[0], FLIPS[1], FLIPS[2], None])
    flip = send(sums, next(flips))

    def exchange(arrived):
        nonlocal sums, flip
        arrived, got, sums = tie(arrived, flip, sums)
        sums = sums + got
        perm = next(flips)
        flip = None if perm is None else send(sums, perm)
        return arrived

    near4 = weight_grad(nts[4], d)
    early = weight_grad(nts[3], d)
    t = [None, None]
    for p in (1, 0):
        s = add(near4[p][0], send(near4[p][1], CORE))
        if p == 0:
            s, d = tie(exchange(s), d)
        t[p] = send(s, BACK)
    slots = {(3, 0), (2, 0), (1, 1), (1, 0), (0, 1)}
    for k in (3, 2, 1):
        g = early if k == 3 else weight_grad(nts[k], d)
        near, far = g[:2], g[2:]
        for p in (1, 0):
            got = send(far[p], CORE)
            back = exchange(t[p]) if (k, p) in slots else t[p]
            if k == 3:
                s = jnp.stack([add(near[p][0], got[0], back), add(near[p][1], got[1])])
            else:
                s = add(near[p], got, back)
            t[p] = send(s, BACK)
    near0 = weight_grad(nts[0], d)
    parts = []
    for p in (1, 0):
        back = exchange(t[p]) if (0, p) in slots else t[p]
        got = send(add(near0[p][1], back[1]), CORE)
        parts.insert(0, add(near0[p][0], back[0], got))
    y = [jnp.concatenate([parts[0][k], parts[1][k]], axis=1) for k in range(4)]
    total = y[0].astype(F4)
    for k in (2, 1, 3):
        total = total + send(y[k], X_BY[k]).astype(F4)
    return total, sums


def doc_layout(lengths):
    ends = jnp.cumsum(lengths, axis=1)
    place = jnp.arange(ROW, dtype=jnp.int32)[None, :, None]
    passed = place >= ends[:, None, :]
    segment = jnp.sum(passed.astype(jnp.int32), axis=2)
    start = jnp.max(jnp.where(passed, ends[:, None, :], 0), axis=2)
    position = (place[:, :, 0] - start).astype(F4)
    real = (place[:, :, 0] < ends[:, -1:]).astype(F4)
    return segment, position, real


def tables(lengths, tokens):
    segment, position, real = doc_layout(lengths)
    freq = 1000000.0 ** (-(2.0 * jnp.arange(D // 2, dtype=F4)) / D)
    angle = position.reshape(tokens, 1) * freq
    cos, sin = jnp.cos(angle), jnp.sin(angle)
    cosf = jnp.concatenate([cos, cos], axis=1)
    sinf = jnp.concatenate([-sin, sin], axis=1)
    causal = jnp.arange(ROW)[:, None] >= jnp.arange(ROW)[None, :]
    mask = ((segment[:, :, None] == segment[:, None, :]) & causal[None]).astype(F4)
    return cosf, sinf, mask, jnp.broadcast_to(real.reshape(tokens, 1), (tokens, D))


def per_device(hidden, gain, w_query, w_keyval, b_query, b_keyval, upstream, lengths):
    tokens = hidden.shape[0]
    i = lax.axis_index("dp")
    pos = jnp.stack([i // 16, (i // 2) % 8, i % 2]).astype(jnp.int32)
    w_all = jnp.concatenate([w_query, w_keyval[0], w_keyval[1]], axis=1)
    extra = jnp.concatenate([gain, jnp.sum(lengths, axis=1).astype(BF)])
    extra = jnp.pad(extra[None, :], ((0, 7), (A_COLS, B_COLS - 84)))
    bias = jnp.concatenate([b_query, b_keyval[0], b_keyval[1]]).reshape(1, 896)
    last, (bias, *tabs), nts = gather_project(
        jnp.concatenate([w_all, extra], axis=0), pos, hidden, lengths, bias, tokens
    )
    nt, attended, d, sums = attention(*last, bias, upstream, tabs)
    g, sums = scatter(nts + [nt], d, sums)
    grad_query = g[:, :640]
    grad_keyval = jnp.stack([g[:, 640:768], g[:, 768:]])
    grad_bias_query = sums[:5].reshape(640)
    grad_bias_keyval = sums[5:7]
    part = jnp.sum(g * w_all.astype(F4), axis=1) / gain.astype(F4)
    one, two, three = [
        lax.ppermute(part, "mp", [(y, y ^ k) for y in range(4)]) for k in (1, 2, 3)
    ]
    gain_gradient = (part + one) + (two + three)
    return (attended, grad_query, grad_keyval, grad_bias_query, grad_bias_keyval, gain_gradient)


def solution(mesh):
    return jax.shard_map(
        per_device,
        mesh=mesh,
        in_specs=(
            P("dp", None),
            P("dp"),
            P("dp", "mp"),
            P(None, "dp", "mp"),
            P("mp"),
            P(None, "mp"),
            P("dp", "mp"),
            P("dp", None),
        ),
        out_specs=(
            P("dp", "mp"),
            P("dp", "mp"),
            P(None, "dp", "mp"),
            P("mp"),
            P(None, "mp"),
            P("dp"),
        ),
        check_vma=False,
    )
```

```python
import functools

import jax
import jax.numpy as jnp
from jax import lax
from jax.experimental import pallas as pl
from jax.experimental.pallas import tpu as pltpu
from jax.sharding import PartitionSpec as P

D = 128
ROW = 128
XS, ZS, CS = 4, 8, 2
BF = jnp.bfloat16
F4 = jnp.float32
A_COLS, B_COLS = 512, 384
W_ROWS = 88


def _perm(move):
    pairs = []
    for x in range(XS):
        for z in range(ZS):
            for c in range(CS):
                a, b, e = move(x, z, c)
                pairs.append(((x * ZS + z) * CS + c, ((a % XS) * ZS + b % ZS) * CS + e % CS))
    return pairs


CORE = _perm(lambda x, z, c: (x, z, 1 - c))
X_BY = [_perm(lambda x, z, c, k=k: (x + k, z, c)) for k in range(XS)]
RING = _perm(lambda x, z, c: (x, z + 1 - 2 * c, c))
BACK = _perm(lambda x, z, c: (x, z - 1 + 2 * c, c))
FLIPS = [
    CORE,
    _perm(lambda x, z, c: (x ^ 1, z, c)),
    _perm(lambda x, z, c: (x ^ 2, z, c)),
    _perm(lambda x, z, c: (x, z ^ 1, c)),
    _perm(lambda x, z, c: (x, z ^ 2, c)),
    _perm(lambda x, z, c: (x, z ^ 4, c)),
]


def send(a, perm):
    return lax.ppermute(a, "dp", perm)


def add(*parts):
    total = parts[0].astype(F4)
    for p in parts[1:]:
        total = total + p.astype(F4)
    return total.astype(BF)


def tie(*arrays):
    return lax.optimization_barrier(arrays)


def dot(a, b, dims):
    return lax.dot_general(a, b, ((dims[:1], dims[1:]), ((), ())), preferred_element_type=F4)


VM = pl.BlockSpec(memory_space=pltpu.VMEM)
HBM = pl.BlockSpec(memory_space=pltpu.HBM)


def params(mib):
    return pltpu.CompilerParams(vmem_limit_bytes=mib * 2**20)


def turn_kernel(pos_ref, h_ref, out_ref, rstd_ref, ht_ref, sem, hs, sems):
    tokens, width = h_ref.shape
    parts = [
        pltpu.make_async_copy(h_ref.at[:, pl.ds(b * 640, 640)], hs.at[b], sems.at[b])
        for b in range(8)
    ]
    for part in parts:
        part.start()
    x, z, c = pos_ref[0], pos_ref[1], pos_ref[2]
    ss = jnp.zeros((1, tokens), F4)
    for b in range(8):
        parts[b].wait()
        ht = hs[b].T
        hf = ht.astype(F4)
        ss = ss + jnp.sum(hf * hf, axis=0, keepdims=True)
        for j in range(8):
            dx = lax.rem(b // 2 - x + XS, XS)
            e = lax.rem((1 - 2 * c) * (z - (b % 2) * 4 - j // 2) + ZS, ZS)
            dc = lax.rem(j % 2 + c, CS)
            ht_ref[e * 8 + dc * 4 + dx] = ht[j * 80 : (j + 1) * 80]
    rstd_ref[...] = lax.rsqrt(ss / width + 1e-06)
    copy = pltpu.make_async_copy(ht_ref, out_ref, sem)
    copy.start()
    copy.wait()


def turn_hidden(pos, hidden):
    tokens, width = hidden.shape
    return pl.pallas_call(
        turn_kernel,
        out_shape=(
            jax.ShapeDtypeStruct((64, 80, tokens), BF),
            jax.ShapeDtypeStruct((1, tokens), F4),
        ),
        in_specs=[pl.BlockSpec(memory_space=pltpu.SMEM), HBM],
        out_specs=(HBM, VM),
        scratch_shapes=[
            pltpu.VMEM((64, 80, tokens), BF),
            pltpu.SemaphoreType.DMA,
            pltpu.VMEM((8, tokens, 640), BF),
            pltpu.SemaphoreType.DMA((8,)),
        ],
        compiler_params=params(20),
        cost_estimate=pl.CostEstimate(
            flops=4 * tokens * width, bytes_accessed=4 * tokens * width, transcendentals=0
        ),
        name="turn_hidden",
    )(pos, hidden)


def project_blocks(blocks, maps, wa_refs, wb_refs, ht_ref, rstd_ref, nt_ref, scratch):
    hs, wa, wb, table, sems, nt, nt_sem = scratch
    groups = []
    n = 0
    for i, e in enumerate(blocks):
        group = [pltpu.make_async_copy(ht_ref.at[pl.ds(e * 8, 8)], hs.at[i], sems.at[n])]
        n += 1
        for refs, dst, part in ((wb_refs, wb, 1), (wa_refs, wa, 0)):
            for src, take, dc in maps[part][i]:
                src = refs[src] if take is None else refs[src].at[take]
                to = dst.at[i] if dc is None else dst.at[i, dc]
                group.append(pltpu.make_async_copy(src, to, sems.at[n]))
                n += 1
        groups.append(group)
    for cp in [cp for group in groups for cp in group]:
        cp.start()
    rstd = rstd_ref[...]
    acc_a = acc_b = None
    outs = []
    for i in range(len(blocks)):
        for cp in groups[i]:
            cp.wait()
        for j in range(8):
            table[j : j + 1, :] = wb[i, j // 4, j % 4, 80:81, 0:128].astype(F4)
        rows = table[...]
        gains = rows.T
        for j in range(8):
            xhat = hs[i, j].astype(F4) * rstd
            nt[i * 8 + j] = (xhat * gains[:80, j : j + 1]).astype(BF)
        part = pl.ds(i * 8, 8)
        out = pltpu.make_async_copy(nt.at[part], nt_ref.at[part], nt_sem.at[i])
        out.start()
        outs.append(out)
        xb = nt[i * 8 : (i + 1) * 8].reshape(640, rstd.shape[1]).T
        pa = dot(xb, wa[i].reshape(640, A_COLS), (1, 0))
        pb = dot(xb, wb[i, :, :, :80].reshape(640, B_COLS), (1, 0))
        lane = lax.broadcasted_iota(jnp.int32, (8, 128), 1)
        real = jnp.sum(jnp.where((lane >= 80) & (lane < 84), rows, 0.0), axis=0, keepdims=True)
        if i == 0:
            acc_a, acc_b, acc_real = pa, pb, real
        else:
            acc_a, acc_b, acc_real = acc_a + pa, acc_b + pb, acc_real + real
    for out in outs:
        out.wait()
    return acc_a, acc_b, acc_real


def project_scratch(n, copies):
    return [
        pltpu.VMEM((n, 8, 80, 512), BF),
        pltpu.VMEM((n, 2, 4, 80, A_COLS), BF),
        pltpu.VMEM((n, 2, 4, W_ROWS, B_COLS), BF),
        pltpu.VMEM((8, 128), F4),
        pltpu.SemaphoreType.DMA((copies,)),
        pltpu.VMEM((8 * n, 80, 512), BF),
        pltpu.SemaphoreType.DMA((n,)),
    ]


def project_kernel(blocks, maps, count, first, *refs):
    wa_refs, wb_refs = refs[:count], refs[count : 2 * count]
    refs = refs[2 * count :]
    ht_ref, rstd_ref = refs[:2]
    refs = refs[2:]
    if not first:
        old, old_real = refs[:2]
        refs = refs[2:]
    nt_ref, acc, acc_real = refs[:3]
    pa, pb, real = project_blocks(
        blocks, maps, wa_refs, wb_refs, ht_ref, rstd_ref, nt_ref, refs[3:]
    )
    if not first:
        pa = pa + old[:, :A_COLS]
        pb = pb + old[:, A_COLS:]
        real = real + old_real[...]
    acc[:, :A_COLS] = pa
    acc[:, A_COLS:] = pb
    acc_real[...] = real


def project(blocks, maps, wa, wb, ht, rstd, state):
    tokens = ht.shape[2]
    n = len(blocks)
    first = state is None
    copies = n + sum(len(m) for part in maps for m in part)
    return pl.pallas_call(
        functools.partial(project_kernel, blocks, maps, len(wa), first),
        out_shape=(
            jax.ShapeDtypeStruct((8 * n, 80, tokens), BF),
            jax.ShapeDtypeStruct((tokens, 896), F4),
            jax.ShapeDtypeStruct((1, 128), F4),
        ),
        in_specs=[HBM] * (2 * len(wa) + 1) + [VM] * (1 if first else 3),
        out_specs=(HBM, VM, VM),
        scratch_shapes=project_scratch(n, copies),
        compiler_params=params(20),
        cost_estimate=pl.CostEstimate(
            flops=2 * n * tokens * 640 * 896, bytes_accessed=n * 2**21, transcendentals=0
        ),
        name="project",
    )(*wa, *wb, ht, rstd, *(() if first else state))


def attention_kernel(blocks, maps, count, *refs):
    wa_refs, wb_refs = refs[:count], refs[count : 2 * count]
    refs = refs[2 * count :]
    ht_ref, rstd_ref, old, old_real, bias, up, cosf, sinf, mask, real = refs[:10]
    nt_ref, out_ref, d_ref, sum_ref, qkv = refs[10:15]
    pa, pb, new_real = project_blocks(
        blocks, maps, wa_refs, wb_refs, ht_ref, rstd_ref, nt_ref, refs[15:]
    )
    qkv[:, :A_COLS] = old[:, :A_COLS] + pa + bias[:, :A_COLS]
    qkv[:, A_COLS:] = old[:, A_COLS:] + pb + bias[:, A_COLS:]
    total = jnp.sum(old_real[...] + new_real, axis=1, keepdims=True)
    scale = 1.0 / D**0.5
    weight = real[...] * 256.0 / total
    for r in range(4):
        rows = slice(r * ROW, (r + 1) * ROW)
        co, si = cosf[rows], sinf[rows]

        def turn(v, s):
            return v * co + pltpu.roll(v, 64, 1) * s

        k = turn(qkv[rows, 640:768], si).astype(BF)
        v = qkv[rows, 768:896].astype(BF)
        q = jnp.concatenate(
            [turn(qkv[rows, h * D : (h + 1) * D], si).astype(BF) for h in range(5)], axis=0
        )
        ga = jnp.concatenate(
            [(up[rows, h * D : (h + 1) * D].astype(F4) * weight[rows]).astype(BF) for h in range(5)],
            axis=0,
        )
        allowed = jnp.concatenate([mask[r]] * 5, axis=0) > 0.0
        scores = jnp.where(allowed, dot(q, k, (1, 1)) * scale, -1e30)
        expo = jnp.exp(scores - jnp.max(scores, axis=1, keepdims=True))
        probs = expo / jnp.sum(expo, axis=1, keepdims=True)
        probs_b = probs.astype(BF)
        att = dot(probs_b, v, (1, 0)).astype(BF)
        dp = dot(ga, v, (1, 1))
        dv = dot(probs_b, ga, (0, 0))
        ds = probs * (dp - jnp.sum(probs * dp, axis=1, keepdims=True)) * scale
        dsb = ds.astype(BF)
        dq = dot(dsb, k, (1, 0))
        dk = dot(dsb, q, (0, 0))
        for h in range(5):
            hs = slice(h * ROW, (h + 1) * ROW)
            out_ref[rows, h * D : (h + 1) * D] = att[hs]
            d_ref[rows, h * D : (h + 1) * D] = turn(dq[hs], -si).astype(BF)
        d_ref[rows, 640:768] = turn(dk, -si).astype(BF)
        d_ref[rows, 768:896] = dv.astype(BF)
    for i in range(7):
        sum_ref[i : i + 1, :] = jnp.sum(
            d_ref[:, i * D : (i + 1) * D].astype(F4), axis=0, keepdims=True
        )
    sum_ref[7:8, :] = jnp.zeros((1, D), F4)


def attention(blocks, maps, wa, wb, ht, rstd, state, bias, up, tables):
    tokens = ht.shape[2]
    copies = len(blocks) + sum(len(m) for part in maps for m in part)
    return pl.pallas_call(
        functools.partial(attention_kernel, blocks, maps, len(wa)),
        out_shape=(
            jax.ShapeDtypeStruct((8, 80, tokens), BF),
            jax.ShapeDtypeStruct((tokens, 640), BF),
            jax.ShapeDtypeStruct((tokens, 896), BF),
            jax.ShapeDtypeStruct((8, D), F4),
        ),
        in_specs=[HBM] * (2 * len(wa) + 1) + [VM] * 9,
        out_specs=(HBM, VM, VM, VM),
        scratch_shapes=[pltpu.VMEM((tokens, 896), F4)] + project_scratch(1, copies),
        compiler_params=params(24),
        cost_estimate=pl.CostEstimate(
            flops=2 * tokens * 1280 * 896, bytes_accessed=8 * 2**20, transcendentals=400000
        ),
        name="attend",
    )(*wa, *wb, ht, rstd, *state, bias, up, *tables)


def grad_kernel(n, nt_ref, d_ref, *refs):
    outs, (nt, sems) = refs[: 2 * n], refs[2 * n :]
    copies = []
    for i in range(n):
        part = pl.ds(i * 8, 8)
        copies.append(pltpu.make_async_copy(nt_ref.at[part], nt.at[part], sems.at[i]))
    for cp in copies:
        cp.start()
    d = d_ref[...]
    for i in range(n):
        copies[i].wait()
        for dc in range(2):
            at = i * 8 + dc * 4
            g = dot(nt[at : at + 4].reshape(320, 512), d, (1, 0)).astype(BF)
            out_a = outs[2 * i]
            out_b = outs[2 * i + 1]
            to = dc if i == 0 else 1 - dc
            for dx in range(4):
                rows = g[dx * 80 : (dx + 1) * 80]
                out_a[to, dx] = rows[:, :A_COLS]
                out_b[to, dx] = rows[:, A_COLS:]


def weight_grad(nt, d):
    n = nt.shape[0] // 8
    shapes = [(2, 4, 80, A_COLS), (2, 4, 80, B_COLS)] * n
    return pl.pallas_call(
        functools.partial(grad_kernel, n),
        out_shape=[jax.ShapeDtypeStruct(shape, BF) for shape in shapes],
        in_specs=[HBM, VM],
        out_specs=[VM] * (2 * n),
        scratch_shapes=[pltpu.VMEM(nt.shape, BF), pltpu.SemaphoreType.DMA((n,))],
        compiler_params=params(12),
        cost_estimate=pl.CostEstimate(
            flops=2 * n * 512 * 640 * 896, bytes_accessed=n * 2**21, transcendentals=0
        ),
        name="weight_grad",
    )(nt, d)


def gather_project(w, pos, hidden, lengths, bias, tokens):
    far = send(w, X_BY[2])
    xs = [w, send(w, X_BY[3]), far, send(w, X_BY[1])]
    ht, rstd = turn_hidden(pos, hidden)
    far, ht, rstd = tie(far, ht, rstd)
    xs[2] = far
    own_a = jnp.stack([a[:80, :A_COLS] for a in xs])
    own_b = jnp.stack([a[:, A_COLS:] for a in xs])
    oth_a = send(own_a, CORE)
    ra = [jnp.stack([own_a, oth_a])]
    own_b, ra[0] = tie(own_b, ra[0])
    oth_b = send(own_b, CORE)
    rb = [jnp.stack([own_b, oth_b])]
    ring, swapped = [(0, None, None)], [(1, 0, 1), (1, 1, 0)]
    pair = ([ring, swapped],) * 2
    single = ([[(0, None, 0), (1, None, 1)]],) * 2
    ra.append(send(ra[0], RING))
    rb.append(send(rb[0], RING))
    lengths, bias, _ = tie(lengths, bias, ra[0])
    tabs = (bias,) + tables(lengths, tokens)
    nts = []
    state = None
    for k in (1, 2, 3):
        if k == 1:
            ra[1], ht, rstd, *tabs = tie(ra[1], ht, rstd, *tabs)
        else:
            ra[k], *state = tie(ra[k], *state)
        last = (lambda r: r[0]) if k == 3 else (lambda r: r)
        ra.append(send(last(ra[k]), RING))
        swap_a = send(ra[k], CORE)
        rb.append(send(last(rb[k]), RING))
        if k == 3:
            ra[4], rb[3] = tie(ra[4], rb[3])
        swap_b = send(rb[k], CORE)
        if k == 1:
            nt, *state = project([0], single, (own_a, oth_a), (own_b, oth_b), ht, rstd, None)
            nts.append(nt)
        nt, *state = project(
            [k, 8 - k], pair, (ra[k], swap_a), (rb[k], swap_b), ht, rstd, state
        )
        nts.append(nt)
    wa = (ra[4], send(ra[4], CORE))
    rb[4], *state = tie(rb[4], *state)
    wb = (rb[4], send(rb[4], CORE))
    return ([4], single, wa, wb, ht, rstd, state), tabs, nts


def scatter(nts, d, sums):
    flips = iter([FLIPS[3], FLIPS[4], FLIPS[5], FLIPS[0], FLIPS[1], FLIPS[2], None])
    flip = send(sums, next(flips))

    def exchange(arrived):
        nonlocal sums, flip
        arrived, got, sums = tie(arrived, flip, sums)
        sums = sums + got
        perm = next(flips)
        flip = None if perm is None else send(sums, perm)
        return arrived

    near4 = weight_grad(nts[4], d)
    early = weight_grad(nts[3], d)
    t = [None, None]
    for p in (1, 0):
        s = add(near4[p][0], send(near4[p][1], CORE))
        if p == 0:
            s, d = tie(exchange(s), d)
        t[p] = send(s, BACK)
    slots = {(3, 0), (2, 0), (1, 1), (1, 0), (0, 1)}
    for k in (3, 2, 1):
        g = early if k == 3 else weight_grad(nts[k], d)
        near, far = g[:2], g[2:]
        for p in (1, 0):
            got = send(far[p], CORE)
            back = exchange(t[p]) if (k, p) in slots else t[p]
            if k == 3:
                s = jnp.stack([add(near[p][0], got[0], back), add(near[p][1], got[1])])
            else:
                s = add(near[p], got, back)
            t[p] = send(s, BACK)
    near0 = weight_grad(nts[0], d)
    parts = []
    for p in (1, 0):
        back = exchange(t[p]) if (0, p) in slots else t[p]
        got = send(add(near0[p][1], back[1]), CORE)
        parts.insert(0, add(near0[p][0], back[0], got))
    y = [jnp.concatenate([parts[0][k], parts[1][k]], axis=1) for k in range(4)]
    total = y[0].astype(F4)
    for k in (2, 1, 3):
        total = total + send(y[k], X_BY[k]).astype(F4)
    return total, sums


def doc_layout(lengths):
    ends = jnp.cumsum(lengths, axis=1)
    place = jnp.arange(ROW, dtype=jnp.int32)[None, :, None]
    passed = place >= ends[:, None, :]
    segment = jnp.sum(passed.astype(jnp.int32), axis=2)
    start = jnp.max(jnp.where(passed, ends[:, None, :], 0), axis=2)
    position = (place[:, :, 0] - start).astype(F4)
    real = (place[:, :, 0] < ends[:, -1:]).astype(F4)
    return segment, position, real


def tables(lengths, tokens):
    segment, position, real = doc_layout(lengths)
    freq = 1000000.0 ** (-(2.0 * jnp.arange(D // 2, dtype=F4)) / D)
    angle = position.reshape(tokens, 1) * freq
    cos, sin = jnp.cos(angle), jnp.sin(angle)
    cosf = jnp.concatenate([cos, cos], axis=1)
    sinf = jnp.concatenate([-sin, sin], axis=1)
    causal = jnp.arange(ROW)[:, None] >= jnp.arange(ROW)[None, :]
    mask = ((segment[:, :, None] == segment[:, None, :]) & causal[None]).astype(F4)
    return cosf, sinf, mask, jnp.broadcast_to(real.reshape(tokens, 1), (tokens, D))


def per_device(hidden, gain, w_query, w_keyval, b_query, b_keyval, upstream, lengths):
    tokens = hidden.shape[0]
    i = lax.axis_index("dp")
    pos = jnp.stack([i // 16, (i // 2) % 8, i % 2]).astype(jnp.int32)
    w_all = jnp.concatenate([w_query, w_keyval[0], w_keyval[1]], axis=1)
    extra = jnp.concatenate([gain, jnp.sum(lengths, axis=1).astype(BF)])
    extra = jnp.pad(extra[None, :], ((0, 7), (A_COLS, B_COLS - 84)))
    bias = jnp.concatenate([b_query, b_keyval[0], b_keyval[1]]).reshape(1, 896)
    last, (bias, *tabs), nts = gather_project(
        jnp.concatenate([w_all, extra], axis=0), pos, hidden, lengths, bias, tokens
    )
    nt, attended, d, sums = attention(*last, bias, upstream, tabs)
    g, sums = scatter(nts + [nt], d, sums)
    grad_query = g[:, :640]
    grad_keyval = jnp.stack([g[:, 640:768], g[:, 768:]])
    grad_bias_query = sums[:5].reshape(640)
    grad_bias_keyval = sums[5:7]
    part = jnp.sum(g * w_all.astype(F4), axis=1) / gain.astype(F4)
    one, two, three = [
        lax.ppermute(part, "mp", [(y, y ^ k) for y in range(4)]) for k in (1, 2, 3)
    ]
    gain_gradient = (part + one) + (two + three)
    return (attended, grad_query, grad_keyval, grad_bias_query, grad_bias_keyval, gain_gradient)


def solution(mesh):
    return jax.shard_map(
        per_device,
        mesh=mesh,
        in_specs=(
            P("dp", None),
            P("dp"),
            P("dp", "mp"),
            P(None, "dp", "mp"),
            P("mp"),
            P(None, "mp"),
            P("dp", "mp"),
            P("dp", None),
        ),
        out_specs=(
            P("dp", "mp"),
            P("dp", "mp"),
            P(None, "dp", "mp"),
            P("mp"),
            P(None, "mp"),
            P("dp"),
        ),
        check_vma=False,
    )
```

```python
import functools

import jax
import jax.numpy as jnp
from jax import lax
from jax.experimental import pallas as pl
from jax.experimental.pallas import tpu as pltpu
from jax.sharding import PartitionSpec as P

D = 128
ROW = 128
XS, ZS, CS = 4, 8, 2
BF = jnp.bfloat16
F4 = jnp.float32
A_COLS, B_COLS = 512, 384
W_ROWS = 88


def _perm(move):
    pairs = []
    for x in range(XS):
        for z in range(ZS):
            for c in range(CS):
                a, b, e = move(x, z, c)
                pairs.append(((x * ZS + z) * CS + c, ((a % XS) * ZS + b % ZS) * CS + e % CS))
    return pairs


CORE = _perm(lambda x, z, c: (x, z, 1 - c))
X_BY = [_perm(lambda x, z, c, k=k: (x + k, z, c)) for k in range(XS)]
RING = _perm(lambda x, z, c: (x, z + 1 - 2 * c, c))
BACK = _perm(lambda x, z, c: (x, z - 1 + 2 * c, c))
FLIPS = [
    CORE,
    _perm(lambda x, z, c: (x ^ 1, z, c)),
    _perm(lambda x, z, c: (x ^ 2, z, c)),
    _perm(lambda x, z, c: (x, z ^ 1, c)),
    _perm(lambda x, z, c: (x, z ^ 2, c)),
    _perm(lambda x, z, c: (x, z ^ 4, c)),
]


def send(a, perm):
    return lax.ppermute(a, "dp", perm)


def add(*parts):
    total = parts[0].astype(F4)
    for p in parts[1:]:
        total = total + p.astype(F4)
    return total.astype(BF)


def tie(*arrays):
    return lax.optimization_barrier(arrays)


def dot(a, b, dims):
    return lax.dot_general(a, b, ((dims[:1], dims[1:]), ((), ())), preferred_element_type=F4)


VM = pl.BlockSpec(memory_space=pltpu.VMEM)
HBM = pl.BlockSpec(memory_space=pltpu.HBM)


def params(mib):
    return pltpu.CompilerParams(vmem_limit_bytes=mib * 2**20)


def turn_kernel(pos_ref, h_ref, out_ref, rstd_ref, ht_ref, sem):
    tokens, width = h_ref.shape
    x, z, c = pos_ref[0], pos_ref[1], pos_ref[2]
    ss = jnp.zeros((1, tokens), F4)
    for b in range(8):
        ht = h_ref[:, b * 640 : (b + 1) * 640].T
        hf = ht.astype(F4)
        ss = ss + jnp.sum(hf * hf, axis=0, keepdims=True)
        for j in range(8):
            dx = lax.rem(b // 2 - x + XS, XS)
            e = lax.rem((1 - 2 * c) * (z - (b % 2) * 4 - j // 2) + ZS, ZS)
            dc = lax.rem(j % 2 + c, CS)
            ht_ref[e * 8 + dc * 4 + dx] = ht[j * 80 : (j + 1) * 80]
    rstd_ref[...] = lax.rsqrt(ss / width + 1e-06)
    copy = pltpu.make_async_copy(ht_ref, out_ref, sem)
    copy.start()
    copy.wait()


def turn_hidden(pos, hidden):
    tokens, width = hidden.shape
    return pl.pallas_call(
        turn_kernel,
        out_shape=(
            jax.ShapeDtypeStruct((64, 80, tokens), BF),
            jax.ShapeDtypeStruct((1, tokens), F4),
        ),
        in_specs=[pl.BlockSpec(memory_space=pltpu.SMEM), VM],
        out_specs=(HBM, VM),
        scratch_shapes=[pltpu.VMEM((64, 80, tokens), BF), pltpu.SemaphoreType.DMA],
        compiler_params=params(20),
        cost_estimate=pl.CostEstimate(
            flops=4 * tokens * width, bytes_accessed=4 * tokens * width, transcendentals=0
        ),
        name="turn_hidden",
    )(pos, hidden)


def project_blocks(blocks, maps, wa_refs, wb_refs, ht_ref, rstd_ref, nt_ref, scratch):
    hs, wa, wb, table, sems, nt, nt_sem = scratch
    groups = []
    n = 0
    for i, e in enumerate(blocks):
        group = [pltpu.make_async_copy(ht_ref.at[pl.ds(e * 8, 8)], hs.at[i], sems.at[n])]
        n += 1
        for refs, dst, part in ((wb_refs, wb, 1), (wa_refs, wa, 0)):
            for src, take, dc in maps[part][i]:
                src = refs[src] if take is None else refs[src].at[take]
                to = dst.at[i] if dc is None else dst.at[i, dc]
                group.append(pltpu.make_async_copy(src, to, sems.at[n]))
                n += 1
        groups.append(group)
    for cp in [cp for group in groups for cp in group]:
        cp.start()
    rstd = rstd_ref[...]
    acc_a = acc_b = None
    outs = []
    for i in range(len(blocks)):
        for cp in groups[i]:
            cp.wait()
        for j in range(8):
            table[j : j + 1, :] = wb[i, j // 4, j % 4, 80:81, 0:128].astype(F4)
        rows = table[...]
        gains = rows.T
        for j in range(8):
            xhat = hs[i, j].astype(F4) * rstd
            nt[i * 8 + j] = (xhat * gains[:80, j : j + 1]).astype(BF)
        part = pl.ds(i * 8, 8)
        out = pltpu.make_async_copy(nt.at[part], nt_ref.at[part], nt_sem.at[i])
        out.start()
        outs.append(out)
        xb = nt[i * 8 : (i + 1) * 8].reshape(640, rstd.shape[1]).T
        pa = dot(xb, wa[i].reshape(640, A_COLS), (1, 0))
        pb = dot(xb, wb[i, :, :, :80].reshape(640, B_COLS), (1, 0))
        lane = lax.broadcasted_iota(jnp.int32, (8, 128), 1)
        real = jnp.sum(jnp.where((lane >= 80) & (lane < 84), rows, 0.0), axis=0, keepdims=True)
        if i == 0:
            acc_a, acc_b, acc_real = pa, pb, real
        else:
            acc_a, acc_b, acc_real = acc_a + pa, acc_b + pb, acc_real + real
    for out in outs:
        out.wait()
    return acc_a, acc_b, acc_real


def project_scratch(n, copies):
    return [
        pltpu.VMEM((n, 8, 80, 512), BF),
        pltpu.VMEM((n, 2, 4, 80, A_COLS), BF),
        pltpu.VMEM((n, 2, 4, W_ROWS, B_COLS), BF),
        pltpu.VMEM((8, 128), F4),
        pltpu.SemaphoreType.DMA((copies,)),
        pltpu.VMEM((8 * n, 80, 512), BF),
        pltpu.SemaphoreType.DMA((n,)),
    ]


def project_kernel(blocks, maps, count, first, *refs):
    wa_refs, wb_refs = refs[:count], refs[count : 2 * count]
    refs = refs[2 * count :]
    ht_ref, rstd_ref = refs[:2]
    refs = refs[2:]
    if not first:
        old, old_real = refs[:2]
        refs = refs[2:]
    nt_ref, acc, acc_real = refs[:3]
    pa, pb, real = project_blocks(
        blocks, maps, wa_refs, wb_refs, ht_ref, rstd_ref, nt_ref, refs[3:]
    )
    if not first:
        pa = pa + old[:, :A_COLS]
        pb = pb + old[:, A_COLS:]
        real = real + old_real[...]
    acc[:, :A_COLS] = pa
    acc[:, A_COLS:] = pb
    acc_real[...] = real


def project(blocks, maps, wa, wb, ht, rstd, state):
    tokens = ht.shape[2]
    n = len(blocks)
    first = state is None
    copies = n + sum(len(m) for part in maps for m in part)
    return pl.pallas_call(
        functools.partial(project_kernel, blocks, maps, len(wa), first),
        out_shape=(
            jax.ShapeDtypeStruct((8 * n, 80, tokens), BF),
            jax.ShapeDtypeStruct((tokens, 896), F4),
            jax.ShapeDtypeStruct((1, 128), F4),
        ),
        in_specs=[HBM] * (2 * len(wa) + 1) + [VM] * (1 if first else 3),
        out_specs=(HBM, VM, VM),
        scratch_shapes=project_scratch(n, copies),
        compiler_params=params(20),
        cost_estimate=pl.CostEstimate(
            flops=2 * n * tokens * 640 * 896, bytes_accessed=n * 2**21, transcendentals=0
        ),
        name="project",
    )(*wa, *wb, ht, rstd, *(() if first else state))


def attention_kernel(blocks, maps, count, *refs):
    wa_refs, wb_refs = refs[:count], refs[count : 2 * count]
    refs = refs[2 * count :]
    ht_ref, rstd_ref, old, old_real, bias, up, cosf, sinf, mask, real = refs[:10]
    nt_ref, out_ref, d_ref, sum_ref, qkv = refs[10:15]
    pa, pb, new_real = project_blocks(
        blocks, maps, wa_refs, wb_refs, ht_ref, rstd_ref, nt_ref, refs[15:]
    )
    qkv[:, :A_COLS] = old[:, :A_COLS] + pa + bias[:, :A_COLS]
    qkv[:, A_COLS:] = old[:, A_COLS:] + pb + bias[:, A_COLS:]
    total = jnp.sum(old_real[...] + new_real, axis=1, keepdims=True)
    scale = 1.0 / D**0.5
    weight = real[...] * 256.0 / total
    for r in range(4):
        rows = slice(r * ROW, (r + 1) * ROW)
        co, si = cosf[rows], sinf[rows]

        def turn(v, s):
            return v * co + pltpu.roll(v, 64, 1) * s

        k = turn(qkv[rows, 640:768], si).astype(BF)
        v = qkv[rows, 768:896].astype(BF)
        q = jnp.concatenate(
            [turn(qkv[rows, h * D : (h + 1) * D], si).astype(BF) for h in range(5)], axis=0
        )
        ga = jnp.concatenate(
            [(up[rows, h * D : (h + 1) * D].astype(F4) * weight[rows]).astype(BF) for h in range(5)],
            axis=0,
        )
        allowed = jnp.concatenate([mask[r]] * 5, axis=0) > 0.0
        scores = jnp.where(allowed, dot(q, k, (1, 1)) * scale, -1e30)
        expo = jnp.exp(scores - jnp.max(scores, axis=1, keepdims=True))
        probs = expo / jnp.sum(expo, axis=1, keepdims=True)
        probs_b = probs.astype(BF)
        att = dot(probs_b, v, (1, 0)).astype(BF)
        dp = dot(ga, v, (1, 1))
        dv = dot(probs_b, ga, (0, 0))
        ds = probs * (dp - jnp.sum(probs * dp, axis=1, keepdims=True)) * scale
        dsb = ds.astype(BF)
        dq = dot(dsb, k, (1, 0))
        dk = dot(dsb, q, (0, 0))
        for h in range(5):
            hs = slice(h * ROW, (h + 1) * ROW)
            out_ref[rows, h * D : (h + 1) * D] = att[hs]
            d_ref[rows, h * D : (h + 1) * D] = turn(dq[hs], -si).astype(BF)
        d_ref[rows, 640:768] = turn(dk, -si).astype(BF)
        d_ref[rows, 768:896] = dv.astype(BF)
    for i in range(7):
        sum_ref[i : i + 1, :] = jnp.sum(
            d_ref[:, i * D : (i + 1) * D].astype(F4), axis=0, keepdims=True
        )
    sum_ref[7:8, :] = jnp.zeros((1, D), F4)


def attention(blocks, maps, wa, wb, ht, rstd, state, bias, up, tables):
    tokens = ht.shape[2]
    copies = len(blocks) + sum(len(m) for part in maps for m in part)
    return pl.pallas_call(
        functools.partial(attention_kernel, blocks, maps, len(wa)),
        out_shape=(
            jax.ShapeDtypeStruct((8, 80, tokens), BF),
            jax.ShapeDtypeStruct((tokens, 640), BF),
            jax.ShapeDtypeStruct((tokens, 896), BF),
            jax.ShapeDtypeStruct((8, D), F4),
        ),
        in_specs=[HBM] * (2 * len(wa) + 1) + [VM] * 9,
        out_specs=(HBM, VM, VM, VM),
        scratch_shapes=[pltpu.VMEM((tokens, 896), F4)] + project_scratch(1, copies),
        compiler_params=params(24),
        cost_estimate=pl.CostEstimate(
            flops=2 * tokens * 1280 * 896, bytes_accessed=8 * 2**20, transcendentals=400000
        ),
        name="attend",
    )(*wa, *wb, ht, rstd, *state, bias, up, *tables)


def grad_kernel(n, nt_ref, d_ref, *refs):
    outs, (nt, sems) = refs[: 2 * n], refs[2 * n :]
    copies = []
    for i in range(n):
        part = pl.ds(i * 8, 8)
        copies.append(pltpu.make_async_copy(nt_ref.at[part], nt.at[part], sems.at[i]))
    for cp in copies:
        cp.start()
    d = d_ref[...]
    for i in range(n):
        copies[i].wait()
        for dc in range(2):
            at = i * 8 + dc * 4
            g = dot(nt[at : at + 4].reshape(320, 512), d, (1, 0)).astype(BF)
            out_a = outs[2 * i]
            out_b = outs[2 * i + 1]
            to = dc if i == 0 else 1 - dc
            for dx in range(4):
                rows = g[dx * 80 : (dx + 1) * 80]
                out_a[to, dx] = rows[:, :A_COLS]
                out_b[to, dx] = rows[:, A_COLS:]


def weight_grad(nt, d):
    n = nt.shape[0] // 8
    shapes = [(2, 4, 80, A_COLS), (2, 4, 80, B_COLS)] * n
    return pl.pallas_call(
        functools.partial(grad_kernel, n),
        out_shape=[jax.ShapeDtypeStruct(shape, BF) for shape in shapes],
        in_specs=[HBM, VM],
        out_specs=[VM] * (2 * n),
        scratch_shapes=[pltpu.VMEM(nt.shape, BF), pltpu.SemaphoreType.DMA((n,))],
        compiler_params=params(12),
        cost_estimate=pl.CostEstimate(
            flops=2 * n * 512 * 640 * 896, bytes_accessed=n * 2**21, transcendentals=0
        ),
        name="weight_grad",
    )(nt, d)


def gather_project(w, pos, hidden, lengths, bias, tokens):
    near = [send(w, X_BY[3]), send(w, X_BY[1])]
    far, w = tie(send(w, X_BY[2]), w)
    xs = [w, near[0], far, near[1]]
    own_a = jnp.stack([a[:80, :A_COLS] for a in xs])
    own_b = jnp.stack([a[:, A_COLS:] for a in xs])
    oth_a = send(own_a, CORE)
    ra = [jnp.stack([own_a, oth_a])]
    own_b, ra[0] = tie(own_b, ra[0])
    oth_b = send(own_b, CORE)
    rb = [jnp.stack([own_b, oth_b])]
    ring, swapped = [(0, None, None)], [(1, 0, 1), (1, 1, 0)]
    pair = ([ring, swapped],) * 2
    single = ([[(0, None, 0), (1, None, 1)]],) * 2
    ra.append(send(ra[0], RING))
    rb.append(send(rb[0], RING))
    hidden, lengths, bias, _ = tie(hidden, lengths, bias, ra[0])
    ht, rstd = turn_hidden(pos, hidden)
    tabs = (bias,) + tables(lengths, tokens)
    nts = []
    state = None
    for k in (1, 2, 3):
        if k == 1:
            ra[1], ht, rstd, *tabs = tie(ra[1], ht, rstd, *tabs)
        else:
            ra[k], *state = tie(ra[k], *state)
        last = (lambda r: r[0]) if k == 3 else (lambda r: r)
        ra.append(send(last(ra[k]), RING))
        swap_a = send(ra[k], CORE)
        rb.append(send(last(rb[k]), RING))
        if k == 3:
            ra[4], rb[3] = tie(ra[4], rb[3])
        swap_b = send(rb[k], CORE)
        if k == 1:
            nt, *state = project([0], single, (own_a, oth_a), (own_b, oth_b), ht, rstd, None)
            nts.append(nt)
        nt, *state = project(
            [k, 8 - k], pair, (ra[k], swap_a), (rb[k], swap_b), ht, rstd, state
        )
        nts.append(nt)
    wa = (ra[4], send(ra[4], CORE))
    rb[4], *state = tie(rb[4], *state)
    wb = (rb[4], send(rb[4], CORE))
    return ([4], single, wa, wb, ht, rstd, state), tabs, nts


def scatter(nts, d, sums):
    flips = iter([FLIPS[3], FLIPS[4], FLIPS[5], FLIPS[0], FLIPS[1], FLIPS[2], None])
    flip = send(sums, next(flips))

    def exchange(arrived):
        nonlocal sums, flip
        arrived, got, sums = tie(arrived, flip, sums)
        sums = sums + got
        perm = next(flips)
        flip = None if perm is None else send(sums, perm)
        return arrived

    near4 = weight_grad(nts[4], d)
    early = weight_grad(nts[3], d)
    t = [None, None]
    for p in (1, 0):
        s = add(near4[p][0], send(near4[p][1], CORE))
        if p == 0:
            s, d = tie(exchange(s), d)
        t[p] = send(s, BACK)
    slots = {(3, 0), (2, 0), (1, 1), (1, 0), (0, 1)}
    for k in (3, 2, 1):
        g = early if k == 3 else weight_grad(nts[k], d)
        near, far = g[:2], g[2:]
        for p in (1, 0):
            got = send(far[p], CORE)
            back = exchange(t[p]) if (k, p) in slots else t[p]
            if k == 3:
                s = jnp.stack([add(near[p][0], got[0], back), add(near[p][1], got[1])])
            else:
                s = add(near[p], got, back)
            t[p] = send(s, BACK)
    near0 = weight_grad(nts[0], d)
    parts = []
    for p in (1, 0):
        back = exchange(t[p]) if (0, p) in slots else t[p]
        got = send(add(near0[p][1], back[1]), CORE)
        parts.insert(0, add(near0[p][0], back[0], got))
    y = [jnp.concatenate([parts[0][k], parts[1][k]], axis=1) for k in range(4)]
    total = y[0].astype(F4)
    for k in (2, 1, 3):
        total = total + send(y[k], X_BY[k]).astype(F4)
    return total, sums


def doc_layout(lengths):
    ends = jnp.cumsum(lengths, axis=1)
    place = jnp.arange(ROW, dtype=jnp.int32)[None, :, None]
    passed = place >= ends[:, None, :]
    segment = jnp.sum(passed.astype(jnp.int32), axis=2)
    start = jnp.max(jnp.where(passed, ends[:, None, :], 0), axis=2)
    position = (place[:, :, 0] - start).astype(F4)
    real = (place[:, :, 0] < ends[:, -1:]).astype(F4)
    return segment, position, real


def tables(lengths, tokens):
    segment, position, real = doc_layout(lengths)
    freq = 1000000.0 ** (-(2.0 * jnp.arange(D // 2, dtype=F4)) / D)
    angle = position.reshape(tokens, 1) * freq
    cos, sin = jnp.cos(angle), jnp.sin(angle)
    cosf = jnp.concatenate([cos, cos], axis=1)
    sinf = jnp.concatenate([-sin, sin], axis=1)
    causal = jnp.arange(ROW)[:, None] >= jnp.arange(ROW)[None, :]
    mask = ((segment[:, :, None] == segment[:, None, :]) & causal[None]).astype(F4)
    return cosf, sinf, mask, jnp.broadcast_to(real.reshape(tokens, 1), (tokens, D))


def per_device(hidden, gain, w_query, w_keyval, b_query, b_keyval, upstream, lengths):
    tokens = hidden.shape[0]
    i = lax.axis_index("dp")
    pos = jnp.stack([i // 16, (i // 2) % 8, i % 2]).astype(jnp.int32)
    w_all = jnp.concatenate([w_query, w_keyval[0], w_keyval[1]], axis=1)
    extra = jnp.concatenate([gain, jnp.sum(lengths, axis=1).astype(BF)])
    extra = jnp.pad(extra[None, :], ((0, 7), (A_COLS, B_COLS - 84)))
    bias = jnp.concatenate([b_query, b_keyval[0], b_keyval[1]]).reshape(1, 896)
    last, (bias, *tabs), nts = gather_project(
        jnp.concatenate([w_all, extra], axis=0), pos, hidden, lengths, bias, tokens
    )
    nt, attended, d, sums = attention(*last, bias, upstream, tabs)
    g, sums = scatter(nts + [nt], d, sums)
    grad_query = g[:, :640]
    grad_keyval = jnp.stack([g[:, 640:768], g[:, 768:]])
    grad_bias_query = sums[:5].reshape(640)
    grad_bias_keyval = sums[5:7]
    part = jnp.sum(g * w_all.astype(F4), axis=1) / gain.astype(F4)
    one, two, three = [
        lax.ppermute(part, "mp", [(y, y ^ k) for y in range(4)]) for k in (1, 2, 3)
    ]
    gain_gradient = (part + one) + (two + three)
    return (attended, grad_query, grad_keyval, grad_bias_query, grad_bias_keyval, gain_gradient)


def solution(mesh):
    return jax.shard_map(
        per_device,
        mesh=mesh,
        in_specs=(
            P("dp", None),
            P("dp"),
            P("dp", "mp"),
            P(None, "dp", "mp"),
            P("mp"),
            P(None, "mp"),
            P("dp", "mp"),
            P("dp", None),
        ),
        out_specs=(
            P("dp", "mp"),
            P("dp", "mp"),
            P(None, "dp", "mp"),
            P("mp"),
            P(None, "mp"),
            P("dp"),
        ),
        check_vma=False,
    )
```
